32 devices in a mesh: branch: 2 (over y), dp: 16 (over z, x, core).
Axes of the slice: x: 2, y: 2, z: 4, core: 2. Of those that a mesh axis runs over, the one named last changes fastest.
Arguments:
- hidden: bfloat16 [64, 512, 768], P('dp'), may hold values from -6 to 6
- bounds: int32 [64, 2], P('dp'), may hold values from 1 to 512, as said below
- query_weight: bfloat16 [768, 384], replicated, may hold values from -0.21875 to 0.21875
- query_bias: float32 [384], replicated, may hold values from -3 to 3
- branch_keys: bfloat16 [2, 768, 384], P('branch'), may hold values from -0.21875 to 0.21875
- branch_values: bfloat16 [2, 768, 384], P('branch'), may hold values from -0.875 to 0.875
- branch_bias: float32 [2, 384], P('branch'), may hold values from -6 to 6
- depth_kernel: float32 [9, 768], replicated, may hold values from -2 to 2
- point_bias: float32 [384], replicated, may hold values from -3 to 3
- kernel_weight: bfloat16 [384, 54], replicated, may hold values from -0.3125 to 0.3125
- kernel_bias: float32 [54], replicated, may hold values from -3 to 3
- mixer_weight: bfloat16 [768, 768], replicated, may hold values from -0.21875 to 0.21875
- mixer_bias: float32 [768], replicated, may hold values from -3 to 3
- first_gain: float32 [768], replicated, may hold values from 0.1 to 1.9
- first_shift: float32 [768], replicated, may hold values from -3 to 3
- inner_weight: bfloat16 [2, 384, 1536], replicated, may hold values from -0.3125 to 0.3125
- inner_bias: float32 [3072], replicated, may hold values from -3 to 3
- outer_weight: bfloat16 [2, 1536, 384], replicated, may hold values from -0.15625 to 0.15625
- outer_bias: float32 [768], replicated, may hold values from -3 to 3
- second_gain: float32 [768], replicated, may hold values from 0.1 to 1.9
- second_shift: float32 [768], replicated, may hold values from -3 to 3
- cotangent: bfloat16 [64, 512, 768], P('dp', 'branch'), may hold values from -6 to 6
Outputs:
- output: bfloat16 [64, 512, 768], P('dp', 'branch')
- hidden_grad: float32 [64, 512, 768], P('dp', 'branch')
- query_weight_grad: float32 [768, 384], replicated
- query_bias_grad: float32 [384], replicated
- branch_keys_grad: float32 [2, 768, 384], P('branch')
- branch_values_grad: float32 [2, 768, 384], P('branch')
- branch_bias_grad: float32 [2, 384], P('branch')
- depth_kernel_grad: float32 [9, 768], replicated
- point_bias_grad: float32 [384], replicated
- kernel_weight_grad: float32 [384, 54], replicated
- kernel_bias_grad: float32 [54], replicated
- mixer_weight_grad: float32 [768, 768], replicated
- mixer_bias_grad: float32 [768], replicated
- first_gain_grad: float32 [768], replicated
- first_shift_grad: float32 [768], replicated
- inner_weight_grad: float32 [2, 384, 1536], replicated
- inner_bias_grad: float32 [3072], replicated
- outer_weight_grad: float32 [2, 1536, 384], replicated
- outer_bias_grad: float32 [768], replicated
- second_gain_grad: float32 [768], replicated
- second_shift_grad: float32 [768], replicated
The draws below stay inside these ranges and needn't reach their ends.
Inputs may be any that keep to these rules, and one draw needn't show every extreme that they name: `bounds`: column 0 of a row is the position of its first segment's separator and column 1 its count of valid positions: 1 <= column 0 <= column 1 - 2 and 128 <= column 1; some row has 512 valid positions.
All inputs are finite; a program needn't handle non-finite values.
Results may differ from the reference program's by a relative error of at most 0.02.
Values may be sent and summed in bfloat16 or wider, within the bound.
No kernel may reach another device: no remote copies, remote signals or barrier semaphores. Data moves between devices by JAX's collectives and lax.ppermute only.
A program may use at most 256 MiB of HBM per device.

```python
import math
import jax
import jax.numpy as jnp
from jax import lax

D = 768
HEADS = 6
HEAD_SIZE = 64
FF = 3072
GROUPS = 2
KERNEL = 9
SEQ = 512
ROWS = 64


def draw_bounds(key, part):
    key = jax.random.fold_in(key, 7)
    first_key, second_key, third_key = jax.random.split(key, 3)
    valid_length = jax.random.randint(first_key, (ROWS,), SEQ // 4, SEQ + 1)
    chosen = jax.random.randint(second_key, (), 0, ROWS)
    valid_length = jnp.where(jnp.arange(ROWS) == chosen, SEQ, valid_length)
    separator = jax.random.randint(third_key, (ROWS,), 1, valid_length - 1)
    return jnp.stack([separator, valid_length], axis=1).astype(jnp.int32)


def levels(key, extent, cuts, smallest, high):
    gain, own = 1.0, jax.random.fold_in(key, 6)
    for axis_at, parts in cuts:
        heights = jnp.exp(jax.random.uniform(jax.random.fold_in(own, axis_at), (parts,), jnp.float32, smallest / len(cuts), high / len(cuts)))
        gain = gain * jnp.repeat(heights, extent[axis_at] // parts).reshape([-1 if axis == axis_at else 1 for axis in range(len(extent))])
    return gain


def centred(own_key, extent, width, bound, cuts=(), kind=jnp.bfloat16):
    values = width * jax.random.normal(own_key, extent, jnp.float32)
    if cuts:
        values = values * levels(own_key, extent, cuts, -0.22, 0.18)
    return jnp.clip(values, -bound, bound).astype(kind)


def setup_inputs(seed: int = 0) -> dict:
    arg_keys = jax.random.split(jax.random.key(seed), 23)
    hidden = centred(arg_keys[0], (ROWS, SEQ, D), 1.0, 6.0, ((0, 16),))
    bounds = draw_bounds(jax.random.fold_in(arg_keys[22], 71), 0)
    query_weight = centred(arg_keys[2], (D, HEADS * HEAD_SIZE), D ** -0.5, 0.21875)
    query_bias = centred(arg_keys[3], (HEADS * HEAD_SIZE,), 0.5, 3.0, (), jnp.float32)
    branch_keys = centred(arg_keys[4], (2, D, HEADS * HEAD_SIZE), D ** -0.5, 0.21875, ((0, 2),))
    branch_values = centred(arg_keys[5], (2, D, HEADS * HEAD_SIZE), (D // 16) ** -0.5, 0.875, ((0, 2),))
    branch_bias = centred(arg_keys[6], (2, HEADS * HEAD_SIZE), 1.0, 6.0, ((0, 2),), jnp.float32)
    depth_kernel = centred(arg_keys[7], (KERNEL, D), KERNEL ** -0.5, 2.0, (), jnp.float32)
    point_bias = centred(arg_keys[8], (HEADS * HEAD_SIZE,), 0.5, 3.0, (), jnp.float32)
    kernel_weight = centred(arg_keys[9], (HEADS * HEAD_SIZE, HEADS * KERNEL), (HEADS * HEAD_SIZE) ** -0.5, 0.3125)
    kernel_bias = centred(arg_keys[10], (HEADS * KERNEL,), 0.5, 3.0, (), jnp.float32)
    mixer_weight = centred(arg_keys[11], (D, D), D ** -0.5, 0.21875)
    mixer_bias = centred(arg_keys[12], (D,), 0.5, 3.0, (), jnp.float32)
    first_gain = jnp.clip(1.0 + 0.18 * jax.random.normal(arg_keys[13], (D,), jnp.float32), 0.1, 1.9)
    first_shift = centred(arg_keys[14], (D,), 0.5, 3.0, (), jnp.float32)
    inner_weight = centred(arg_keys[15], (GROUPS, D // GROUPS, FF // GROUPS), (D // GROUPS) ** -0.5, 0.3125)
    inner_bias = centred(arg_keys[16], (FF,), 0.5, 3.0, (), jnp.float32)
    outer_weight = centred(arg_keys[17], (GROUPS, FF // GROUPS, D // GROUPS), (FF // GROUPS) ** -0.5, 0.15625)
    outer_bias = centred(arg_keys[18], (D,), 0.5, 3.0, (), jnp.float32)
    second_gain = jnp.clip(1.0 + 0.18 * jax.random.normal(arg_keys[19], (D,), jnp.float32), 0.1, 1.9)
    second_shift = centred(arg_keys[20], (D,), 0.5, 3.0, (), jnp.float32)
    cotangent = centred(arg_keys[21], (ROWS, SEQ, D), 1.0, 6.0, ((0, 16), (1, 2)))
    return dict(hidden=hidden, bounds=bounds, query_weight=query_weight, query_bias=query_bias, branch_keys=branch_keys, branch_values=branch_values, branch_bias=branch_bias, depth_kernel=depth_kernel, point_bias=point_bias, kernel_weight=kernel_weight, kernel_bias=kernel_bias, mixer_weight=mixer_weight, mixer_bias=mixer_bias, first_gain=first_gain, first_shift=first_shift, inner_weight=inner_weight, inner_bias=inner_bias, outer_weight=outer_weight, outer_bias=outer_bias, second_gain=second_gain, second_shift=second_shift, cotangent=cotangent)


@jax.custom_vjp
def low(v):
    return lax.optimization_barrier(v.astype(jnp.bfloat16)).astype(jnp.float32)

@jax.custom_vjp
def low_back(v):
    return v

def low_keep(v):
    return (low(v), None)

def low_pass(kept, grad):
    return (grad,)

def back_keep(v):
    return (v, None)

def back_low(kept, grad):
    return (low(grad),)
low.defvjp(low_keep, low_pass)
low_back.defvjp(back_keep, back_low)
HIGHEST = lax.Precision.HIGHEST
NEGATIVE = -1000000000.0
EPSILON = 1e-05

def shifted(source, offset, filler, radius):
    padding = [(0, 0)] * source.ndim
    padding[1] = (radius, radius)
    padded = jnp.pad(source, padding, constant_values=filler)
    return lax.slice_in_dim(padded, radius + offset, radius + offset + source.shape[1], axis=1)

def project(source, matrix):
    return jnp.einsum('rsd,de->rse', source, matrix, precision=HIGHEST)

def grouped(source, matrix):
    row_count, length = (source.shape[0], source.shape[1])
    split_source = source.reshape(row_count, length, matrix.shape[0], matrix.shape[1])
    return jnp.einsum('rsgi,gio->rsgo', split_source, matrix, precision=HIGHEST).reshape(row_count, length, -1)

def layer_norm(source, gain_vector, shift_vector):
    center = source - lax.optimization_barrier(jnp.mean(source, axis=-1, keepdims=True))
    spread = lax.optimization_barrier(jnp.mean(center * center, axis=-1, keepdims=True))
    return center * lax.rsqrt(spread + EPSILON) * gain_vector + shift_vector

def softmax_last(scores):
    row_peak = lax.optimization_barrier(jnp.max(scores, axis=-1, keepdims=True))
    raised = jnp.exp(scores - row_peak)
    return raised / lax.optimization_barrier(jnp.sum(raised, axis=-1, keepdims=True))

def segment_ids(bounds, length):
    position = jnp.arange(length, dtype=jnp.int32)[None, :]
    inner_ids = jnp.where(position < bounds[:, 1:2], 1, 2)
    return jnp.where(position <= bounds[:, 0:1], 0, inner_ids).astype(jnp.int32)

def layer_rows(params, hidden, bounds):
    query_weight, query_bias, branch_keys, branch_values, branch_bias, depth_kernel, point_bias, kernel_weight, kernel_bias, mixer_weight, mixer_bias, first_gain, first_shift, inner_weight, inner_bias, outer_weight, outer_bias, second_gain, second_shift = params
    row_count, length = (hidden.shape[0], hidden.shape[1])
    radius = KERNEL // 2

    def to_heads(source):
        return source.reshape(row_count, length, HEADS, HEAD_SIZE)
    query_attend = low_back(low(project(hidden, query_weight) + query_bias))
    key_attend = low_back(low(project(hidden, branch_keys[0])))
    value_attend = low_back(low(project(hidden, branch_values[0]) + branch_bias[0]))
    scores = jnp.einsum('rqhe,rkhe->rhqk', to_heads(query_attend), to_heads(key_attend), precision=HIGHEST) * HEAD_SIZE ** (-0.5)
    position = jnp.arange(length, dtype=jnp.int32)
    visible = position[None, None, None, :] < bounds[:, 1][:, None, None, None]
    scores = low_back(jnp.where(visible, scores, NEGATIVE))
    attend_weights = low(softmax_last(scores))
    attended = jnp.einsum('rhqk,rkhe->rqhe', attend_weights, to_heads(value_attend), precision=HIGHEST)
    attended = low_back(low(attended.reshape(row_count, length, -1)))
    query_kernel = low_back(low(project(hidden, query_weight) + query_bias))
    depth_sum = jnp.zeros_like(hidden)
    for tap_index in range(KERNEL):
        depth_sum = depth_sum + shifted(hidden, tap_index - radius, 0.0, radius) * depth_kernel[tap_index]
    depth_mixed = low_back(low(depth_sum))
    key_kernel = low_back(project(depth_mixed, branch_keys[1]) + point_bias)
    joint_key = low_back(low(key_kernel * query_kernel))
    logits = low_back(jnp.einsum('rsa,ac->rsc', joint_key, kernel_weight, precision=HIGHEST) + kernel_bias)
    logits = logits.reshape(row_count, length, HEADS, KERNEL)
    segment = segment_ids(bounds, length)
    same_segment = jnp.stack([shifted(segment, tap_index - radius, -1, radius) == segment for tap_index in range(KERNEL)], axis=-1)
    tap_weights = softmax_last(jnp.where(same_segment[:, :, None, :], logits, NEGATIVE))
    value_kernel = to_heads(low_back(low(project(hidden, branch_values[1]) + branch_bias[1])))
    conv_sum = jnp.zeros_like(value_kernel)
    for tap_index in range(KERNEL):
        conv_sum = conv_sum + tap_weights[..., tap_index:tap_index + 1] * shifted(value_kernel, tap_index - radius, 0.0, radius)
    convolved = low_back(low(conv_sum.reshape(row_count, length, -1)))
    concat = jnp.concatenate([attended, convolved], axis=-1)
    mixed_out = low_back(project(concat, mixer_weight) + mixer_bias)
    first_out = low(layer_norm(hidden + mixed_out, first_gain, first_shift))
    inner_pre = low_back(grouped(first_out, inner_weight) + inner_bias)
    active = low_back(low(jax.nn.gelu(inner_pre, approximate=False)))
    projected = low_back(grouped(active, outer_weight) + outer_bias)
    return layer_norm(first_out + projected, second_gain, second_shift)

def reference(hidden, bounds, query_weight, query_bias, branch_keys, branch_values, branch_bias, depth_kernel, point_bias, kernel_weight, kernel_bias, mixer_weight, mixer_bias, first_gain, first_shift, inner_weight, inner_bias, outer_weight, outer_bias, second_gain, second_shift, cotangent):
    params = tuple((member.astype(jnp.float32) for member in (query_weight, query_bias, branch_keys, branch_values, branch_bias, depth_kernel, point_bias, kernel_weight, kernel_bias, mixer_weight, mixer_bias, first_gain, first_shift, inner_weight, inner_bias, outer_weight, outer_bias, second_gain, second_shift)))
    hidden_float = hidden.astype(jnp.float32)
    row_total = hidden.shape[0]
    group_rows = math.gcd(row_total, 8)

    def forward(weights, source):

        def one_block(block_pair):
            return layer_rows(weights, block_pair[0], block_pair[1])
        blocks = source.reshape(row_total // group_rows, group_rows, SEQ, D)
        bound_blocks = bounds.reshape(row_total // group_rows, group_rows, 2)
        result = lax.map(jax.checkpoint(one_block), (blocks, bound_blocks))
        return result.reshape(row_total, SEQ, D)
    output, pullback = jax.vjp(forward, params, hidden_float)
    weight_grads, hidden_grad = pullback(cotangent.astype(jnp.float32))
    grad_query_weight, grad_query_bias, grad_keys, grad_values, grad_branch_bias, grad_depth, grad_point_bias, grad_kernel, grad_kernel_bias, grad_mixer_weight, grad_mixer_bias, grad_first_gain, grad_first_shift, grad_inner_weight, grad_inner_bias, grad_outer_weight, grad_outer_bias, grad_second_gain, grad_second_shift = weight_grads
    return (output.astype(jnp.bfloat16), hidden_grad, grad_query_weight, grad_query_bias, grad_keys, grad_values, grad_branch_bias, grad_depth, grad_point_bias, grad_kernel, grad_kernel_bias, grad_mixer_weight, grad_mixer_bias, grad_first_gain, grad_first_shift, grad_inner_weight, grad_inner_bias, grad_outer_weight, grad_outer_bias, grad_second_gain, grad_second_shift)
```

```python
import functools

import jax
import jax.numpy as jnp
import numpy as np
from jax import lax
from jax.experimental import pallas as pl
from jax.experimental.pallas import tpu as pltpu
from jax.sharding import PartitionSpec as P

HEADS = 6
HEAD_SIZE = 64
KERNEL = 9
RADIUS = KERNEL // 2
SLAB = 8
LANES = 128
PAD = 8

NEGATIVE = -1000000000.0
EPSILON = 1e-05
INV_ROOT_TAU = 0.3989422804014327
TAIL_SLOPE = 0.36
TAIL_TERMS = (
    0.14361732768142335,
    0.14369104425682297,
    0.12391285318517967,
    0.09656500864495021,
    -0.002026438221833662,
    0.11038580625572408,
    -0.22684055188970365,
    0.1413848307004008,
    -0.030689918446024287,
)

BF = jnp.bfloat16
F32 = jnp.float32
VMEM_LIMIT = 62 * 1024 * 1024


def mm(left, right):
    return jnp.dot(left, right, preferred_element_type=F32)


def mm_nt(left, right):
    return lax.dot_general(left, right, (((1,), (1,)), ((), ())), preferred_element_type=F32)


def rowsum(value):
    return jnp.sum(value, axis=0, keepdims=True)


def fill_strips(strips_ref, value, length):
    strips = strips_ref.shape[0]
    zero = jnp.zeros((PAD, LANES), F32)
    for strip in range(strips):
        strips_ref[strip, 0:PAD, :] = zero
        strips_ref[strip, PAD + length : 2 * PAD + length, :] = zero
        strips_ref[strip, PAD : PAD + length, :] = value[
            :, strip * LANES : (strip + 1) * LANES
        ].astype(F32)


def head_pair_rows(rows, head):
    own = rows[head * HEAD_SIZE : (head + 1) * HEAD_SIZE, :]
    zero = jnp.zeros_like(own)
    return jnp.concatenate([own, zero] if head % 2 == 0 else [zero, own], axis=0)


def forward_kernel(
    place,
    bounds,
    x_ref,
    wq_ref,
    bq_ref,
    wa_ref,
    wb_ref,
    bb_ref,
    depth_ref,
    pb_ref,
    kwt_ref,
    kb_ref,
    spread_ref,
    *rest,
):
    (
        cat_ref,
        q_ref,
        k_ref,
        v_ref,
        probs_ref,
        att_t_ref,
        dm_ref,
        kc_ref,
        cq_ref,
        joint_ref,
        taps_ref,
        vc_ref,
        qt_s,
        vt_s,
        xs_s,
        vs_s,
        tw_s,
        wide_s,
    ) = rest[-18:]
    row = place[0] + pl.program_id(0)
    first_end = bounds[row, 0]
    valid = bounds[row, 1]
    length = x_ref.shape[1]
    x = x_ref[0]
    queries = (mm(x, wq_ref[...]) + bq_ref[...]).astype(BF)

    @pl.when(place[1] == 1)
    def _():
        scaled = (queries.astype(F32) * (HEAD_SIZE**-0.5)).astype(BF)
        q_ref[0] = scaled
        qt_s[...] = scaled.T
        k_ref[0] = mm(x, wa_ref[...]).astype(BF)
        v = (mm(x, wb_ref[...]) + bb_ref[...]).astype(BF)
        v_ref[0] = v
        vt_s[...] = v.T
        seen = lax.broadcasted_iota(jnp.int32, (length, 1), 0) < valid
        for head in range(HEADS):
            pair = head // 2
            keys = k_ref[0, :, pair * LANES : (pair + 1) * LANES]
            scores = mm(keys, head_pair_rows(qt_s, head))
            scores = jnp.where(seen, scores, NEGATIVE)
            raised = jnp.exp(scores - jnp.max(scores, axis=0, keepdims=True))
            probs = (raised * (1.0 / rowsum(raised))).astype(BF)
            probs_ref[0, head] = probs
            span = slice(head * HEAD_SIZE, (head + 1) * HEAD_SIZE)
            att_t_ref[0, span, :] = mm(vt_s[span, :], probs).astype(BF)
        cat_ref[0] = att_t_ref[0].T

    @pl.when(place[1] == 0)
    def _():
        fill_strips(xs_s, x, length)
        piece = LANES
        for strip in range(xs_s.shape[0]):
            lanes = slice(strip * LANES, (strip + 1) * LANES)
            for at in range(0, length, piece):
                total = None
                for tap in range(KERNEL):
                    begin = PAD - RADIUS + tap + at
                    term = xs_s[strip, begin : begin + piece, :] * depth_ref[tap : tap + 1, lanes]
                    total = term if total is None else total + term
                dm_ref[0, at : at + piece, lanes] = total.astype(BF)
        key_conv = mm(dm_ref[0], wa_ref[...]) + pb_ref[...]
        kc_ref[0] = key_conv
        cq_ref[0] = queries
        joint = (key_conv * queries.astype(F32)).astype(BF)
        joint_ref[0] = joint
        logits = mm_nt(kwt_ref[...], joint) + kb_ref[:, 0:1]
        here = lax.broadcasted_iota(jnp.int32, (SLAB, length), 1)

        def segment(position):
            return jnp.where(position <= first_end, 0, jnp.where(position < valid, 1, 2))

        own_segment = segment(here)
        slabs = []
        for tap in range(KERNEL):
            other = here + (tap - RADIUS)
            same = (other >= 0) & (other < length) & (segment(other) == own_segment)
            slabs.append(jnp.where(same, logits[tap * SLAB : (tap + 1) * SLAB], NEGATIVE))
        peak = functools.reduce(jnp.maximum, slabs)
        slabs = [jnp.exp(slab - peak) for slab in slabs]
        inverse = 1.0 / functools.reduce(jnp.add, slabs)
        for tap in range(KERNEL):
            tw_s[tap * SLAB : (tap + 1) * SLAB, :] = slabs[tap] * inverse
        tw_s[KERNEL * SLAB :, :] = jnp.zeros((LANES - KERNEL * SLAB, length), F32)
        taps_ref[0] = tw_s[...]
        taps = tw_s[...].T
        high = taps.astype(BF)
        low = (taps - high.astype(F32)).astype(BF)
        both = jnp.concatenate([high, low], axis=1)
        width = HEADS * HEAD_SIZE
        for tap in range(KERNEL):
            cols = slice(tap * width, (tap + 1) * width)
            wide_s[:, cols] = mm(both, spread_ref[:, cols])
        vc = (mm(x, wb_ref[...]) + bb_ref[...]).astype(BF)
        vc_ref[0] = vc
        fill_strips(vs_s, vc, length)
        for strip in range(vs_s.shape[0]):
            for at in range(0, length, piece):
                total = None
                for tap in range(KERNEL):
                    begin = PAD - RADIUS + tap + at
                    col = tap * width + strip * LANES
                    term = (
                        vs_s[strip, begin : begin + piece, :]
                        * wide_s[at : at + piece, col : col + LANES]
                    )
                    total = term if total is None else total + term
                cat_ref[0, at : at + piece, strip * LANES : (strip + 1) * LANES] = total.astype(BF)


def spread_table():
    table = np.zeros((2 * LANES, KERNEL, HEADS, HEAD_SIZE), np.float32)
    for tap in range(KERNEL):
        for head in range(HEADS):
            table[tap * SLAB + head, tap, head, :] = 1
            table[LANES + tap * SLAB + head, tap, head, :] = 1
    return jnp.asarray(table.reshape(2 * LANES, -1), BF)


def gather_table():
    table = np.zeros((KERNEL, HEADS, HEAD_SIZE, LANES), np.float32)
    for tap in range(KERNEL):
        for head in range(HEADS):
            table[tap, head, :, tap * SLAB + head] = 1
    return jnp.asarray(table.reshape(-1, LANES), BF)


def whole(array):
    rank = array.ndim
    return pl.BlockSpec(array.shape, lambda *_: (0,) * rank)


def forward(place, bounds, hidden, weights, rows, before=None):
    length, features = hidden.shape[1:]
    width = HEADS * HEAD_SIZE
    spare = rows

    def att_row(r, place, bounds):
        return jnp.where(place[1] == 1, r, spare)

    def conv_row(r, place, bounds):
        return jnp.where(place[1] == 0, r, spare)

    def saved(row_of, shape, dtype):
        zeros = (0,) * len(shape)
        return (
            jax.ShapeDtypeStruct((rows + 1,) + shape, dtype),
            pl.BlockSpec((1,) + shape, lambda r, p, b: (row_of(r, p, b),) + zeros),
        )

    outs = [
        (
            jax.ShapeDtypeStruct((rows, length, 2 * width), BF),
            pl.BlockSpec((1, length, width), lambda r, p, b: (r, 0, 1 - p[1])),
        ),
        saved(att_row, (length, width), BF),
        saved(att_row, (length, width), BF),
        saved(att_row, (length, width), BF),
        saved(att_row, (HEADS, length, length), BF),
        saved(att_row, (width, length), BF),
        saved(conv_row, (length, features), BF),
        saved(conv_row, (length, width), F32),
        saved(conv_row, (length, width), BF),
        saved(conv_row, (length, width), BF),
        saved(conv_row, (LANES, length), F32),
        saved(conv_row, (length, width), BF),
    ]
    in_specs = [pl.BlockSpec((1, length, features), lambda r, p, b: (p[0] + r, 0, 0))]
    in_specs += [whole(w) for w in weights]
    args = [place, bounds, hidden, *weights]
    aliases = {}
    if before is not None:
        aliases = {len(args) + i: i for i in range(len(before))}
        in_specs += [pl.BlockSpec(memory_space=pl.ANY)] * len(before)
        args += list(before)
    return pl.pallas_call(
        forward_kernel,
        out_shape=[o[0] for o in outs],
        grid_spec=pltpu.PrefetchScalarGridSpec(
            num_scalar_prefetch=2,
            grid=(rows,),
            in_specs=in_specs,
            out_specs=[o[1] for o in outs],
            scratch_shapes=[
                pltpu.VMEM((width, length), BF),
                pltpu.VMEM((width, length), BF),
                pltpu.VMEM((features // LANES, length + 2 * PAD, LANES), F32),
                pltpu.VMEM((width // LANES, length + 2 * PAD, LANES), F32),
                pltpu.VMEM((LANES, length), F32),
                pltpu.VMEM((length, KERNEL * width), F32),
            ],
        ),
        input_output_aliases=aliases,
        compiler_params=pltpu.CompilerParams(vmem_limit_bytes=VMEM_LIMIT),
        name="branch_forward",
    )(*args)


def norm(value):
    center = value - jnp.mean(value, axis=-1, keepdims=True)
    factor = lax.rsqrt(jnp.mean(center * center, axis=-1, keepdims=True) + EPSILON)
    return center * factor, factor


def norm_back(gradient, normed, factor):
    return factor * (
        gradient
        - jnp.mean(gradient, axis=-1, keepdims=True)
        - normed * jnp.mean(gradient * normed, axis=-1, keepdims=True)
    )


def middle_kernel(
    place,
    x_ref,
    cat_ref,
    cot_own_ref,
    cot_got_ref,
    mw_ref,
    mb_ref,
    g1_ref,
    b1_ref,
    iw_ref,
    ib_ref,
    ow_ref,
    ob_ref,
    g2_ref,
    b2_ref,
    own_ref,
    send_ref,
    dcat_ref,
    datt_ref,
    dmix_ref,
    grad_ref,
    vec_ref,
    acc_i,
    acc_o,
    acc_m,
    act_s,
    slope_s,
    din_s,
):
    step = pl.program_id(0)
    half = step % 2
    mine = half == place[1]
    features = x_ref.shape[2]
    groups, width, inner = iw_ref.shape
    piece = 512

    @pl.when(step == 0)
    def _():
        acc_i[...] = jnp.zeros_like(acc_i)
        acc_o[...] = jnp.zeros_like(acc_o)
        acc_m[...] = jnp.zeros_like(acc_m)
        vec_ref[...] = jnp.zeros_like(vec_ref)

    cat = cat_ref[0]
    normed1, factor1 = norm(x_ref[0].astype(F32) + (mm(cat, mw_ref[...]) + mb_ref[...]))
    first = (normed1 * g1_ref[...] + b1_ref[...]).astype(BF)
    projected = []
    for g in range(groups):
        part = first[:, g * width : (g + 1) * width]
        for at in range(0, inner, piece):
            lanes = slice(g * inner + at, g * inner + at + piece)
            pre = mm(part, iw_ref[g, :, at : at + piece]) + ib_ref[:, lanes]
            bell = jnp.exp(-0.5 * pre * pre)
            t = 1.0 / (1.0 + TAIL_SLOPE * jnp.abs(pre))
            tail = jnp.full_like(t, TAIL_TERMS[-1])
            for term in TAIL_TERMS[-2::-1]:
                tail = tail * t + term
            tail = bell * (t * tail)
            phi = jnp.where(pre >= 0, 1.0 - tail, tail)
            act_s[:, lanes] = (pre * phi).astype(BF)
            slope_s[:, lanes] = phi + pre * (bell * INV_ROOT_TAU)
        projected.append(mm(act_s[:, g * inner : (g + 1) * inner], ow_ref[g]))
    projected = jnp.concatenate(projected, axis=1)
    normed2, factor2 = norm(first.astype(F32) + (projected + ob_ref[...]))
    output = (normed2 * g2_ref[...] + b2_ref[...]).astype(BF)

    @pl.when(mine)
    def _():
        own_ref[0] = output

    @pl.when(jnp.logical_not(mine))
    def _():
        send_ref[0] = output

    cot = jnp.where(mine, cot_own_ref[0].astype(F32), cot_got_ref[0].astype(F32))
    dsecond = norm_back(cot * g2_ref[...], normed2, factor2)
    dproj = dsecond.astype(BF)
    vec_ref[1:2, 3 * features : 4 * features] += rowsum(dproj.astype(F32))
    vec_ref[2:3, 0:features] += rowsum(cot * normed2)
    vec_ref[2:3, features : 2 * features] += rowsum(cot)
    dfirst = []
    for g in range(groups):
        cols = slice(g * width, (g + 1) * width)
        dpart = dproj[:, cols]
        for at in range(0, inner, piece):
            lanes = slice(g * inner + at, g * inner + at + piece)
            dact = mm_nt(dpart, ow_ref[g, at : at + piece, :]).astype(BF)
            din = (dact.astype(F32) * slope_s[:, lanes]).astype(BF)
            din_s[:, lanes] = din
            vec_ref[0:1, lanes] += rowsum(din.astype(F32))
        group = slice(g * inner, (g + 1) * inner)
        acc_o[g] += mm(dpart.T, act_s[:, group])
        acc_i[g] += mm(first[:, cols].T, din_s[:, group])
        dfirst.append(dsecond[:, cols] + mm_nt(din_s[:, group], iw_ref[g]))
    dfirst = jnp.concatenate(dfirst, axis=1)
    vec_ref[1:2, features : 2 * features] += rowsum(dfirst * normed1)
    vec_ref[1:2, 2 * features : 3 * features] += rowsum(dfirst)
    dmixed = norm_back(dfirst * g1_ref[...], normed1, factor1)
    dmix_ref[0] = dmixed
    dmixer = dmixed.astype(BF)
    vec_ref[1:2, 0:features] += rowsum(dmixer.astype(F32))
    acc_m[...] += mm(cat.T, dmixer)
    dcat_ref[0] = mm_nt(dmixer, mw_ref[...]).astype(BF)
    datt_ref[0] = mm_nt(mw_ref[0:width, :], dmixer).astype(BF)

    @pl.when(step == pl.num_programs(0) - 1)
    def _():
        for g in range(groups):
            grad_ref[g * width : (g + 1) * width, :] = acc_i[g].astype(BF)
            grad_ref[(groups + g) * width : (groups + g + 1) * width, :] = acc_o[g].astype(BF)
        grad_ref[2 * groups * width :, 0:features] = acc_m[0:width, :].astype(BF)
        grad_ref[2 * groups * width :, features:] = acc_m[width:, :].astype(BF)


def middle(place, hidden, cat, cot_own, cot_got, weights, rows):
    length, features = hidden.shape[1:]
    half = length // 2
    groups, width, inner = weights[4].shape

    def per_chunk(shape, dtype):
        return (
            jax.ShapeDtypeStruct((rows, length, shape), dtype),
            pl.BlockSpec((1, half, shape), lambda s, p: (s // 2, s % 2, 0)),
        )

    per_row = (
        jax.ShapeDtypeStruct((rows, half, features), BF),
        pl.BlockSpec((1, half, features), lambda s, p: (s // 2, 0, 0)),
    )
    outs = [
        per_row,
        per_row,
        per_chunk(features, BF),
        (
            jax.ShapeDtypeStruct((rows, width, length), BF),
            pl.BlockSpec((1, width, half), lambda s, p: (s // 2, 0, s % 2)),
        ),
        per_chunk(features, F32),
        (
            jax.ShapeDtypeStruct((5 * width, inner), BF),
            pl.BlockSpec((5 * width, inner), lambda s, p: (0, 0)),
        ),
        (
            jax.ShapeDtypeStruct((SLAB, groups * inner), F32),
            pl.BlockSpec((SLAB, groups * inner), lambda s, p: (0, 0)),
        ),
    ]
    return pl.pallas_call(
        middle_kernel,
        out_shape=[o[0] for o in outs],
        grid_spec=pltpu.PrefetchScalarGridSpec(
            num_scalar_prefetch=1,
            grid=(2 * rows,),
            in_specs=[
                pl.BlockSpec((1, half, features), lambda s, p: (p[0] + s // 2, s % 2, 0)),
                pl.BlockSpec((1, half, features), lambda s, p: (s // 2, s % 2, 0)),
                pl.BlockSpec((1, half, features), lambda s, p: (p[0] + s // 2, 0, 0)),
                pl.BlockSpec((1, half, features), lambda s, p: (s // 2, 0, 0)),
                *[whole(w) for w in weights],
            ],
            out_specs=[o[1] for o in outs],
            scratch_shapes=[
                pltpu.VMEM((groups, width, inner), F32),
                pltpu.VMEM((groups, width, inner), F32),
                pltpu.VMEM((features, features), F32),
                pltpu.VMEM((half, groups * inner), BF),
                pltpu.VMEM((half, groups * inner), F32),
                pltpu.VMEM((half, groups * inner), BF),
            ],
        ),
        compiler_params=pltpu.CompilerParams(vmem_limit_bytes=VMEM_LIMIT),
        name="shared_layers",
    )(place, hidden, cat, cot_own, cot_got, *weights)


def conv_back_kernel(
    place,
    x_ref,
    dcat_ref,
    dmix_ref,
    dm_ref,
    kc_ref,
    q_ref,
    joint_ref,
    taps_ref,
    vc_ref,
    wa_ref,
    wb_ref,
    depth_ref,
    kwt_ref,
    spread_ref,
    collect_ref,
    part_ref,
    dq_ref,
    grad_ref,
    small_ref,
    kgrad_ref,
    vs_s,
    xs_s,
    ys_s,
    ds_s,
    prod_s,
    acc_a,
    acc_b,
):
    step = pl.program_id(0)
    length, features = x_ref.shape[1:]
    width = HEADS * HEAD_SIZE
    piece = LANES

    @pl.when(step == 0)
    def _():
        acc_a[...] = jnp.zeros_like(acc_a)
        acc_b[...] = jnp.zeros_like(acc_b)
        small_ref[...] = jnp.zeros_like(small_ref)
        kgrad_ref[...] = jnp.zeros_like(kgrad_ref)

    x = x_ref[0]
    dconv = dcat_ref[0].astype(F32)
    fill_strips(vs_s, vc_ref[0], length)
    taps_t = taps_ref[0]
    taps = taps_t.T
    high = taps.astype(BF)
    low = (taps - high.astype(F32)).astype(BF)
    both = jnp.concatenate([high, low], axis=1)
    zero = jnp.zeros((PAD, LANES), F32)
    for tap in range(KERNEL):
        spread = mm(both, spread_ref[:, tap * width : (tap + 1) * width])
        for strip in range(width // LANES):
            lanes = slice(strip * LANES, (strip + 1) * LANES)
            begin = PAD - RADIUS + tap
            prod_s[:, tap * width + strip * LANES : tap * width + (strip + 1) * LANES] = (
                dconv[:, lanes] * vs_s[strip, begin : begin + length, :]
            ).astype(BF)
            slot = tap * (width // LANES) + strip
            ys_s[slot, 0:PAD, :] = zero
            ys_s[slot, PAD + length :, :] = zero
            ys_s[slot, PAD : PAD + length, :] = spread[:, lanes] * dconv[:, lanes]
    dvc = []
    for strip in range(width // LANES):
        total = None
        for tap in range(KERNEL):
            begin = PAD + RADIUS - tap
            term = ys_s[tap * (width // LANES) + strip, begin : begin + length, :]
            total = term if total is None else total + term
        dvc.append(total.astype(BF))
    dvc = jnp.concatenate(dvc, axis=1)
    dtaps = mm(prod_s[...], collect_ref[...]).T
    slabs = [dtaps[t * SLAB : (t + 1) * SLAB] for t in range(KERNEL)]
    weights = [taps_t[t * SLAB : (t + 1) * SLAB] for t in range(KERNEL)]
    total = functools.reduce(jnp.add, [a * b for a, b in zip(slabs, weights)])
    slabs = [b * (a - total) for a, b in zip(slabs, weights)]
    slabs.append(jnp.zeros((LANES - KERNEL * SLAB, length), F32))
    dlogits_t = jnp.concatenate(slabs, axis=0)
    dlogits = dlogits_t.T.astype(BF)
    rounded_t = dlogits_t.astype(BF)
    kgrad_ref[:, 0:width] += mm(rounded_t, joint_ref[0])
    kgrad_ref[:, width : width + LANES] += jnp.broadcast_to(
        jnp.sum(rounded_t.astype(F32), axis=1, keepdims=True), (LANES, LANES)
    )
    djoint = mm(dlogits, kwt_ref[...]).astype(BF).astype(F32)
    dkey = (djoint * q_ref[0].astype(F32)).astype(BF)
    dq_ref[0] = (djoint * kc_ref[0]).astype(BF)
    small_ref[9:10, 0:width] += rowsum(dkey.astype(F32))
    small_ref[9:10, width : 2 * width] += rowsum(dvc.astype(F32))
    ddepth = mm_nt(dkey, wa_ref[...]).astype(BF)
    acc_a[...] += mm(dm_ref[0].T, dkey)
    acc_b[...] += mm(x.T, dvc)
    part_ref[0] = dmix_ref[0] + mm_nt(dvc, wb_ref[...])
    fill_strips(ds_s, ddepth, length)
    fill_strips(xs_s, x, length)
    for strip in range(features // LANES):
        lanes = slice(strip * LANES, (strip + 1) * LANES)
        sums = [None] * KERNEL
        for at in range(0, length, piece):
            total = part_ref[0, at : at + piece, lanes]
            center = ds_s[strip, PAD + at : PAD + at + piece, :]
            for tap in range(KERNEL):
                begin = PAD + RADIUS - tap + at
                total = total + ds_s[strip, begin : begin + piece, :] * depth_ref[tap : tap + 1, lanes]
                begin = PAD - RADIUS + tap + at
                term = (xs_s[strip, begin : begin + piece, :] * center).reshape(-1, SLAB, LANES)
                term = jnp.sum(term, axis=0)
                sums[tap] = term if sums[tap] is None else sums[tap] + term
            part_ref[0, at : at + piece, lanes] = total
        for tap in range(KERNEL):
            small_ref[tap : tap + 1, lanes] += rowsum(sums[tap])

    @pl.when(step == pl.num_programs(0) - 1)
    def _():
        grad_ref[0] = acc_a[...].astype(BF)
        grad_ref[1] = acc_b[...].astype(BF)


def conv_back(place, hidden, dcat, dmix, kept, weights, rows):
    length, features = hidden.shape[1:]
    width = HEADS * HEAD_SIZE

    def by_row(array):
        zeros = (0,) * (array.ndim - 1)
        return pl.BlockSpec((1,) + array.shape[1:], lambda r, p: (r,) + zeros)

    outs = [
        (
            jax.ShapeDtypeStruct((rows, length, features), F32),
            pl.BlockSpec((1, length, features), lambda r, p: (r, 0, 0)),
        ),
        (
            jax.ShapeDtypeStruct((rows, length, width), BF),
            pl.BlockSpec((1, length, width), lambda r, p: (r, 0, 0)),
        ),
        (
            jax.ShapeDtypeStruct((2, features, width), BF),
            pl.BlockSpec((2, features, width), lambda r, p: (0, 0, 0)),
        ),
        (
            jax.ShapeDtypeStruct((16, features), F32),
            pl.BlockSpec((16, features), lambda r, p: (0, 0)),
        ),
        (
            jax.ShapeDtypeStruct((LANES, width + LANES), F32),
            pl.BlockSpec((LANES, width + LANES), lambda r, p: (0, 0)),
        ),
    ]
    strips = features // LANES
    return pl.pallas_call(
        conv_back_kernel,
        out_shape=[o[0] for o in outs],
        grid_spec=pltpu.PrefetchScalarGridSpec(
            num_scalar_prefetch=1,
            grid=(rows,),
            in_specs=[
                pl.BlockSpec((1, length, features), lambda r, p: (p[0] + r, 0, 0)),
                pl.BlockSpec((1, length, width), lambda r, p: (r, 0, 1)),
                by_row(dmix),
                *[by_row(a) for a in kept],
                *[whole(w) for w in weights],
            ],
            out_specs=[o[1] for o in outs],
            scratch_shapes=[
                pltpu.VMEM((width // LANES, length + 2 * PAD, LANES), F32),
                pltpu.VMEM((strips, length + 2 * PAD, LANES), F32),
                pltpu.VMEM((KERNEL * width // LANES, length + 2 * PAD, LANES), F32),
                pltpu.VMEM((strips, length + 2 * PAD, LANES), F32),
                pltpu.VMEM((length, KERNEL * width), BF),
                pltpu.VMEM((features, width), F32),
                pltpu.VMEM((features, width), F32),
            ],
        ),
        compiler_params=pltpu.CompilerParams(vmem_limit_bytes=VMEM_LIMIT),
        name="convolution_backward",
    )(place, hidden, dcat, dmix, *kept, *weights)


def att_back_kernel(
    place,
    x_ref,
    dcat_ref,
    datt_ref,
    part_ref,
    dqc_ref,
    q_ref,
    k_ref,
    v_ref,
    probs_ref,
    att_t_ref,
    wq_ref,
    wk_ref,
    wv_ref,
    own_ref,
    send_ref,
    grad_ref,
    small_ref,
    kt_s,
    dqt_s,
    dk_s,
    dv_s,
    total_s,
    acc_s,
):
    step = pl.program_id(0)
    length, features = x_ref.shape[1:]
    width = HEADS * HEAD_SIZE

    @pl.when(step == 0)
    def _():
        acc_s[...] = jnp.zeros_like(acc_s)
        small_ref[...] = jnp.zeros_like(small_ref)

    scaled_keys = (k_ref[0].astype(F32) * (HEAD_SIZE**-0.5)).astype(BF)
    kt_s[...] = scaled_keys.T
    low_lane = lax.broadcasted_iota(jnp.int32, (1, LANES), 1) < HEAD_SIZE
    for pair in range(HEADS // 2):
        lanes = slice(pair * LANES, (pair + 1) * LANES)
        d_pair = dcat_ref[0, :, lanes]
        q_pair = q_ref[0, :, lanes]
        v_pair = v_ref[0, :, lanes]
        dk = jnp.zeros((length, LANES), F32)
        dv = jnp.zeros((length, LANES), F32)
        for head in (2 * pair, 2 * pair + 1):
            span = slice(head * HEAD_SIZE, (head + 1) * HEAD_SIZE)
            keep = low_lane if head % 2 == 0 else jnp.logical_not(low_lane)
            d_own = datt_ref[0, span, :].astype(F32)
            delta = rowsum(d_own * att_t_ref[0, span, :].astype(F32))
            dp = mm(v_pair, head_pair_rows(datt_ref[0], head))
            probs = probs_ref[0, head]
            dscores = (probs.astype(F32) * (dp - delta)).astype(BF)
            dqt_s[span, :] = mm(kt_s[span, :], dscores)
            dv = dv + mm(probs, jnp.where(keep, d_pair, jnp.zeros_like(d_pair)))
            dk = dk + mm(dscores, jnp.where(keep, q_pair, jnp.zeros_like(q_pair)))
        dk_s[:, lanes] = dk.astype(BF)
        dv_s[:, lanes] = dv.astype(BF)
    dq = dqt_s[...].T.astype(BF).astype(F32) + dqc_ref[0].astype(F32)
    small_ref[0:1, 0:width] += rowsum(dq)
    small_ref[0:1, width : 2 * width] += rowsum(dv_s[...].astype(F32))
    dq = dq.astype(BF)
    x_t = x_ref[0].T
    acc_s[0] += mm(x_t, dq)
    acc_s[1] += mm(x_t, dk_s[...])
    acc_s[2] += mm(x_t, dv_s[...])
    total_s[...] = (
        part_ref[0]
        + mm_nt(dq, wq_ref[...])
        + mm_nt(dk_s[...], wk_ref[...])
        + mm_nt(dv_s[...], wv_ref[...])
    )
    half = length // 2
    mine = pl.multiple_of(place[1] * half, half)
    other = pl.multiple_of((1 - place[1]) * half, half)
    own_ref[0] = total_s[pl.ds(mine, half), :]
    send_ref[0] = total_s[pl.ds(other, half), :].astype(BF)

    @pl.when(step == pl.num_programs(0) - 1)
    def _():
        grad_ref[...] = acc_s[...].astype(BF)


def att_back(place, hidden, dcat, datt, part, dqc, kept, weights, rows):
    length, features = hidden.shape[1:]
    width = HEADS * HEAD_SIZE
    half = length // 2

    def by_row(array):
        zeros = (0,) * (array.ndim - 1)
        return pl.BlockSpec((1,) + array.shape[1:], lambda r, p: (r,) + zeros)

    outs = [
        (
            jax.ShapeDtypeStruct((rows, half, features), F32),
            pl.BlockSpec((1, half, features), lambda r, p: (r, 0, 0)),
        ),
        (
            jax.ShapeDtypeStruct((rows, half, features), BF),
            pl.BlockSpec((1, half, features), lambda r, p: (r, 0, 0)),
        ),
        (
            jax.ShapeDtypeStruct((3, features, width), BF),
            pl.BlockSpec((3, features, width), lambda r, p: (0, 0, 0)),
        ),
        (
            jax.ShapeDtypeStruct((SLAB, features), F32),
            pl.BlockSpec((SLAB, features), lambda r, p: (0, 0)),
        ),
    ]
    return pl.pallas_call(
        att_back_kernel,
        out_shape=[o[0] for o in outs],
        grid_spec=pltpu.PrefetchScalarGridSpec(
            num_scalar_prefetch=1,
            grid=(rows,),
            in_specs=[
                pl.BlockSpec((1, length, features), lambda r, p: (p[0] + r, 0, 0)),
                pl.BlockSpec((1, length, width), lambda r, p: (r, 0, 0)),
                by_row(datt),
                by_row(part),
                by_row(dqc),
                *[by_row(a) for a in kept],
                *[whole(w) for w in weights],
            ],
            out_specs=[o[1] for o in outs],
            scratch_shapes=[
                pltpu.VMEM((width, length), BF),
                pltpu.VMEM((width, length), F32),
                pltpu.VMEM((length, width), BF),
                pltpu.VMEM((length, width), BF),
                pltpu.VMEM((length, features), F32),
                pltpu.VMEM((3, features, width), F32),
            ],
        ),
        compiler_params=pltpu.CompilerParams(vmem_limit_bytes=VMEM_LIMIT),
        name="attention_backward",
    )(place, hidden, dcat, datt, part, dqc, *kept, *weights)


def shards(
    hidden,
    bounds,
    query_weight,
    query_bias,
    branch_keys,
    branch_values,
    branch_bias,
    depth_kernel,
    point_bias,
    kernel_weight,
    kernel_bias,
    mixer_weight,
    mixer_bias,
    first_gain,
    first_shift,
    inner_weight,
    inner_bias,
    outer_weight,
    outer_bias,
    second_gain,
    second_shift,
    cotangent,
):
    side = lax.axis_index("branch")
    both = ("branch", "dp")
    rows = hidden.shape[0] // 2
    half = cotangent.shape[1]
    features = hidden.shape[2]
    width = query_weight.shape[1]
    groups, _, inner = inner_weight.shape
    swap = [(0, 1), (1, 0)]

    def exchange(value):
        return lax.ppermute(value, "branch", swap)

    base = (side * rows).astype(jnp.int32)
    far = ((1 - side) * rows).astype(jnp.int32)
    own_weights = (branch_keys[0], branch_values[0], branch_bias)
    got_weights = tuple(exchange(w) for w in own_weights)
    cot_got = exchange(lax.dynamic_slice_in_dim(cotangent, far, rows, 0))

    def line(vector):
        return vector.reshape(1, -1)

    def by_tap(matrix):
        tapped = matrix.reshape(matrix.shape[0], HEADS, KERNEL).transpose(2, 1, 0)
        tapped = jnp.pad(tapped, ((0, 0), (0, SLAB - HEADS), (0, 0)))
        return tapped.reshape(KERNEL * SLAB, -1)

    kwt = jnp.pad(by_tap(kernel_weight), ((0, LANES - KERNEL * SLAB), (0, 0)))
    kb = jnp.pad(by_tap(kernel_bias[None, :]), ((0, LANES - KERNEL * SLAB), (0, LANES - 1)))
    spread = spread_table()
    common = (depth_kernel, line(point_bias), kwt, kb, spread)

    def run(order, weights, before):
        is_att = jnp.where(side == order, 1, 0).astype(jnp.int32)
        place = jnp.stack([base, is_att])
        return forward(
            place,
            bounds,
            hidden,
            (query_weight, line(query_bias), *weights, *common),
            rows,
            before,
        )

    kept = run(0, own_weights, None)
    kept = run(1, got_weights, kept)
    cat, q, k, v, probs, att_t, dm, kc, cq, joint, taps, vc = kept
    spot = jnp.stack([base, side.astype(jnp.int32)])
    out_own, out_send, dcat, datt, dmix, grad_mid, vec_mid = middle(
        spot,
        hidden,
        cat,
        cotangent,
        cot_got,
        (
            mixer_weight,
            line(mixer_bias),
            line(first_gain),
            line(first_shift),
            inner_weight,
            line(inner_bias),
            outer_weight,
            line(outer_bias),
            line(second_gain),
            line(second_shift),
        ),
        rows,
    )
    out_got = exchange(out_send)
    attend = tuple(jnp.where(side == 0, o, g) for o, g in zip(own_weights, got_weights))
    convolve = tuple(jnp.where(side == 0, g, o) for o, g in zip(own_weights, got_weights))
    part, dqc, grad_conv, small_conv, kgrad = conv_back(
        spot,
        hidden,
        dcat,
        dmix,
        (dm, kc, cq, joint, taps, vc),
        (convolve[0], convolve[1], depth_kernel, kwt, spread, gather_table()),
        rows,
    )
    hid_own, hid_send, grad_att, small_att = att_back(
        spot,
        hidden,
        dcat,
        datt,
        part,
        dqc,
        (q, k, v, probs, att_t),
        (query_weight, attend[0], attend[1]),
        rows,
    )
    hid_got = exchange(hid_send).astype(F32)

    def join(own, got):
        return jnp.where(
            side == 0, jnp.concatenate([own, got], 0), jnp.concatenate([got, own], 0)
        )

    output = join(out_own, out_got)
    hidden_grad = join(hid_own, hid_got)
    grad_mid = lax.psum(grad_mid, both).astype(F32)
    grad_conv, grad_att = lax.psum((grad_conv, grad_att), both)
    vec_mid, small_conv, kgrad, small_att = lax.psum(
        (vec_mid, small_conv, kgrad, small_att), both
    )
    rows_i = groups * width
    grad_inner = grad_mid[:rows_i].reshape(groups, width, inner)
    grad_outer = grad_mid[rows_i : 2 * rows_i].reshape(groups, width, inner).transpose(0, 2, 1)
    grad_mixer = jnp.concatenate(
        [grad_mid[2 * rows_i :, :features], grad_mid[2 * rows_i :, features:]], 0
    )
    keys = jnp.where(side == 0, grad_att[1], grad_conv[0]).astype(F32)[None]
    values = jnp.where(side == 0, grad_att[2], grad_conv[1]).astype(F32)[None]
    value_bias = jnp.where(side == 0, small_att[0, width : 2 * width], small_conv[9, width : 2 * width])[None]
    kernel_grads = kgrad[: KERNEL * SLAB].reshape(KERNEL, SLAB, -1)[:, :HEADS].transpose(1, 0, 2)
    kernel_grads = kernel_grads.reshape(HEADS * KERNEL, -1)
    return (
        output,
        hidden_grad,
        grad_att[0].astype(F32),
        small_att[0, :width],
        keys,
        values,
        value_bias,
        small_conv[:KERNEL],
        small_conv[9, :width],
        kernel_grads[:, :width].T,
        kernel_grads[:, width],
        grad_mixer,
        vec_mid[1, :features],
        vec_mid[1, features : 2 * features],
        vec_mid[1, 2 * features : 3 * features],
        grad_inner,
        vec_mid[0],
        grad_outer,
        vec_mid[1, 3 * features : 4 * features],
        vec_mid[2, :features],
        vec_mid[2, features : 2 * features],
    )


def solution(mesh):
    split = P("dp", "branch", None)
    owned = P("branch", None, None)
    return jax.shard_map(
        shards,
        mesh=mesh,
        in_specs=(
            P("dp", None, None),
            P("dp", None),
            P(),
            P(),
            owned,
            owned,
            P("branch", None),
            *([P()] * 14),
            split,
        ),
        out_specs=(
            split,
            split,
            P(),
            P(),
            owned,
            owned,
            P("branch", None),
            *([P()] * 14),
        ),
        check_vma=False,
    )
```

```python
import functools

import jax
import jax.numpy as jnp
import numpy as np
from jax import lax
from jax.experimental import pallas as pl
from jax.experimental.pallas import tpu as pltpu
from jax.sharding import PartitionSpec as P

HEADS = 6
HEAD_SIZE = 64
KERNEL = 9
RADIUS = KERNEL // 2
SLAB = 8
LANES = 128
PAD = 8

NEGATIVE = -1000000000.0
EPSILON = 1e-05
INV_ROOT_TAU = 0.3989422804014327
ROOT_HALF = 0.7071067811865476
MID_BLOCKS = 64
TAIL_BLOCKS = 32
ORDER_BIT = 16
BASE, SIDE, CORE, MASK_A, MASK_B, MASK_T = range(6)

BF = jnp.bfloat16
F32 = jnp.float32
VMEM_LIMIT = 62 * 1024 * 1024


def mm(left, right):
    return jnp.dot(left, right, preferred_element_type=F32)


def mm_nt(left, right):
    return lax.dot_general(left, right, (((1,), (1,)), ((), ())), preferred_element_type=F32)


def block_rows(rows, blocks):
    return -(-rows // (16 * blocks)) * 16


def mid_slot(block, place):
    return block ^ (place[MASK_B] if block & ORDER_BIT else place[MASK_A])


def tail_block(width):
    return 4 * width // TAIL_BLOCKS + tail_shared(width)


def tail_shared(width):
    return -(-(width + LANES) // (16 * TAIL_BLOCKS)) * 16


def tail_rows(width, features):
    owned = 4 * width // TAIL_BLOCKS
    shared = tail_shared(width)
    spots = []
    for block in range(TAIL_BLOCKS):
        branch = block >> 2 & 1
        within = (block >> 3) * 4 + (block & 3)
        start = within * owned
        spots.append((1 + 2 * branch + start // width, start % width, block, 0, owned))
        spots.append((0, block * shared, block, owned, shared))
    return spots


def tail_slot(block, place):
    return block ^ place[MASK_T]


def send_halves(buffer, keep, away, sems):
    half = keep.shape[0]
    copies = [
        pltpu.make_async_copy(buffer.at[half : 2 * half], away, sems.at[1]),
        pltpu.make_async_copy(buffer.at[0:half], keep, sems.at[0]),
    ]
    for copy in copies:
        copy.start()
    for copy in copies:
        copy.wait()


def pick_weights(place, branch, weights):
    own_keys, own_values, first, second = (w[...] for w in weights)
    mine, even = place[SIDE] == branch, place[CORE] == 0
    return (
        jnp.where(mine, own_keys, jnp.where(even, first, second)),
        jnp.where(mine, own_values, jnp.where(even, second, first)),
    )


def rowsum(value):
    return jnp.sum(value, axis=0, keepdims=True)


def fill_strips(strips_ref, value, length):
    strips = strips_ref.shape[0]
    zero = jnp.zeros((PAD, LANES), F32)
    for strip in range(strips):
        strips_ref[strip, 0:PAD, :] = zero
        strips_ref[strip, PAD + length : 2 * PAD + length, :] = zero
        strips_ref[strip, PAD : PAD + length, :] = value[
            :, strip * LANES : (strip + 1) * LANES
        ].astype(F32)


def head_pair_rows(rows, head):
    own = rows[head * HEAD_SIZE : (head + 1) * HEAD_SIZE, :]
    zero = jnp.zeros_like(own)
    return jnp.concatenate([own, zero] if head % 2 == 0 else [zero, own], axis=0)


def line(ref):
    return ref[...].reshape(1, -1)


def tapped_weights(order_ref, kw_ref):
    return mm(order_ref[...], kw_ref[...]).astype(BF)


def forward_kernel(
    order,
    place,
    bounds,
    x_ref,
    wq_ref,
    wa_ref,
    wb_ref,
    bb_ref,
    depth_ref,
    qb_ref,
    pb_ref,
    kb_ref,
    kw_ref,
    order_ref,
    spread_ref,
    *rest,
):
    (
        cat_ref,
        q_ref,
        k_ref,
        v_ref,
        probs_ref,
        att_t_ref,
        dm_ref,
        kc_ref,
        cq_ref,
        joint_ref,
        taps_ref,
        vc_ref,
        qt_s,
        vt_s,
        xs_s,
        vs_s,
        tw_s,
        wide_s,
    ) = rest[-18:]
    row = place[BASE] + pl.program_id(0)
    width = HEADS * HEAD_SIZE
    wa, wb = wa_ref[...], wb_ref[...]
    if order:
        even = place[CORE] == 0
        wa, wb = jnp.where(even, wa, wb), jnp.where(even, wb, wa)
    first_end = bounds[0, row]
    valid = bounds[1, row]
    length = x_ref.shape[1]
    x = x_ref[0]
    queries = (mm(x, wq_ref[...]) + line(qb_ref)).astype(BF)

    @pl.when(place[SIDE] == order)
    def _():
        scaled = (queries.astype(F32) * (HEAD_SIZE**-0.5)).astype(BF)
        q_ref[0] = scaled
        qt_s[...] = scaled.T
        k_ref[0] = mm(x, wa).astype(BF)
        v = (mm(x, wb) + bb_ref[...]).astype(BF)
        v_ref[0] = v
        vt_s[...] = v.T
        seen = lax.broadcasted_iota(jnp.int32, (length, 1), 0) < valid
        for head in range(HEADS):
            pair = head // 2
            keys = k_ref[0, :, pair * LANES : (pair + 1) * LANES]
            scores = mm(keys, head_pair_rows(qt_s, head))
            scores = jnp.where(seen, scores, NEGATIVE)
            raised = jnp.exp(scores - jnp.max(scores, axis=0, keepdims=True))
            probs = (raised * (1.0 / rowsum(raised))).astype(BF)
            probs_ref[0, head] = probs
            span = slice(head * HEAD_SIZE, (head + 1) * HEAD_SIZE)
            att_t_ref[0, span, :] = mm(vt_s[span, :], probs).astype(BF)
        cat_ref[0] = att_t_ref[0].T

    @pl.when(place[SIDE] != order)
    def _():
        fill_strips(xs_s, x, length)
        piece = LANES
        for strip in range(xs_s.shape[0]):
            lanes = slice(strip * LANES, (strip + 1) * LANES)
            for at in range(0, length, piece):
                total = None
                for tap in range(KERNEL):
                    begin = PAD - RADIUS + tap + at
                    term = xs_s[strip, begin : begin + piece, :] * depth_ref[tap : tap + 1, lanes]
                    total = term if total is None else total + term
                dm_ref[0, at : at + piece, lanes] = total.astype(BF)
        key_conv = mm(dm_ref[0], wa) + line(pb_ref)
        kc_ref[0] = key_conv
        cq_ref[0] = queries
        joint = (key_conv * queries.astype(F32)).astype(BF)
        joint_ref[0] = joint
        tap_bias = jnp.sum(order_ref[...].astype(F32) * line(kb_ref), axis=1, keepdims=True)
        logits = mm_nt(tapped_weights(order_ref, kw_ref), joint) + tap_bias
        here = lax.broadcasted_iota(jnp.int32, (SLAB, length), 1)

        def segment(position):
            return jnp.where(position <= first_end, 0, jnp.where(position < valid, 1, 2))

        own_segment = segment(here)
        slabs = []
        for tap in range(KERNEL):
            other = here + (tap - RADIUS)
            same = (other >= 0) & (other < length) & (segment(other) == own_segment)
            slabs.append(jnp.where(same, logits[tap * SLAB : (tap + 1) * SLAB], NEGATIVE))
        peak = functools.reduce(jnp.maximum, slabs)
        slabs = [jnp.exp(slab - peak) for slab in slabs]
        inverse = 1.0 / functools.reduce(jnp.add, slabs)
        for tap in range(KERNEL):
            tw_s[tap * SLAB : (tap + 1) * SLAB, :] = slabs[tap] * inverse
        tw_s[KERNEL * SLAB :, :] = jnp.zeros((LANES - KERNEL * SLAB, length), F32)
        taps_ref[0] = tw_s[...]
        taps = tw_s[...].T
        high = taps.astype(BF)
        low = (taps - high.astype(F32)).astype(BF)
        both = jnp.concatenate([high, low], axis=1)
        for tap in range(KERNEL):
            cols = slice(tap * width, (tap + 1) * width)
            wide_s[:, cols] = mm(both, spread_ref[:, cols])
        vc = (mm(x, wb) + bb_ref[...]).astype(BF)
        vc_ref[0] = vc
        fill_strips(vs_s, vc, length)
        for strip in range(vs_s.shape[0]):
            for at in range(0, length, piece):
                total = None
                for tap in range(KERNEL):
                    begin = PAD - RADIUS + tap + at
                    col = tap * width + strip * LANES
                    term = (
                        vs_s[strip, begin : begin + piece, :]
                        * wide_s[at : at + piece, col : col + LANES]
                    )
                    total = term if total is None else total + term
                cat_ref[0, at : at + piece, strip * LANES : (strip + 1) * LANES] = total.astype(BF)


def spread_table():
    table = np.zeros((2 * LANES, KERNEL, HEADS, HEAD_SIZE), np.float32)
    for tap in range(KERNEL):
        for head in range(HEADS):
            table[tap * SLAB + head, tap, head, :] = 1
            table[LANES + tap * SLAB + head, tap, head, :] = 1
    return jnp.asarray(table.reshape(2 * LANES, -1), BF)


def gather_table():
    table = np.zeros((KERNEL, HEADS, HEAD_SIZE, LANES), np.float32)
    for tap in range(KERNEL):
        for head in range(HEADS):
            table[tap, head, :, tap * SLAB + head] = 1
    return jnp.asarray(table.reshape(-1, LANES), BF)


def order_table():
    table = np.zeros((LANES, HEADS * KERNEL), np.float32)
    for tap in range(KERNEL):
        for head in range(HEADS):
            table[tap * SLAB + head, head * KERNEL + tap] = 1
    return jnp.asarray(table, BF)


def whole(array, buffers=2):
    rank = len(array.shape)
    mode = pl.Buffered(buffers) if buffers < 2 else None
    return pl.BlockSpec(array.shape, lambda *_: (0,) * rank, pipeline_mode=mode)


def forward(order, place, bounds, hidden, weights, rows, before=None):
    length, features = hidden.shape[1:]
    width = HEADS * HEAD_SIZE
    spare = rows

    def att_row(r, place, bounds):
        return jnp.where(place[SIDE] == order, r, spare)

    def conv_row(r, place, bounds):
        return jnp.where(place[SIDE] != order, r, spare)

    def saved(row_of, shape, dtype):
        zeros = (0,) * len(shape)
        return (
            jax.ShapeDtypeStruct((rows + 1,) + shape, dtype),
            pl.BlockSpec((1,) + shape, lambda r, p, b: (row_of(r, p, b),) + zeros),
        )

    outs = [
        (
            jax.ShapeDtypeStruct((rows, length, 2 * width), BF),
            pl.BlockSpec((1, length, width), lambda r, p, b: (r, 0, jnp.where(p[SIDE] == order, 0, 1))),
        ),
        saved(att_row, (length, width), BF),
        saved(att_row, (length, width), BF),
        saved(att_row, (length, width), BF),
        saved(att_row, (HEADS, length, length), BF),
        saved(att_row, (width, length), BF),
        saved(conv_row, (length, features), BF),
        saved(conv_row, (length, width), F32),
        saved(conv_row, (length, width), BF),
        saved(conv_row, (length, width), BF),
        saved(conv_row, (LANES, length), F32),
        saved(conv_row, (length, width), BF),
    ]
    in_specs = [pl.BlockSpec((1, length, features), lambda r, p, b: (p[0] + r, 0, 0))]
    in_specs += [whole(w) for w in weights]
    args = [place, bounds, hidden, *weights]
    aliases = {}
    if before is not None:
        aliases = {len(args) + i: i for i in range(len(before))}
        in_specs += [pl.BlockSpec(memory_space=pl.ANY)] * len(before)
        args += list(before)
    return pl.pallas_call(
        functools.partial(forward_kernel, order),
        out_shape=[o[0] for o in outs],
        grid_spec=pltpu.PrefetchScalarGridSpec(
            num_scalar_prefetch=2,
            grid=(rows,),
            in_specs=in_specs,
            out_specs=[o[1] for o in outs],
            scratch_shapes=[
                pltpu.VMEM((width, length), BF),
                pltpu.VMEM((width, length), BF),
                pltpu.VMEM((features // LANES, length + 2 * PAD, LANES), F32),
                pltpu.VMEM((width // LANES, length + 2 * PAD, LANES), F32),
                pltpu.VMEM((LANES, length), F32),
                pltpu.VMEM((length, KERNEL * width), F32),
            ],
        ),
        input_output_aliases=aliases,
        compiler_params=pltpu.CompilerParams(vmem_limit_bytes=VMEM_LIMIT),
        cost_estimate=pl.CostEstimate(flops=10**10, bytes_accessed=2 * 10**7, transcendentals=0),
        name="branch_forward",
    )(*args)


def norm(value):
    center = value - jnp.mean(value, axis=-1, keepdims=True)
    factor = lax.rsqrt(jnp.mean(center * center, axis=-1, keepdims=True) + EPSILON)
    return center * factor, factor


def norm_back(gradient, normed, factor):
    return factor * (
        gradient
        - jnp.mean(gradient, axis=-1, keepdims=True)
        - normed * jnp.mean(gradient * normed, axis=-1, keepdims=True)
    )


def middle_kernel(
    place,
    x_ref,
    cat_ref,
    cot_own_ref,
    cot_got_ref,
    mw_ref,
    iw_ref,
    ow_ref,
    mixer_bias,
    gain1,
    shift1,
    inner_bias,
    outer_bias,
    gain2,
    shift2,
    own_ref,
    send_ref,
    dcat_ref,
    datt_ref,
    dmix_ref,
    keep_ref,
    away_ref,
    grad_ref,
    sems,
    vec_s,
    rest_s,
    acc_i,
    acc_o,
    acc_m,
    act_s,
    slope_s,
    din_s,
):
    step = pl.program_id(0)
    first_side = place[SIDE] == 0
    features = x_ref.shape[2]
    half = x_ref.shape[1] // 2
    groups, width, inner = iw_ref.shape
    piece = 512

    mixer_bias, gain1, shift1, inner_bias, outer_bias, gain2, shift2 = (
        line(r) for r in (mixer_bias, gain1, shift1, inner_bias, outer_bias, gain2, shift2)
    )

    @pl.when(step == 0)
    def _():
        acc_i[...] = jnp.zeros_like(acc_i)
        acc_o[...] = jnp.zeros_like(acc_o)
        acc_m[...] = jnp.zeros_like(acc_m)
        vec_s[...] = jnp.zeros_like(vec_s)

    cat = cat_ref[0]
    normed1, factor1 = norm(x_ref[0].astype(F32) + (mm(cat, mw_ref[...]) + mixer_bias))
    first = (normed1 * gain1 + shift1).astype(BF)
    projected = []
    for g in range(groups):
        part = first[:, g * width : (g + 1) * width]
        for at in range(0, inner, piece):
            lanes = slice(g * inner + at, g * inner + at + piece)
            pre = mm(part, iw_ref[g, :, at : at + piece]) + inner_bias[:, lanes]
            phi = 0.5 + 0.5 * lax.erf(pre * ROOT_HALF)
            bell = jnp.exp(-0.5 * pre * pre) * INV_ROOT_TAU
            act_s[:, lanes] = (pre * phi).astype(BF)
            slope_s[:, lanes] = phi + pre * bell
        projected.append(mm(act_s[:, g * inner : (g + 1) * inner], ow_ref[g]))
    projected = jnp.concatenate(projected, axis=1)
    normed2, factor2 = norm(first.astype(F32) + (projected + outer_bias))
    output = normed2 * gain2 + shift2
    own_ref[0] = jnp.where(first_side, output[:half], output[half:]).astype(BF)
    send_ref[0] = jnp.where(first_side, output[half:], output[:half]).astype(BF)
    cot_own, cot_got = cot_own_ref[0].astype(F32), cot_got_ref[0].astype(F32)
    cot = jnp.concatenate(
        [jnp.where(first_side, cot_own, cot_got), jnp.where(first_side, cot_got, cot_own)], axis=0
    )
    dsecond = norm_back(cot * gain2, normed2, factor2)
    dproj = dsecond.astype(BF)
    vec_s[1:2, 3 * features : 4 * features] += rowsum(dproj.astype(F32))
    vec_s[2:3, 0:features] += rowsum(cot * normed2)
    vec_s[2:3, features : 2 * features] += rowsum(cot)
    dfirst = []
    for g in range(groups):
        cols = slice(g * width, (g + 1) * width)
        dpart = dproj[:, cols]
        for at in range(0, inner, piece):
            lanes = slice(g * inner + at, g * inner + at + piece)
            dact = mm_nt(dpart, ow_ref[g, at : at + piece, :]).astype(BF)
            din = (dact.astype(F32) * slope_s[:, lanes]).astype(BF)
            din_s[:, lanes] = din
            vec_s[0:1, lanes] += rowsum(din.astype(F32))
        group = slice(g * inner, (g + 1) * inner)
        acc_o[g] += mm(dpart.T, act_s[:, group])
        acc_i[g] += mm(first[:, cols].T, din_s[:, group])
        dfirst.append(dsecond[:, cols] + mm_nt(din_s[:, group], iw_ref[g]))
    dfirst = jnp.concatenate(dfirst, axis=1)
    vec_s[1:2, features : 2 * features] += rowsum(dfirst * normed1)
    vec_s[1:2, 2 * features : 3 * features] += rowsum(dfirst)
    dmixed = norm_back(dfirst * gain1, normed1, factor1)
    dmix_ref[0] = dmixed
    dmixer = dmixed.astype(BF)
    vec_s[1:2, 0:features] += rowsum(dmixer.astype(F32))
    acc_m[...] += mm(cat.T, dmixer)
    dcat_ref[0] = mm_nt(dmixer, mw_ref[...]).astype(BF)
    datt_ref[0] = mm_nt(mw_ref[0:width, :], dmixer).astype(BF)

    @pl.when(step == pl.num_programs(0) - 1)
    def _():
        rest_s[0:1, :] = vec_s[0:1, 0:inner]
        rest_s[1:2, :] = vec_s[0:1, inner:]
        rest_s[2:3, :] = vec_s[1:2, 0:inner]
        rest_s[3:4, :] = vec_s[1:2, inner:]
        rest_s[4:5, :] = vec_s[2:3, 0:inner]
        rest_s[5:, :] = jnp.zeros((rest_s.shape[0] - 5, inner), F32)
        block = grad_ref.shape[1]
        sources = [acc_i.at[0], acc_i.at[1], acc_o.at[0], acc_o.at[1]]
        for part in range(MID_BLOCKS):
            start = part * block
            slot = mid_slot(part, place)
            if start < 2 * groups * width:
                source = sources[start // width]
                start = start % width
                grad_ref[slot] = source[start : start + block, :].astype(BF)
            elif start < 5 * width:
                start = start - 2 * groups * width
                grad_ref[slot, :, 0:features] = acc_m[start : start + block, :].astype(BF)
                start = start + width
                grad_ref[slot, :, features:] = acc_m[start : start + block, :].astype(BF)
            else:
                start = start - 5 * width
                grad_ref[slot] = rest_s[start : start + block, :].astype(BF)
        send_halves(grad_ref, keep_ref, away_ref, sems)


def middle(place, hidden, cat, cot_own, cot_got, weights, rows):
    length, features = hidden.shape[1:]
    half = length // 2
    groups, width, inner = weights[1].shape
    block = block_rows(5 * width, MID_BLOCKS)
    sent = jax.ShapeDtypeStruct((MID_BLOCKS // 2, block, inner), BF)

    def per_row(*shape, dtype=BF):
        return (
            jax.ShapeDtypeStruct((rows,) + shape, dtype),
            pl.BlockSpec((1,) + shape, lambda s, p: (s, 0, 0)),
        )

    outs = [
        per_row(half, features),
        per_row(half, features),
        per_row(length, features),
        per_row(width, length),
        per_row(length, features, dtype=F32),
        (sent, pl.BlockSpec(memory_space=pl.ANY)),
        (sent, pl.BlockSpec(memory_space=pl.ANY)),
    ]
    return pl.pallas_call(
        middle_kernel,
        out_shape=[o[0] for o in outs],
        grid_spec=pltpu.PrefetchScalarGridSpec(
            num_scalar_prefetch=1,
            grid=(rows,),
            in_specs=[
                pl.BlockSpec((1, length, features), lambda s, p: (p[0] + s, 0, 0)),
                pl.BlockSpec((1, length, features), lambda s, p: (s, 0, 0)),
                pl.BlockSpec((1, half, features), lambda s, p: (p[0] + s, 0, 0)),
                pl.BlockSpec((1, half, features), lambda s, p: (s, 0, 0)),
                *[whole(w, 1) for w in weights],
            ],
            out_specs=[o[1] for o in outs],
            scratch_shapes=[
                pltpu.VMEM((MID_BLOCKS, block, inner), BF),
                pltpu.SemaphoreType.DMA((2,)),
                pltpu.VMEM((SLAB, groups * inner), F32),
                pltpu.VMEM((MID_BLOCKS * block - 5 * width, inner), F32),
                pltpu.VMEM((groups, width, inner), F32),
                pltpu.VMEM((groups, width, inner), F32),
                pltpu.VMEM((features, features), F32),
                pltpu.VMEM((length, groups * inner), BF),
                pltpu.VMEM((length, groups * inner), F32),
                pltpu.VMEM((length, groups * inner), BF),
            ],
        ),
        compiler_params=pltpu.CompilerParams(vmem_limit_bytes=VMEM_LIMIT),
        cost_estimate=pl.CostEstimate(flops=10**10, bytes_accessed=2 * 10**7, transcendentals=0),
        name="shared_layers",
    )(place, hidden, cat, cot_own, cot_got, *weights)


def conv_back_kernel(
    waits,
    place,
    x_ref,
    dcat_ref,
    dmix_ref,
    dm_ref,
    kc_ref,
    q_ref,
    joint_ref,
    taps_ref,
    vc_ref,
    own_a_ref,
    own_b_ref,
    got_a_ref,
    got_b_ref,
    depth_ref,
    kw_ref,
    order_ref,
    spread_ref,
    collect_ref,
    *rest,
):
    rest = rest[waits:]
    part_ref, dq_ref, acc_a, acc_b, small_ref, kgrad_ref = rest[-11:-5]
    vs_s, xs_s, ys_s, ds_s, prod_s = rest[-5:]
    length, features = x_ref.shape[1:]
    width = HEADS * HEAD_SIZE
    piece = LANES

    for index, ref in enumerate((acc_a, acc_b, small_ref, kgrad_ref)):
        ref[...] = jnp.zeros_like(ref) if len(rest) == 11 else rest[index][...]
    wa, wb = pick_weights(place, 1, (own_a_ref, own_b_ref, got_a_ref, got_b_ref))
    x = x_ref[0]
    dconv = dcat_ref[0].astype(F32)
    fill_strips(vs_s, vc_ref[0], length)
    taps_t = taps_ref[0]
    taps = taps_t.T
    high = taps.astype(BF)
    low = (taps - high.astype(F32)).astype(BF)
    both = jnp.concatenate([high, low], axis=1)
    zero = jnp.zeros((PAD, LANES), F32)
    for tap in range(KERNEL):
        spread = mm(both, spread_ref[:, tap * width : (tap + 1) * width])
        for strip in range(width // LANES):
            lanes = slice(strip * LANES, (strip + 1) * LANES)
            begin = PAD - RADIUS + tap
            prod_s[:, tap * width + strip * LANES : tap * width + (strip + 1) * LANES] = (
                dconv[:, lanes] * vs_s[strip, begin : begin + length, :]
            ).astype(BF)
            slot = tap * (width // LANES) + strip
            ys_s[slot, 0:PAD, :] = zero
            ys_s[slot, PAD + length :, :] = zero
            ys_s[slot, PAD : PAD + length, :] = spread[:, lanes] * dconv[:, lanes]
    dvc = []
    for strip in range(width // LANES):
        total = None
        for tap in range(KERNEL):
            begin = PAD + RADIUS - tap
            term = ys_s[tap * (width // LANES) + strip, begin : begin + length, :]
            total = term if total is None else total + term
        dvc.append(total.astype(BF))
    dvc = jnp.concatenate(dvc, axis=1)
    dtaps = mm(prod_s[...], collect_ref[...]).T
    slabs = [dtaps[t * SLAB : (t + 1) * SLAB] for t in range(KERNEL)]
    weights = [taps_t[t * SLAB : (t + 1) * SLAB] for t in range(KERNEL)]
    total = functools.reduce(jnp.add, [a * b for a, b in zip(slabs, weights)])
    slabs = [b * (a - total) for a, b in zip(slabs, weights)]
    slabs.append(jnp.zeros((LANES - KERNEL * SLAB, length), F32))
    dlogits_t = jnp.concatenate(slabs, axis=0)
    dlogits = dlogits_t.T.astype(BF)
    rounded_t = dlogits_t.astype(BF)
    kgrad_ref[:, 0:width] += mm(rounded_t, joint_ref[0])
    kgrad_ref[:, width : width + LANES] += jnp.broadcast_to(
        jnp.sum(rounded_t.astype(F32), axis=1, keepdims=True), (LANES, LANES)
    )
    djoint = mm(dlogits, tapped_weights(order_ref, kw_ref)).astype(BF).astype(F32)
    dkey = (djoint * q_ref[0].astype(F32)).astype(BF)
    dq_ref[0] = (djoint * kc_ref[0]).astype(BF)
    small_ref[9:10, 0:width] += rowsum(dkey.astype(F32))
    small_ref[9:10, width : 2 * width] += rowsum(dvc.astype(F32))
    ddepth = mm_nt(dkey, wa).astype(BF)
    acc_a[...] += mm(dm_ref[0].T, dkey)
    acc_b[...] += mm(x.T, dvc)
    part_ref[0] = dmix_ref[0] + mm_nt(dvc, wb)
    fill_strips(ds_s, ddepth, length)
    fill_strips(xs_s, x, length)
    for strip in range(features // LANES):
        lanes = slice(strip * LANES, (strip + 1) * LANES)
        sums = [None] * KERNEL
        for at in range(0, length, piece):
            total = part_ref[0, at : at + piece, lanes]
            center = ds_s[strip, PAD + at : PAD + at + piece, :]
            for tap in range(KERNEL):
                begin = PAD + RADIUS - tap + at
                total = total + ds_s[strip, begin : begin + piece, :] * depth_ref[tap : tap + 1, lanes]
                begin = PAD - RADIUS + tap + at
                term = (xs_s[strip, begin : begin + piece, :] * center).reshape(-1, SLAB, LANES)
                term = jnp.sum(term, axis=0)
                sums[tap] = term if sums[tap] is None else sums[tap] + term
            part_ref[0, at : at + piece, lanes] = total
        for tap in range(KERNEL):
            small_ref[tap : tap + 1, lanes] += rowsum(sums[tap])


def conv_back(place, row, hidden, dcat, dmix, kept, weights, before, waits):
    length, features = hidden.shape[1:]
    width = HEADS * HEAD_SIZE

    def by_row(array):
        zeros = (0,) * (array.ndim - 1)
        return pl.BlockSpec((1,) + array.shape[1:], lambda r, p: (row,) + zeros)

    outs = [
        jax.ShapeDtypeStruct((1, length, features), F32),
        jax.ShapeDtypeStruct((1, length, width), BF),
        jax.ShapeDtypeStruct((features, width), F32),
        jax.ShapeDtypeStruct((features, width), F32),
        jax.ShapeDtypeStruct((16, features), F32),
        jax.ShapeDtypeStruct((LANES, width + LANES), F32),
    ]
    strips = features // LANES
    return pl.pallas_call(
        functools.partial(conv_back_kernel, len(waits)),
        out_shape=outs,
        grid_spec=pltpu.PrefetchScalarGridSpec(
            num_scalar_prefetch=1,
            grid=(1,),
            in_specs=[
                pl.BlockSpec((1, length, features), lambda r, p: (p[0] + row, 0, 0)),
                pl.BlockSpec((1, length, width), lambda r, p: (row, 0, 1)),
                by_row(dmix),
                *[by_row(a) for a in kept],
                *[whole(w) for w in weights],
                *[pl.BlockSpec(memory_space=pl.ANY)] * len(waits),
                *[whole(a) for a in before],
            ],
            out_specs=[whole(o) for o in outs],
            scratch_shapes=[
                pltpu.VMEM((width // LANES, length + 2 * PAD, LANES), F32),
                pltpu.VMEM((strips, length + 2 * PAD, LANES), F32),
                pltpu.VMEM((KERNEL * width // LANES, length + 2 * PAD, LANES), F32),
                pltpu.VMEM((strips, length + 2 * PAD, LANES), F32),
                pltpu.VMEM((length, KERNEL * width), BF),
            ],
        ),
        compiler_params=pltpu.CompilerParams(vmem_limit_bytes=VMEM_LIMIT),
        cost_estimate=pl.CostEstimate(flops=10**10, bytes_accessed=2 * 10**7, transcendentals=0),
        name="convolution_backward",
    )(place, hidden, dcat, dmix, *kept, *weights, *waits, *before)


def att_back_kernel(
    waits,
    place,
    x_ref,
    dcat_ref,
    datt_ref,
    part_ref,
    dqc_ref,
    q_ref,
    k_ref,
    v_ref,
    probs_ref,
    att_t_ref,
    wq_ref,
    own_a_ref,
    own_b_ref,
    got_a_ref,
    got_b_ref,
    *rest,
):
    rest = rest[waits:]
    own_ref, send_ref, acc_s, small_ref, kt_s, dqt_s, dk_s, dv_s, total_s = rest[-9:]
    if len(rest) > 9:
        acc_s[...] = rest[0][...]
        small_ref[...] = rest[1][...]
    else:
        acc_s[...] = jnp.zeros_like(acc_s)
        small_ref[...] = jnp.zeros_like(small_ref)
    length, features = x_ref.shape[1:]
    width = HEADS * HEAD_SIZE

    wk, wv = pick_weights(place, 0, (own_a_ref, own_b_ref, got_a_ref, got_b_ref))
    scaled_keys = (k_ref[0].astype(F32) * (HEAD_SIZE**-0.5)).astype(BF)
    kt_s[...] = scaled_keys.T
    low_lane = lax.broadcasted_iota(jnp.int32, (1, LANES), 1) < HEAD_SIZE
    for pair in range(HEADS // 2):
        lanes = slice(pair * LANES, (pair + 1) * LANES)
        d_pair = dcat_ref[0, :, lanes]
        q_pair = q_ref[0, :, lanes]
        v_pair = v_ref[0, :, lanes]
        dk = jnp.zeros((length, LANES), F32)
        dv = jnp.zeros((length, LANES), F32)
        for head in (2 * pair, 2 * pair + 1):
            span = slice(head * HEAD_SIZE, (head + 1) * HEAD_SIZE)
            keep = low_lane if head % 2 == 0 else jnp.logical_not(low_lane)
            d_own = datt_ref[0, span, :].astype(F32)
            delta = rowsum(d_own * att_t_ref[0, span, :].astype(F32))
            dp = mm(v_pair, head_pair_rows(datt_ref[0], head))
            probs = probs_ref[0, head]
            dscores = (probs.astype(F32) * (dp - delta)).astype(BF)
            dqt_s[span, :] = mm(kt_s[span, :], dscores)
            dv = dv + mm(probs, jnp.where(keep, d_pair, jnp.zeros_like(d_pair)))
            dk = dk + mm(dscores, jnp.where(keep, q_pair, jnp.zeros_like(q_pair)))
        dk_s[:, lanes] = dk.astype(BF)
        dv_s[:, lanes] = dv.astype(BF)
    dq = dqt_s[...].T.astype(BF).astype(F32) + dqc_ref[0].astype(F32)
    small_ref[0:1, 0:width] += rowsum(dq)
    small_ref[0:1, width : 2 * width] += rowsum(dv_s[...].astype(F32))
    dq = dq.astype(BF)
    x_t = x_ref[0].T
    acc_s[0] += mm(x_t, dq)
    acc_s[1] += mm(x_t, dk_s[...])
    acc_s[2] += mm(x_t, dv_s[...])
    total_s[...] = (
        part_ref[0]
        + mm_nt(dq, wq_ref[...])
        + mm_nt(dk_s[...], wk)
        + mm_nt(dv_s[...], wv)
    )
    half = length // 2
    mine = pl.multiple_of(place[SIDE] * half, half)
    other = pl.multiple_of((1 - place[SIDE]) * half, half)
    own_ref[0] = total_s[pl.ds(mine, half), :]
    send_ref[0] = total_s[pl.ds(other, half), :].astype(BF)


def att_back(place, row, hidden, dcat, datt, part, dqc, kept, weights, before, waits):
    length, features = hidden.shape[1:]
    width = HEADS * HEAD_SIZE
    half = length // 2

    def by_row(array):
        zeros = (0,) * (array.ndim - 1)
        return pl.BlockSpec((1,) + array.shape[1:], lambda r, p: (row,) + zeros)

    outs = [
        jax.ShapeDtypeStruct((1, half, features), F32),
        jax.ShapeDtypeStruct((1, half, features), BF),
        jax.ShapeDtypeStruct((3, features, width), F32),
        jax.ShapeDtypeStruct((SLAB, features), F32),
    ]
    return pl.pallas_call(
        functools.partial(att_back_kernel, len(waits)),
        out_shape=outs,
        grid_spec=pltpu.PrefetchScalarGridSpec(
            num_scalar_prefetch=1,
            grid=(1,),
            in_specs=[
                pl.BlockSpec((1, length, features), lambda r, p: (p[0] + row, 0, 0)),
                pl.BlockSpec((1, length, width), lambda r, p: (row, 0, 0)),
                by_row(datt),
                whole(part),
                whole(dqc),
                *[by_row(a) for a in kept],
                *[whole(w) for w in weights],
                *[pl.BlockSpec(memory_space=pl.ANY)] * len(waits),
                *[whole(a) for a in before],
            ],
            out_specs=[whole(o) for o in outs],
            scratch_shapes=[
                pltpu.VMEM((width, length), BF),
                pltpu.VMEM((width, length), F32),
                pltpu.VMEM((length, width), BF),
                pltpu.VMEM((length, width), BF),
                pltpu.VMEM((length, features), F32),
            ],
        ),
        compiler_params=pltpu.CompilerParams(vmem_limit_bytes=VMEM_LIMIT),
        cost_estimate=pl.CostEstimate(flops=10**10, bytes_accessed=2 * 10**7, transcendentals=0),
        name="attention_backward",
    )(place, hidden, dcat, datt, part, dqc, *kept, *weights, *waits, *before)


def pack_kernel(place, acc_ref, small_ref, acc_a, acc_b, small_conv, kgrad, *rest):
    keep_ref, away_ref, rest_s, grad_ref, sems = rest[-5:]
    features, width = acc_a.shape
    taps = KERNEL * SLAB
    rest_s[...] = jnp.zeros_like(rest_s)
    rest_s[0:taps, 0 : width + LANES] = kgrad[0:taps, :]
    rest_s[taps : taps + 16, :] = small_conv[...]
    rest_s[taps + 16 : taps + 16 + SLAB, :] = small_ref[...]
    sources = [acc_ref.at[0], acc_ref.at[1], acc_ref.at[2], acc_a, acc_b]
    for source, start, block, at, size in tail_rows(width, features):
        slot = tail_slot(block, place)
        if start < width:
            left = sources[source][start : start + size, :]
            right = sources[source][width + start : width + start + size, :]
            grad_ref[slot, at : at + size, 0:width] = left.astype(BF)
            grad_ref[slot, at : at + size, width:] = right.astype(BF)
        else:
            start = start - width
            grad_ref[slot, at : at + size, :] = rest_s[start : start + size, :].astype(BF)
    send_halves(grad_ref, keep_ref, away_ref, sems)


def pack(place, sums, waits):
    features, width = sums[2].shape
    sent = jax.ShapeDtypeStruct((TAIL_BLOCKS // 2, tail_block(width), features), BF)
    anywhere = pl.BlockSpec(memory_space=pl.ANY)
    return pl.pallas_call(
        pack_kernel,
        out_shape=[sent, sent],
        grid_spec=pltpu.PrefetchScalarGridSpec(
            num_scalar_prefetch=1,
            grid=(1,),
            in_specs=[whole(a) for a in sums] + [anywhere] * len(waits),
            out_specs=[anywhere, anywhere],
            scratch_shapes=[
                pltpu.VMEM((TAIL_BLOCKS * tail_shared(width) - width, features), F32),
                pltpu.VMEM((TAIL_BLOCKS, tail_block(width), features), BF),
                pltpu.SemaphoreType.DMA((2,)),
            ],
        ),
        compiler_params=pltpu.CompilerParams(vmem_limit_bytes=VMEM_LIMIT),
        cost_estimate=pl.CostEstimate(flops=10**9, bytes_accessed=10**7, transcendentals=0),
        name="pack_gradients",
    )(place, *sums, *waits)


def merge(body, outs, ins, waits=(), steps=1):
    waited = len(waits)

    def kernel(*refs):
        body(refs[: len(ins)], refs[len(ins) + waited :])

    def spec(array):
        if steps == 1:
            return whole(array)
        axis = 1 if array.ndim == 4 else 0
        shape = list(array.shape)
        shape[axis] //= steps
        return pl.BlockSpec(
            tuple(shape), lambda i: tuple(i if d == axis else 0 for d in range(len(shape)))
        )

    outs = [jax.ShapeDtypeStruct(shape, BF) for shape in outs]
    return pl.pallas_call(
        kernel,
        out_shape=outs,
        grid=(steps,),
        in_specs=[spec(a) for a in ins] + [pl.BlockSpec(memory_space=pl.ANY)] * waited,
        out_specs=[spec(o) for o in outs],
        compiler_params=pltpu.CompilerParams(vmem_limit_bytes=VMEM_LIMIT),
        cost_estimate=pl.CostEstimate(flops=10**9, bytes_accessed=4 * 10**6, transcendentals=0),
        name="exchange_step",
    )(*ins, *waits)


def total(*values):
    result = values[0].astype(F32)
    for value in values[1:]:
        result = result + value.astype(F32)
    return result.astype(BF)


def sum_core(ins, outs):
    for part, out in enumerate(outs):
        out[...] = total(ins[0][part], ins[1][part])


def sum_first(ins, outs):
    keep_a, got_a, keep_b, got_b = ins
    half = outs[0].shape[0]
    for part in range(2):
        span = slice(part * half, (part + 1) * half)
        outs[part][...] = total(keep_a[span], got_a[span])
        outs[2 + part][...] = total(keep_b[span], got_b[span])


def sum_second(ins, outs):
    keep_a, got_a, keep_b, got_b = ins
    for part, out in enumerate(outs):
        out[0] = total(keep_a[part], got_a[part])
        out[1] = total(keep_b[part], got_b[part])


def sum_all(ins, outs):
    outs[0][...] = total(*[i[...] for i in ins])


def sum_parts(ins, outs):
    for part, out in enumerate(outs):
        span = slice(part * out.shape[0], (part + 1) * out.shape[0])
        out[...] = total(*[i[span] for i in ins])


def first_of(value):
    corner = lax.slice(value, (0,) * value.ndim, (1,) * value.ndim)
    return jnp.clip(corner.astype(F32).reshape(()), 0.0, 0.0)


def late(value, zero):
    return (value.astype(F32) + zero).astype(BF)


def across(value, links):
    if links.size <= 16:
        return value
    groups = [[low + 16 * high for high in range(links.size // 16)] for low in range(16)]
    return lax.psum(value, "dp", axis_index_groups=groups)


def join(*values):
    return jnp.concatenate(values, axis=0)


class Links:
    def __init__(self, size):
        self.size = size
        self.core = ("dp", self.flip(1))
        self.x = ("dp", self.flip(2))
        self.y = ("branch", [(0, 1), (1, 0)])
        self.corner = (
            ("branch", "dp"),
            [(b * size + i, (1 - b) * size + (i ^ 2)) for b in range(2) for i in range(size)],
        )
        self.z = [("dp", self.flip(4 * d)) for d in range(1, 4)]

    def flip(self, bits):
        return [(i, i ^ bits) for i in range(self.size)]


def cut(value, parts):
    return value.reshape(parts, -1, *value.shape[1:])


def send(pairs):
    return [lax.ppermute(value, *hop) for value, hop in pairs]


def plane(links):
    return [links.y, links.x, links.corner]


def load_pieces(pieces, buffer, sems):
    size = pieces[0].shape[0]
    copies = [
        pltpu.make_async_copy(piece, buffer.at[i * size : (i + 1) * size], sems.at[i])
        for i, piece in enumerate(pieces)
    ]
    for copy in copies:
        copy.start()
    for copy in copies:
        copy.wait()


def spread_middle_kernel(place, *rest):
    pieces, outs = rest[:8], rest[8:]
    inner_ref, outer_ref, mixer_ref, ib_ref, *vector_refs = outs[:-4]
    turn_s, rest_ref, grad_ref, sems = outs[-4:]
    load_pieces(pieces, grad_ref, sems)
    groups, width, inner = inner_ref.shape
    block = grad_ref.shape[1]
    features = mixer_ref.shape[1]
    targets = [inner_ref.at[0], inner_ref.at[1], turn_s.at[0], turn_s.at[1]]
    for part in range(MID_BLOCKS):
        start = part * block
        value = grad_ref[mid_slot(part, place)].astype(F32)
        if start < 2 * groups * width:
            target = targets[start // width]
            start = start % width
            target[start : start + block, :] = value
        elif start < 5 * width:
            start = start - 2 * groups * width
            mixer_ref[start : start + block, :] = value[:, :features]
            mixer_ref[width + start : width + start + block, :] = value[:, features:]
        else:
            start = start - 5 * width
            rest_ref[start : start + block, :] = value
    for g in range(groups):
        outer_ref[g] = turn_s[g].T
    ib_ref[...] = jnp.concatenate([rest_ref[0:1, :], rest_ref[1:2, :]], axis=1).reshape(-1)
    for number, ref in enumerate(vector_refs):
        row, col = 2 + number // 2, number % 2 * features
        ref[...] = rest_ref[row : row + 1, col : col + features].reshape(-1)


def spread_middle(place, pieces, width, inner, features):
    block = pieces[0].shape[1]
    outs = [
        jax.ShapeDtypeStruct((2, width, inner), F32),
        jax.ShapeDtypeStruct((2, inner, width), F32),
        jax.ShapeDtypeStruct((features, features), F32),
        jax.ShapeDtypeStruct((2 * inner,), F32),
        *[jax.ShapeDtypeStruct((features,), F32)] * 6,
    ]
    return pl.pallas_call(
        spread_middle_kernel,
        out_shape=outs,
        grid_spec=pltpu.PrefetchScalarGridSpec(
            num_scalar_prefetch=1,
            grid=(1,),
            in_specs=[pl.BlockSpec(memory_space=pl.ANY)] * len(pieces),
            out_specs=[whole(o) for o in outs],
            scratch_shapes=[
                pltpu.VMEM((2, width, inner), F32),
                pltpu.VMEM((MID_BLOCKS * block - 5 * width, inner), F32),
                pltpu.VMEM((MID_BLOCKS, block, inner), BF),
                pltpu.SemaphoreType.DMA((len(pieces),)),
            ],
        ),
        compiler_params=pltpu.CompilerParams(vmem_limit_bytes=VMEM_LIMIT),
        cost_estimate=pl.CostEstimate(flops=3 * 10**9, bytes_accessed=2 * 10**7, transcendentals=0),
        name="shared_gradients",
    )(place, *pieces)


def spread_branch_kernel(place, order_ref, turned_ref, *rest):
    pieces, outs = rest[:8], rest[9:]
    query_ref, keys_ref, values_ref, qb_ref, vb_ref, depth_ref, pb_ref, kw_ref, kb_ref = outs[:9]
    grad_ref, rest_s, sems = outs[9:]
    width = query_ref.shape[1]
    size = pieces[0].shape[0]
    shared = tail_shared(width)
    owned = grad_ref.shape[1] - shared
    copies = []
    for number, piece in enumerate(pieces):
        core, x, y = number // 4, number % 2, number // 2 % 2
        start = core << 4 | x << 3 | y << 2
        target = grad_ref.at[start : start + size]
        if y:
            target = grad_ref.at[start : start + size, owned:, :]
        copies.append(pltpu.make_async_copy(piece, target, sems.at[number]))
    for copy in copies:
        copy.start()
    for copy in copies:
        copy.wait()
    for within in range(4 * width // owned // 2):
        block = (within >> 2) << 3 | within & 3
        value = grad_ref[block ^ (place[MASK_T] & ~4), 0:owned, :].astype(F32)
        start = within * owned
        target = keys_ref if start < width else values_ref
        start = start % width
        target[0, start : start + owned, :] = value[:, :width]
        target[0, width + start : width + start + owned, :] = value[:, width:]
    for block in range(TAIL_BLOCKS):
        value = grad_ref[tail_slot(block, place), owned:, :].astype(F32)
        start = block * shared
        if start < width:
            query_ref[start : start + shared, :] = value[:, :width]
            query_ref[width + start : width + start + shared, :] = value[:, width:]
        else:
            rest_s[start - width : start - width + shared, :] = value
    taps = KERNEL * SLAB
    depth_ref[...] = rest_s[taps : taps + KERNEL, :]
    conv_line = rest_s[taps + KERNEL : taps + KERNEL + 1, :]
    att_line = rest_s[taps + 16 : taps + 17, :]
    qb_ref[...] = att_line[:, :width].reshape(-1)
    pb_ref[...] = conv_line[:, :width].reshape(-1)
    vb_ref[...] = jnp.where(place[SIDE] == 0, att_line[:, width:], conv_line[:, width:])
    kw_ref[...] = mm(turned_ref[...], rest_s[:, 0:width].astype(BF))
    taps_bias = mm(rest_s[:, width : width + LANES].T.astype(BF), order_ref[...])[0:1]
    kb_ref[...] = taps_bias.reshape(-1)


def spread_branch(place, ordered, pieces, width, features, wait):
    block = pieces[0].shape[1]
    outs = [
        jax.ShapeDtypeStruct((features, width), F32),
        jax.ShapeDtypeStruct((1, features, width), F32),
        jax.ShapeDtypeStruct((1, features, width), F32),
        jax.ShapeDtypeStruct((width,), F32),
        jax.ShapeDtypeStruct((1, width), F32),
        jax.ShapeDtypeStruct((KERNEL, features), F32),
        jax.ShapeDtypeStruct((width,), F32),
        jax.ShapeDtypeStruct((HEADS * KERNEL, width), F32),
        jax.ShapeDtypeStruct((HEADS * KERNEL,), F32),
    ]
    return pl.pallas_call(
        spread_branch_kernel,
        out_shape=outs,
        grid_spec=pltpu.PrefetchScalarGridSpec(
            num_scalar_prefetch=1,
            grid=(1,),
            in_specs=[whole(o) for o in ordered]
            + [pl.BlockSpec(memory_space=pl.ANY)] * (len(pieces) + 1),
            out_specs=[whole(o) for o in outs],
            scratch_shapes=[
                pltpu.VMEM((TAIL_BLOCKS, block, features), BF),
                pltpu.VMEM((TAIL_BLOCKS * tail_shared(width) - width, features), F32),
                pltpu.SemaphoreType.DMA((len(pieces),)),
            ],
        ),
        compiler_params=pltpu.CompilerParams(vmem_limit_bytes=VMEM_LIMIT),
        cost_estimate=pl.CostEstimate(flops=2 * 10**9, bytes_accessed=2 * 10**7, transcendentals=0),
        name="branch_gradients",
    )(place, *ordered, *pieces, wait)


def after(values, *others):
    return lax.optimization_barrier((tuple(values), others))[0]


def shards(
    size,
    hidden,
    bounds,
    query_weight,
    query_bias,
    branch_keys,
    branch_values,
    branch_bias,
    depth_kernel,
    point_bias,
    kernel_weight,
    kernel_bias,
    mixer_weight,
    mixer_bias,
    first_gain,
    first_shift,
    inner_weight,
    inner_bias,
    outer_weight,
    outer_bias,
    second_gain,
    second_shift,
    cotangent,
):
    links = Links(size)
    side = lax.axis_index("branch")
    index = lax.axis_index("dp")
    core, x, z = index & 1, (index >> 1) & 1, (index >> 2) & 3
    rows = hidden.shape[0] // 2
    features = hidden.shape[2]
    width = query_weight.shape[1]
    inner = inner_weight.shape[2]
    place = jnp.stack(
        [
            side * rows,
            side,
            core,
            core << 5 | x << 3 | side << 2 | z,
            core << 5 | side << 3 | x << 2 | z,
            core << 4 | x << 3 | side << 2 | z,
        ]
    ).astype(jnp.int32)

    def exchange(value):
        return lax.ppermute(value, *links.y)

    got = exchange(jnp.where(core == 0, branch_keys[0], branch_values[0]))
    got_bias = exchange(branch_bias)
    own_weights = (branch_keys[0], branch_values[0])
    far = ((1 - side) * rows).astype(jnp.int32)
    spread, ordered = spread_table(), order_table()
    flat_kernel = kernel_weight.T
    common = (depth_kernel, query_bias, point_bias, kernel_bias, flat_kernel, ordered, spread)
    bounds = bounds.T
    kept = forward(
        0, place, bounds, hidden, (query_weight, *own_weights, branch_bias, *common), rows
    )
    got, got_bias, cotangent = after((got, got_bias, cotangent), kept[0])
    got_weights = (got, lax.ppermute(got, *links.core))
    cot_got = exchange(lax.dynamic_slice_in_dim(cotangent, far, rows, 0))
    kept = forward(
        1, place, bounds, hidden, (query_weight, *got_weights, got_bias, *common), rows, kept
    )
    cat, q, k, v, probs, att_t, dm, kc, cq, joint, taps, vc = kept
    (cot_got,) = after([cot_got], cat)
    out_own, out_send, dcat, datt, dmix, mid_keep, mid_away = middle(
        place,
        hidden,
        cat,
        cotangent,
        cot_got,
        (
            mixer_weight,
            inner_weight,
            outer_weight,
            mixer_bias,
            first_gain,
            first_shift,
            inner_bias,
            outer_bias,
            second_gain,
            second_shift,
        ),
        rows,
    )
    conv_weights = (
        *own_weights, *got_weights, depth_kernel, flat_kernel, ordered, spread, gather_table()
    )
    att_weights = (query_weight, *own_weights, *got_weights)
    conv_kept = (dm, kc, cq, joint, taps, vc)
    att_kept = (q, k, v, probs, att_t)

    block = mid_keep.shape[1:]
    mid_keep, mid_away = cut(mid_keep, 4), cut(mid_away, 4)
    (mid_got,) = send([(mid_away, links.core)])
    conv0 = conv_back(place, 0, hidden, dcat, dmix, conv_kept, conv_weights, (), ())
    keep_a, away_a, keep_b, away_b = merge(
        sum_core, [(8, *block)] * 4, (mid_keep, mid_got), (), 4
    )
    got_a, got_b, out_got = send([(away_a, links.x), (away_b, links.y), (out_send, links.y)])
    conv1 = conv_back(
        place, 1, hidden, dcat, dmix, conv_kept, conv_weights, tuple(conv0[2:]), (keep_a,)
    )
    keep_a, away_a, keep_b, away_b = merge(
        sum_first, [(4, *block)] * 4, (keep_a, got_a, keep_b, got_b)
    )
    got_a, got_b = send([(away_a, links.y), (away_b, links.x)])
    att0 = att_back(
        place, 0, hidden, dcat, datt, conv0[0], conv0[1], att_kept, att_weights, (), (keep_a,)
    )
    mid, *away = merge(
        sum_second, [(2, *block)] * 4, (keep_a, got_a, keep_b, got_b)
    )
    got_z = send(zip(away, links.z))
    (hid_got0,) = send([(att0[1], links.y)])
    att1 = att_back(
        place,
        1,
        hidden,
        dcat,
        datt,
        conv1[0],
        conv1[1],
        att_kept,
        att_weights,
        tuple(att0[2:]),
        (mid, out_got),
    )
    tail_rows_each = tail_block(width)
    mid = across(total(mid, *got_z), links)
    tail_keep, tail_away = pack(place, (*att1[2:], *conv1[2:]), (mid, hid_got0))
    tail_got = send([(tail_away, links.core)])
    piece = (tail_rows_each, features)
    got_mid = send([(mid, hop) for hop in links.z])
    tail = cut(total(tail_keep, *tail_got), 4)
    got_tail = send(zip(tail[1:], plane(links)))
    tail = cut(total(tail[0], *got_tail), 4)
    got_tail = send(zip(tail[1:], links.z))
    zero = first_of(tail)
    pieces = [mid] + [late(got, zero) for got in got_mid]
    mid_a, mid_b = (join(*[m[order : order + 1] for m in pieces]) for order in range(2))
    got_a, got_b = send([(mid_a, links.y), (mid_b, links.x)])
    tail = across(total(tail[0], *got_tail), links)
    zero = first_of(tail)
    mid_a, mid_b = join(mid_a, late(got_a, zero)), join(mid_b, late(got_b, zero))
    got_a, got_b = send([(mid_a, links.x), (mid_b, links.y)])
    tail = late(tail, first_of(mid_a) + first_of(mid_b))
    got_tail = send([(tail, hop) for hop in links.z])
    mid = (mid_a, got_a, mid_b, got_b)
    tail = join(tail, *got_tail)
    zero = first_of(tail)
    far_mid = send([(late(m, zero), links.core) for m in mid])
    mid = (*mid, *far_mid)
    zero = first_of(far_mid[0])
    tail = late(tail, zero)
    shared = tail[:, tail.shape[1] - tail_shared(width) :]
    got_tail = send([(tail, links.x), (shared, links.y), (shared, links.corner)])
    (hid_got1,) = send([(late(att1[1], first_of(got_tail[0])), links.y)])
    tail = (tail, *got_tail)
    tail = (*tail, *send([(t, links.core) for t in tail]))
    grad_inner, grad_outer, grad_mixer, inner_line, *mid_lines = spread_middle(
        place, mid, width, inner, features
    )
    mixer_line, gain1_line, shift1_line, outer_line, gain2_line, shift2_line = mid_lines
    (
        query_grad,
        keys,
        values,
        query_line,
        value_line,
        depth,
        point_line,
        kernel_grad,
        kernel_line,
    ) = spread_branch(
        place, (ordered, jnp.asarray(ordered.T)), tail, width, features, mixer_line
    )
    def combine(own, got):
        return jnp.where(side == 0, join(own, got), join(got, own))

    output = combine(out_own, out_got)
    hidden_grad = combine(join(att0[0], att1[0]), join(hid_got0, hid_got1).astype(F32))
    return (
        output,
        hidden_grad,
        query_grad,
        query_line,
        keys,
        values,
        value_line,
        depth,
        point_line,
        kernel_grad.T,
        kernel_line,
        grad_mixer,
        mixer_line,
        gain1_line,
        shift1_line,
        grad_inner,
        inner_line,
        grad_outer,
        outer_line,
        gain2_line,
        shift2_line,
    )


def solution(mesh):
    split = P("dp", "branch", None)
    owned = P("branch", None, None)
    return jax.shard_map(
        functools.partial(shards, mesh.shape["dp"]),
        mesh=mesh,
        in_specs=(
            P("dp", None, None),
            P("dp", None),
            P(),
            P(),
            owned,
            owned,
            P("branch", None),
            *([P()] * 14),
            split,
        ),
        out_specs=(
            split,
            split,
            P(),
            P(),
            owned,
            owned,
            P("branch", None),
            *([P()] * 14),
        ),
        check_vma=False,
    )
```

```python
import functools

import jax
import jax.numpy as jnp
import numpy as np
from jax import lax
from jax.experimental import pallas as pl
from jax.experimental.pallas import tpu as pltpu
from jax.sharding import PartitionSpec as P

HEADS = 6
HEAD_SIZE = 64
KERNEL = 9
RADIUS = KERNEL // 2
SLAB = 8
LANES = 128
PAD = 8

NEGATIVE = -1000000000.0
EPSILON = 1e-05
INV_ROOT_TAU = 0.3989422804014327
ROOT_HALF = 0.7071067811865476
MID_BLOCKS = 64
TAIL_BLOCKS = 32
ORDER_BIT = 16
BASE, SIDE, CORE, MASK_A, MASK_B, MASK_T = range(6)

BF = jnp.bfloat16
F32 = jnp.float32
VMEM_LIMIT = 62 * 1024 * 1024


def mm(left, right):
    return jnp.dot(left, right, preferred_element_type=F32)


def mm_nt(left, right):
    return lax.dot_general(left, right, (((1,), (1,)), ((), ())), preferred_element_type=F32)


def block_rows(rows, blocks):
    return -(-rows // (16 * blocks)) * 16


def mid_slot(block, place):
    return block ^ (place[MASK_B] if block & ORDER_BIT else place[MASK_A])


def tail_block(width):
    return 4 * width // TAIL_BLOCKS + tail_shared(width)


def tail_shared(width):
    return -(-(width + LANES) // (16 * TAIL_BLOCKS)) * 16


def tail_rows(width, features):
    owned = 4 * width // TAIL_BLOCKS
    shared = tail_shared(width)
    spots = []
    for block in range(TAIL_BLOCKS):
        branch = block >> 2 & 1
        within = (block >> 3) * 4 + (block & 3)
        start = within * owned
        spots.append((1 + 2 * branch + start // width, start % width, block, 0, owned))
        spots.append((0, block * shared, block, owned, shared))
    return spots


def tail_slot(block, place):
    return block ^ place[MASK_T]


def send_halves(buffer, keep, away, sems):
    half = keep.shape[0]
    copies = [
        pltpu.make_async_copy(buffer.at[half : 2 * half], away, sems.at[1]),
        pltpu.make_async_copy(buffer.at[0:half], keep, sems.at[0]),
    ]
    for copy in copies:
        copy.start()
    for copy in copies:
        copy.wait()


def start_copies(pairs, sems):
    copies = [pltpu.make_async_copy(a, b, sems.at[i]) for i, (a, b) in enumerate(pairs)]
    for copy in copies:
        copy.start()
    return copies


def pick_weights(place, branch, weights):
    own_keys, own_values, first, second = (weights[i] for i in range(4))
    mine, even = place[SIDE] == branch, place[CORE] == 0
    return (
        jnp.where(mine, own_keys, jnp.where(even, first, second)),
        jnp.where(mine, own_values, jnp.where(even, second, first)),
    )


def rowsum(value):
    return jnp.sum(value, axis=0, keepdims=True)


def fill_strips(strips_ref, value, length):
    strips = strips_ref.shape[0]
    zero = jnp.zeros((PAD, LANES), F32)
    for strip in range(strips):
        strips_ref[strip, 0:PAD, :] = zero
        strips_ref[strip, PAD + length : 2 * PAD + length, :] = zero
        strips_ref[strip, PAD : PAD + length, :] = value[
            :, strip * LANES : (strip + 1) * LANES
        ].astype(F32)


def head_pair_rows(rows, head):
    own = rows[head * HEAD_SIZE : (head + 1) * HEAD_SIZE, :]
    zero = jnp.zeros_like(own)
    return jnp.concatenate([own, zero] if head % 2 == 0 else [zero, own], axis=0)


def line(ref):
    return ref[...].reshape(1, -1)


def tapped_weights(order_ref, kw_ref):
    return mm(order_ref[...], kw_ref[...]).astype(BF)


def forward_kernel(
    order,
    place,
    bounds,
    x_ref,
    wq_ref,
    wa_ref,
    wb_ref,
    bb_ref,
    depth_ref,
    qb_ref,
    pb_ref,
    kb_ref,
    kw_ref,
    order_ref,
    spread_ref,
    *rest,
):
    (
        cat_ref,
        q_ref,
        k_ref,
        v_ref,
        probs_ref,
        att_t_ref,
        dm_ref,
        kc_ref,
        cq_ref,
        joint_ref,
        taps_ref,
        vc_ref,
        qt_s,
        vt_s,
        xs_s,
        vs_s,
        tw_s,
        wide_s,
    ) = rest[-18:]
    row = place[BASE] + pl.program_id(0)
    width = HEADS * HEAD_SIZE
    wa, wb = wa_ref[...], wb_ref[...]
    if order:
        even = place[CORE] == 0
        wa, wb = jnp.where(even, wa, wb), jnp.where(even, wb, wa)
    first_end = bounds[0, row]
    valid = bounds[1, row]
    length = x_ref.shape[1]
    x = x_ref[0]
    queries = (mm(x, wq_ref[...]) + line(qb_ref)).astype(BF)

    @pl.when(place[SIDE] == order)
    def _():
        scaled = (queries.astype(F32) * (HEAD_SIZE**-0.5)).astype(BF)
        q_ref[0] = scaled
        qt_s[...] = scaled.T
        k_ref[0] = mm(x, wa).astype(BF)
        v = (mm(x, wb) + bb_ref[...]).astype(BF)
        v_ref[0] = v
        vt_s[...] = v.T
        seen = lax.broadcasted_iota(jnp.int32, (length, 1), 0) < valid
        for head in range(HEADS):
            pair = head // 2
            keys = k_ref[0, :, pair * LANES : (pair + 1) * LANES]
            scores = mm(keys, head_pair_rows(qt_s, head))
            scores = jnp.where(seen, scores, NEGATIVE)
            raised = jnp.exp(scores - jnp.max(scores, axis=0, keepdims=True))
            probs = (raised * (1.0 / rowsum(raised))).astype(BF)
            probs_ref[0, head] = probs
            span = slice(head * HEAD_SIZE, (head + 1) * HEAD_SIZE)
            att_t_ref[0, span, :] = mm(vt_s[span, :], probs).astype(BF)
        cat_ref[0] = att_t_ref[0].T

    @pl.when(place[SIDE] != order)
    def _():
        fill_strips(xs_s, x, length)
        piece = LANES
        for strip in range(xs_s.shape[0]):
            lanes = slice(strip * LANES, (strip + 1) * LANES)
            for at in range(0, length, piece):
                total = None
                for tap in range(KERNEL):
                    begin = PAD - RADIUS + tap + at
                    term = xs_s[strip, begin : begin + piece, :] * depth_ref[tap : tap + 1, lanes]
                    total = term if total is None else total + term
                dm_ref[0, at : at + piece, lanes] = total.astype(BF)
        key_conv = mm(dm_ref[0], wa) + line(pb_ref)
        kc_ref[0] = key_conv
        cq_ref[0] = queries
        joint = (key_conv * queries.astype(F32)).astype(BF)
        joint_ref[0] = joint
        tap_bias = jnp.sum(order_ref[...].astype(F32) * line(kb_ref), axis=1, keepdims=True)
        logits = mm_nt(tapped_weights(order_ref, kw_ref), joint) + tap_bias
        here = lax.broadcasted_iota(jnp.int32, (SLAB, length), 1)

        def segment(position):
            return jnp.where(position <= first_end, 0, jnp.where(position < valid, 1, 2))

        own_segment = segment(here)
        slabs = []
        for tap in range(KERNEL):
            other = here + (tap - RADIUS)
            same = (other >= 0) & (other < length) & (segment(other) == own_segment)
            slabs.append(jnp.where(same, logits[tap * SLAB : (tap + 1) * SLAB], NEGATIVE))
        peak = functools.reduce(jnp.maximum, slabs)
        slabs = [jnp.exp(slab - peak) for slab in slabs]
        inverse = 1.0 / functools.reduce(jnp.add, slabs)
        for tap in range(KERNEL):
            tw_s[tap * SLAB : (tap + 1) * SLAB, :] = slabs[tap] * inverse
        tw_s[KERNEL * SLAB :, :] = jnp.zeros((LANES - KERNEL * SLAB, length), F32)
        taps_ref[0] = tw_s[...]
        taps = tw_s[...].T
        high = taps.astype(BF)
        low = (taps - high.astype(F32)).astype(BF)
        both = jnp.concatenate([high, low], axis=1)
        for tap in range(KERNEL):
            cols = slice(tap * width, (tap + 1) * width)
            wide_s[:, cols] = mm(both, spread_ref[:, cols])
        vc = (mm(x, wb) + bb_ref[...]).astype(BF)
        vc_ref[0] = vc
        fill_strips(vs_s, vc, length)
        for strip in range(vs_s.shape[0]):
            for at in range(0, length, piece):
                total = None
                for tap in range(KERNEL):
                    begin = PAD - RADIUS + tap + at
                    col = tap * width + strip * LANES
                    term = (
                        vs_s[strip, begin : begin + piece, :]
                        * wide_s[at : at + piece, col : col + LANES]
                    )
                    total = term if total is None else total + term
                cat_ref[0, at : at + piece, strip * LANES : (strip + 1) * LANES] = total.astype(BF)


def spread_table():
    table = np.zeros((2 * LANES, KERNEL, HEADS, HEAD_SIZE), np.float32)
    for tap in range(KERNEL):
        for head in range(HEADS):
            table[tap * SLAB + head, tap, head, :] = 1
            table[LANES + tap * SLAB + head, tap, head, :] = 1
    return jnp.asarray(table.reshape(2 * LANES, -1), BF)


def gather_table():
    table = np.zeros((KERNEL, HEADS, HEAD_SIZE, LANES), np.float32)
    for tap in range(KERNEL):
        for head in range(HEADS):
            table[tap, head, :, tap * SLAB + head] = 1
    return jnp.asarray(table.reshape(-1, LANES), BF)


def order_table():
    table = np.zeros((LANES, HEADS * KERNEL), np.float32)
    for tap in range(KERNEL):
        for head in range(HEADS):
            table[tap * SLAB + head, head * KERNEL + tap] = 1
    return jnp.asarray(table, BF)


def whole(array, buffers=2):
    rank = len(array.shape)
    mode = pl.Buffered(buffers) if buffers < 2 else None
    return pl.BlockSpec(array.shape, lambda *_: (0,) * rank, pipeline_mode=mode)


def forward(order, place, bounds, hidden, weights, rows, before=None):
    length, features = hidden.shape[1:]
    width = HEADS * HEAD_SIZE
    spare = rows

    def att_row(r, place, bounds):
        return jnp.where(place[SIDE] == order, r, spare)

    def conv_row(r, place, bounds):
        return jnp.where(place[SIDE] != order, r, spare)

    def saved(row_of, shape, dtype):
        zeros = (0,) * len(shape)
        return (
            jax.ShapeDtypeStruct((rows + 1,) + shape, dtype),
            pl.BlockSpec((1,) + shape, lambda r, p, b: (row_of(r, p, b),) + zeros),
        )

    outs = [
        (
            jax.ShapeDtypeStruct((rows, length, 2 * width), BF),
            pl.BlockSpec((1, length, width), lambda r, p, b: (r, 0, jnp.where(p[SIDE] == order, 0, 1))),
        ),
        saved(att_row, (length, width), BF),
        saved(att_row, (length, width), BF),
        saved(att_row, (length, width), BF),
        saved(att_row, (HEADS, length, length), BF),
        saved(att_row, (width, length), BF),
        saved(conv_row, (length, features), BF),
        saved(conv_row, (length, width), F32),
        saved(conv_row, (length, width), BF),
        saved(conv_row, (length, width), BF),
        saved(conv_row, (LANES, length), F32),
        saved(conv_row, (length, width), BF),
    ]
    in_specs = [pl.BlockSpec((1, length, features), lambda r, p, b: (p[0] + r, 0, 0))]
    in_specs += [whole(w) for w in weights]
    args = [place, bounds, hidden, *weights]
    aliases = {}
    if before is not None:
        aliases = {len(args) + i: i for i in range(len(before))}
        in_specs += [pl.BlockSpec(memory_space=pl.ANY)] * len(before)
        args += list(before)
    return pl.pallas_call(
        functools.partial(forward_kernel, order),
        out_shape=[o[0] for o in outs],
        grid_spec=pltpu.PrefetchScalarGridSpec(
            num_scalar_prefetch=2,
            grid=(rows,),
            in_specs=in_specs,
            out_specs=[o[1] for o in outs],
            scratch_shapes=[
                pltpu.VMEM((width, length), BF),
                pltpu.VMEM((width, length), BF),
                pltpu.VMEM((features // LANES, length + 2 * PAD, LANES), F32),
                pltpu.VMEM((width // LANES, length + 2 * PAD, LANES), F32),
                pltpu.VMEM((LANES, length), F32),
                pltpu.VMEM((length, KERNEL * width), F32),
            ],
        ),
        input_output_aliases=aliases,
        compiler_params=pltpu.CompilerParams(vmem_limit_bytes=VMEM_LIMIT),
        cost_estimate=pl.CostEstimate(flops=10**10, bytes_accessed=2 * 10**7, transcendentals=0),
        name="branch_forward",
    )(*args)


def norm(value):
    center = value - jnp.mean(value, axis=-1, keepdims=True)
    factor = lax.rsqrt(jnp.mean(center * center, axis=-1, keepdims=True) + EPSILON)
    return center * factor, factor


def norm_back(gradient, normed, factor):
    return factor * (
        gradient
        - jnp.mean(gradient, axis=-1, keepdims=True)
        - normed * jnp.mean(gradient * normed, axis=-1, keepdims=True)
    )


def middle_kernel(
    place,
    x_ref,
    cat_ref,
    cot_own_ref,
    cot_got_ref,
    mw_ref,
    iw_ref,
    ow_ref,
    mixer_bias,
    gain1,
    shift1,
    inner_bias,
    outer_bias,
    gain2,
    shift2,
    own_ref,
    send_ref,
    dcat_ref,
    datt_ref,
    dmix_ref,
    keep_ref,
    away_ref,
    grad_ref,
    sems,
    vec_s,
    rest_s,
    acc_i,
    acc_o,
    acc_m,
    act_s,
    slope_s,
    din_s,
):
    step = pl.program_id(0)
    first_side = place[SIDE] == 0
    features = x_ref.shape[2]
    half = x_ref.shape[1] // 2
    groups, width, inner = iw_ref.shape
    piece = 512

    mixer_bias, gain1, shift1, inner_bias, outer_bias, gain2, shift2 = (
        line(r) for r in (mixer_bias, gain1, shift1, inner_bias, outer_bias, gain2, shift2)
    )

    @pl.when(step == 0)
    def _():
        acc_i[...] = jnp.zeros_like(acc_i)
        acc_o[...] = jnp.zeros_like(acc_o)
        acc_m[...] = jnp.zeros_like(acc_m)
        vec_s[...] = jnp.zeros_like(vec_s)

    cat = cat_ref[0]
    normed1, factor1 = norm(x_ref[0].astype(F32) + (mm(cat, mw_ref[...]) + mixer_bias))
    first = (normed1 * gain1 + shift1).astype(BF)
    projected = []
    for g in range(groups):
        part = first[:, g * width : (g + 1) * width]
        for at in range(0, inner, piece):
            lanes = slice(g * inner + at, g * inner + at + piece)
            pre = mm(part, iw_ref[g, :, at : at + piece]) + inner_bias[:, lanes]
            phi = 0.5 + 0.5 * lax.erf(pre * ROOT_HALF)
            bell = jnp.exp(-0.5 * pre * pre) * INV_ROOT_TAU
            act_s[:, lanes] = (pre * phi).astype(BF)
            slope_s[:, lanes] = phi + pre * bell
        projected.append(mm(act_s[:, g * inner : (g + 1) * inner], ow_ref[g]))
    projected = jnp.concatenate(projected, axis=1)
    normed2, factor2 = norm(first.astype(F32) + (projected + outer_bias))
    output = normed2 * gain2 + shift2
    own_ref[0] = jnp.where(first_side, output[:half], output[half:]).astype(BF)
    send_ref[0] = jnp.where(first_side, output[half:], output[:half]).astype(BF)
    cot_own, cot_got = cot_own_ref[0].astype(F32), cot_got_ref[0].astype(F32)
    cot = jnp.concatenate(
        [jnp.where(first_side, cot_own, cot_got), jnp.where(first_side, cot_got, cot_own)], axis=0
    )
    dsecond = norm_back(cot * gain2, normed2, factor2)
    dproj = dsecond.astype(BF)
    vec_s[1:2, 3 * features : 4 * features] += rowsum(dproj.astype(F32))
    vec_s[2:3, 0:features] += rowsum(cot * normed2)
    vec_s[2:3, features : 2 * features] += rowsum(cot)
    dfirst = []
    for g in range(groups):
        cols = slice(g * width, (g + 1) * width)
        dpart = dproj[:, cols]
        for at in range(0, inner, piece):
            lanes = slice(g * inner + at, g * inner + at + piece)
            dact = mm_nt(dpart, ow_ref[g, at : at + piece, :]).astype(BF)
            din = (dact.astype(F32) * slope_s[:, lanes]).astype(BF)
            din_s[:, lanes] = din
            vec_s[0:1, lanes] += rowsum(din.astype(F32))
        group = slice(g * inner, (g + 1) * inner)
        acc_o[g] += mm(dpart.T, act_s[:, group])
        acc_i[g] += mm(first[:, cols].T, din_s[:, group])
        dfirst.append(dsecond[:, cols] + mm_nt(din_s[:, group], iw_ref[g]))
    dfirst = jnp.concatenate(dfirst, axis=1)
    vec_s[1:2, features : 2 * features] += rowsum(dfirst * normed1)
    vec_s[1:2, 2 * features : 3 * features] += rowsum(dfirst)
    dmixed = norm_back(dfirst * gain1, normed1, factor1)
    dmix_ref[0] = dmixed
    dmixer = dmixed.astype(BF)
    vec_s[1:2, 0:features] += rowsum(dmixer.astype(F32))
    acc_m[...] += mm(cat.T, dmixer)
    dcat_ref[0] = mm_nt(dmixer, mw_ref[...]).astype(BF)
    datt_ref[0] = mm_nt(mw_ref[0:width, :], dmixer).astype(BF)

    @pl.when(step == pl.num_programs(0) - 1)
    def _():
        rest_s[0:1, :] = vec_s[0:1, 0:inner]
        rest_s[1:2, :] = vec_s[0:1, inner:]
        rest_s[2:3, :] = vec_s[1:2, 0:inner]
        rest_s[3:4, :] = vec_s[1:2, inner:]
        rest_s[4:5, :] = vec_s[2:3, 0:inner]
        rest_s[5:, :] = jnp.zeros((rest_s.shape[0] - 5, inner), F32)
        block = grad_ref.shape[1]
        sources = [acc_i.at[0], acc_i.at[1], acc_o.at[0], acc_o.at[1]]
        for part in range(MID_BLOCKS):
            start = part * block
            slot = mid_slot(part, place)
            if start < 2 * groups * width:
                source = sources[start // width]
                start = start % width
                grad_ref[slot] = source[start : start + block, :].astype(BF)
            elif start < 5 * width:
                start = start - 2 * groups * width
                grad_ref[slot, :, 0:features] = acc_m[start : start + block, :].astype(BF)
                start = start + width
                grad_ref[slot, :, features:] = acc_m[start : start + block, :].astype(BF)
            else:
                start = start - 5 * width
                grad_ref[slot] = rest_s[start : start + block, :].astype(BF)
        send_halves(grad_ref, keep_ref, away_ref, sems)


def middle(place, hidden, cat, cot_own, cot_got, weights, rows):
    length, features = hidden.shape[1:]
    half = length // 2
    groups, width, inner = weights[1].shape
    block = block_rows(5 * width, MID_BLOCKS)
    sent = jax.ShapeDtypeStruct((MID_BLOCKS // 2, block, inner), BF)

    def per_row(*shape, dtype=BF):
        return (
            jax.ShapeDtypeStruct((rows,) + shape, dtype),
            pl.BlockSpec((1,) + shape, lambda s, p: (s, 0, 0)),
        )

    outs = [
        per_row(half, features),
        per_row(half, features),
        per_row(length, features),
        per_row(width, length),
        per_row(length, features, dtype=F32),
        (sent, pl.BlockSpec(memory_space=pl.ANY)),
        (sent, pl.BlockSpec(memory_space=pl.ANY)),
    ]
    return pl.pallas_call(
        middle_kernel,
        out_shape=[o[0] for o in outs],
        grid_spec=pltpu.PrefetchScalarGridSpec(
            num_scalar_prefetch=1,
            grid=(rows,),
            in_specs=[
                pl.BlockSpec((1, length, features), lambda s, p: (p[0] + s, 0, 0)),
                pl.BlockSpec((1, length, features), lambda s, p: (s, 0, 0)),
                pl.BlockSpec((1, half, features), lambda s, p: (p[0] + s, 0, 0)),
                pl.BlockSpec((1, half, features), lambda s, p: (s, 0, 0)),
                *[whole(w, 1) for w in weights],
            ],
            out_specs=[o[1] for o in outs],
            scratch_shapes=[
                pltpu.VMEM((MID_BLOCKS, block, inner), BF),
                pltpu.SemaphoreType.DMA((2,)),
                pltpu.VMEM((SLAB, groups * inner), F32),
                pltpu.VMEM((MID_BLOCKS * block - 5 * width, inner), F32),
                pltpu.VMEM((groups, width, inner), F32),
                pltpu.VMEM((groups, width, inner), F32),
                pltpu.VMEM((features, features), F32),
                pltpu.VMEM((length, groups * inner), BF),
                pltpu.VMEM((length, groups * inner), F32),
                pltpu.VMEM((length, groups * inner), BF),
            ],
        ),
        compiler_params=pltpu.CompilerParams(vmem_limit_bytes=VMEM_LIMIT),
        cost_estimate=pl.CostEstimate(flops=10**10, bytes_accessed=2 * 10**7, transcendentals=0),
        name="shared_layers",
    )(place, hidden, cat, cot_own, cot_got, *weights)


def conv_back_kernel(
    row,
    waits,
    place,
    x_ref,
    dcat_ref,
    dmix_ref,
    dm_ref,
    kc_ref,
    q_ref,
    joint_ref,
    taps_ref,
    vc_ref,
    own_a_ref,
    own_b_ref,
    got_a_ref,
    got_b_ref,
    depth_ref,
    kw_ref,
    order_ref,
    spread_ref,
    collect_ref,
    *rest,
):
    rest = rest[waits:]
    before = rest[:-20]
    part_ref, dq_ref, acc_a, acc_b, small_ref, kgrad_ref = rest[-20:-14]
    vs_s, xs_s, ys_s, ds_s, prod_s = rest[-14:-9]
    joint_s, q_s, kc_s, w_s, dm_s, x_s, dmix_s, old_s, sems = rest[-9:]
    length, features = x_s.shape
    width = HEADS * HEAD_SIZE
    piece = LANES
    weights = (own_a_ref, own_b_ref, got_a_ref, got_b_ref)
    pairs = [(joint_ref.at[row], joint_s), (q_ref.at[row], q_s), (kc_ref.at[row], kc_s)]
    pairs += [(weight, w_s.at[i]) for i, weight in enumerate(weights)]
    pairs += [(dm_ref.at[row], dm_s), (x_ref.at[place[BASE] + row], x_s), (dmix_ref.at[row], dmix_s)]
    pairs += [(old, old_s.at[i]) for i, old in enumerate(before[:2])]
    copies = start_copies(pairs, sems)
    for index, ref in enumerate((small_ref, kgrad_ref)):
        ref[...] = before[2 + index][...] if before else jnp.zeros_like(ref)
    dconv = dcat_ref[0].astype(F32)
    fill_strips(vs_s, vc_ref[0], length)
    taps_t = taps_ref[0]
    taps = taps_t.T
    high = taps.astype(BF)
    low = (taps - high.astype(F32)).astype(BF)
    both = jnp.concatenate([high, low], axis=1)
    zero = jnp.zeros((PAD, LANES), F32)
    for tap in range(KERNEL):
        spread = mm(both, spread_ref[:, tap * width : (tap + 1) * width])
        for strip in range(width // LANES):
            lanes = slice(strip * LANES, (strip + 1) * LANES)
            begin = PAD - RADIUS + tap
            prod_s[:, tap * width + strip * LANES : tap * width + (strip + 1) * LANES] = (
                dconv[:, lanes] * vs_s[strip, begin : begin + length, :]
            ).astype(BF)
            slot = tap * (width // LANES) + strip
            ys_s[slot, 0:PAD, :] = zero
            ys_s[slot, PAD + length :, :] = zero
            ys_s[slot, PAD : PAD + length, :] = spread[:, lanes] * dconv[:, lanes]
    dvc = []
    for strip in range(width // LANES):
        total = None
        for tap in range(KERNEL):
            begin = PAD + RADIUS - tap
            term = ys_s[tap * (width // LANES) + strip, begin : begin + length, :]
            total = term if total is None else total + term
        dvc.append(total.astype(BF))
    dvc = jnp.concatenate(dvc, axis=1)
    dtaps = mm(prod_s[...], collect_ref[...]).T
    slabs = [dtaps[t * SLAB : (t + 1) * SLAB] for t in range(KERNEL)]
    weights = [taps_t[t * SLAB : (t + 1) * SLAB] for t in range(KERNEL)]
    total = functools.reduce(jnp.add, [a * b for a, b in zip(slabs, weights)])
    slabs = [b * (a - total) for a, b in zip(slabs, weights)]
    slabs.append(jnp.zeros((LANES - KERNEL * SLAB, length), F32))
    dlogits_t = jnp.concatenate(slabs, axis=0)
    dlogits = dlogits_t.T.astype(BF)
    rounded_t = dlogits_t.astype(BF)
    for copy in copies:
        copy.wait()
    wa, wb = pick_weights(place, 1, w_s)
    x = x_s[...]
    kgrad_ref[:, 0:width] += mm(rounded_t, joint_s[...])
    kgrad_ref[:, width : width + LANES] += jnp.broadcast_to(
        jnp.sum(rounded_t.astype(F32), axis=1, keepdims=True), (LANES, LANES)
    )
    djoint = mm(dlogits, tapped_weights(order_ref, kw_ref)).astype(BF).astype(F32)
    dkey = (djoint * q_s[...].astype(F32)).astype(BF)
    dq_ref[0] = (djoint * kc_s[...]).astype(BF)
    small_ref[9:10, 0:width] += rowsum(dkey.astype(F32))
    small_ref[9:10, width : 2 * width] += rowsum(dvc.astype(F32))
    ddepth = mm_nt(dkey, wa).astype(BF)
    acc_a[...] = mm(dm_s[...].T, dkey)
    acc_b[...] = mm(x.T, dvc)
    if before:
        acc_a[...] += old_s[0]
        acc_b[...] += old_s[1]
    part_ref[0] = dmix_s[...] + mm_nt(dvc, wb)
    fill_strips(ds_s, ddepth, length)
    fill_strips(xs_s, x, length)
    for strip in range(features // LANES):
        lanes = slice(strip * LANES, (strip + 1) * LANES)
        sums = [None] * KERNEL
        for at in range(0, length, piece):
            total = part_ref[0, at : at + piece, lanes]
            center = ds_s[strip, PAD + at : PAD + at + piece, :]
            for tap in range(KERNEL):
                begin = PAD + RADIUS - tap + at
                total = total + ds_s[strip, begin : begin + piece, :] * depth_ref[tap : tap + 1, lanes]
                begin = PAD - RADIUS + tap + at
                term = (xs_s[strip, begin : begin + piece, :] * center).reshape(-1, SLAB, LANES)
                term = jnp.sum(term, axis=0)
                sums[tap] = term if sums[tap] is None else sums[tap] + term
            part_ref[0, at : at + piece, lanes] = total
        for tap in range(KERNEL):
            small_ref[tap : tap + 1, lanes] += rowsum(sums[tap])


def conv_back(place, row, hidden, dcat, dmix, kept, weights, before, waits):
    length, features = hidden.shape[1:]
    width = HEADS * HEAD_SIZE

    def by_row(array):
        zeros = (0,) * (array.ndim - 1)
        return pl.BlockSpec((1,) + array.shape[1:], lambda r, p: (row,) + zeros)

    outs = [
        jax.ShapeDtypeStruct((1, length, features), F32),
        jax.ShapeDtypeStruct((1, length, width), BF),
        jax.ShapeDtypeStruct((features, width), F32),
        jax.ShapeDtypeStruct((features, width), F32),
        jax.ShapeDtypeStruct((16, features), F32),
        jax.ShapeDtypeStruct((LANES, width + LANES), F32),
    ]
    strips = features // LANES
    anywhere = pl.BlockSpec(memory_space=pl.ANY)
    return pl.pallas_call(
        functools.partial(conv_back_kernel, row, len(waits)),
        out_shape=outs,
        grid_spec=pltpu.PrefetchScalarGridSpec(
            num_scalar_prefetch=1,
            grid=(1,),
            in_specs=[
                anywhere,
                pl.BlockSpec((1, length, width), lambda r, p: (row, 0, 1)),
                *[anywhere] * 5,
                *[by_row(a) for a in kept[4:]],
                *[anywhere] * 4,
                *[whole(w) for w in weights[4:]],
                *[anywhere] * len(waits),
                *[anywhere] * len(before[:2]),
                *[whole(a) for a in before[2:]],
            ],
            out_specs=[whole(o) for o in outs],
            scratch_shapes=[
                pltpu.VMEM((width // LANES, length + 2 * PAD, LANES), F32),
                pltpu.VMEM((strips, length + 2 * PAD, LANES), F32),
                pltpu.VMEM((KERNEL * width // LANES, length + 2 * PAD, LANES), F32),
                pltpu.VMEM((strips, length + 2 * PAD, LANES), F32),
                pltpu.VMEM((length, KERNEL * width), BF),
                pltpu.VMEM((length, width), BF),
                pltpu.VMEM((length, width), BF),
                pltpu.VMEM((length, width), F32),
                pltpu.VMEM((4, features, width), BF),
                pltpu.VMEM((length, features), BF),
                pltpu.VMEM((length, features), BF),
                pltpu.VMEM((length, features), F32),
                pltpu.VMEM((2, features, width), F32),
                pltpu.SemaphoreType.DMA((12,)),
            ],
        ),
        compiler_params=pltpu.CompilerParams(vmem_limit_bytes=VMEM_LIMIT),
        cost_estimate=pl.CostEstimate(flops=10**10, bytes_accessed=2 * 10**7, transcendentals=0),
        name="convolution_backward",
    )(place, hidden, dcat, dmix, *kept, *weights, *waits, *before)


def att_back_kernel(
    row,
    waits,
    place,
    x_ref,
    dcat_ref,
    datt_ref,
    part_ref,
    dqc_ref,
    q_ref,
    k_ref,
    v_ref,
    probs_ref,
    att_t_ref,
    wq_ref,
    own_a_ref,
    own_b_ref,
    got_a_ref,
    got_b_ref,
    *rest,
):
    rest = rest[waits:]
    before = rest[:-15]
    own_ref, send_ref, acc_s, small_ref, kt_s, dqt_s, dk_s, dv_s, total_s = rest[-15:-6]
    probs_s, x_s, w_s, part_s, old_s, sems = rest[-6:]
    length, features = x_s.shape
    width = HEADS * HEAD_SIZE
    weights = (own_a_ref, own_b_ref, got_a_ref, got_b_ref, wq_ref)
    pairs = [(probs_ref.at[row, head], probs_s.at[head]) for head in range(HEADS)]
    pairs += [(x_ref.at[place[BASE] + row], x_s)]
    pairs += [(weight, w_s.at[i]) for i, weight in enumerate(weights)]
    pairs += [(part_ref.at[0], part_s)]
    pairs += [(old, old_s) for old in before[:1]]
    copies = start_copies(pairs, sems)
    small_ref[...] = before[1][...] if before else jnp.zeros_like(small_ref)
    scaled_keys = (k_ref[0].astype(F32) * (HEAD_SIZE**-0.5)).astype(BF)
    kt_s[...] = scaled_keys.T
    low_lane = lax.broadcasted_iota(jnp.int32, (1, LANES), 1) < HEAD_SIZE
    for pair in range(HEADS // 2):
        lanes = slice(pair * LANES, (pair + 1) * LANES)
        d_pair = dcat_ref[0, :, lanes]
        q_pair = q_ref[0, :, lanes]
        v_pair = v_ref[0, :, lanes]
        dk = jnp.zeros((length, LANES), F32)
        dv = jnp.zeros((length, LANES), F32)
        for head in (2 * pair, 2 * pair + 1):
            span = slice(head * HEAD_SIZE, (head + 1) * HEAD_SIZE)
            keep = low_lane if head % 2 == 0 else jnp.logical_not(low_lane)
            d_own = datt_ref[0, span, :].astype(F32)
            delta = rowsum(d_own * att_t_ref[0, span, :].astype(F32))
            dp = mm(v_pair, head_pair_rows(datt_ref[0], head))
            copies[head].wait()
            probs = probs_s[head]
            dscores = (probs.astype(F32) * (dp - delta)).astype(BF)
            dqt_s[span, :] = mm(kt_s[span, :], dscores)
            dv = dv + mm(probs, jnp.where(keep, d_pair, jnp.zeros_like(d_pair)))
            dk = dk + mm(dscores, jnp.where(keep, q_pair, jnp.zeros_like(q_pair)))
        dk_s[:, lanes] = dk.astype(BF)
        dv_s[:, lanes] = dv.astype(BF)
    dq = dqt_s[...].T.astype(BF).astype(F32) + dqc_ref[0].astype(F32)
    small_ref[0:1, 0:width] += rowsum(dq)
    small_ref[0:1, width : 2 * width] += rowsum(dv_s[...].astype(F32))
    dq = dq.astype(BF)
    for copy in copies[HEADS:]:
        copy.wait()
    wk, wv = pick_weights(place, 0, w_s)
    x_t = x_s[...].T
    for number, gradient in enumerate((dq, dk_s[...], dv_s[...])):
        product = mm(x_t, gradient)
        acc_s[number] = product + old_s[number] if before else product
    total_s[...] = (
        part_s[...]
        + mm_nt(dq, w_s[4])
        + mm_nt(dk_s[...], wk)
        + mm_nt(dv_s[...], wv)
    )
    half = length // 2
    mine = pl.multiple_of(place[SIDE] * half, half)
    other = pl.multiple_of((1 - place[SIDE]) * half, half)
    own_ref[0] = total_s[pl.ds(mine, half), :]
    send_ref[0] = total_s[pl.ds(other, half), :].astype(BF)


def att_back(place, row, hidden, dcat, datt, part, dqc, kept, weights, before, waits):
    length, features = hidden.shape[1:]
    width = HEADS * HEAD_SIZE
    half = length // 2
    anywhere = pl.BlockSpec(memory_space=pl.ANY)

    def by_row(array):
        zeros = (0,) * (array.ndim - 1)
        return pl.BlockSpec((1,) + array.shape[1:], lambda r, p: (row,) + zeros)

    outs = [
        jax.ShapeDtypeStruct((1, half, features), F32),
        jax.ShapeDtypeStruct((1, half, features), BF),
        jax.ShapeDtypeStruct((3, features, width), F32),
        jax.ShapeDtypeStruct((SLAB, features), F32),
    ]
    return pl.pallas_call(
        functools.partial(att_back_kernel, row, len(waits)),
        out_shape=outs,
        grid_spec=pltpu.PrefetchScalarGridSpec(
            num_scalar_prefetch=1,
            grid=(1,),
            in_specs=[
                anywhere,
                pl.BlockSpec((1, length, width), lambda r, p: (row, 0, 0)),
                by_row(datt),
                anywhere,
                whole(dqc),
                *[by_row(a) for a in kept[:3]],
                anywhere,
                by_row(kept[4]),
                *[anywhere] * (len(weights) + len(waits)),
                *[anywhere] * len(before[:1]),
                *[whole(a) for a in before[1:]],
            ],
            out_specs=[whole(o) for o in outs],
            scratch_shapes=[
                pltpu.VMEM((width, length), BF),
                pltpu.VMEM((width, length), F32),
                pltpu.VMEM((length, width), BF),
                pltpu.VMEM((length, width), BF),
                pltpu.VMEM((length, features), F32),
                pltpu.VMEM((HEADS, length, length), BF),
                pltpu.VMEM((length, features), BF),
                pltpu.VMEM((5, features, width), BF),
                pltpu.VMEM((length, features), F32),
                pltpu.VMEM((3, features, width), F32),
                pltpu.SemaphoreType.DMA((HEADS + 8,)),
            ],
        ),
        compiler_params=pltpu.CompilerParams(vmem_limit_bytes=VMEM_LIMIT),
        cost_estimate=pl.CostEstimate(flops=10**10, bytes_accessed=2 * 10**7, transcendentals=0),
        name="attention_backward",
    )(place, hidden, dcat, datt, part, dqc, *kept, *weights, *waits, *before)


def pack_kernel(place, acc_ref, small_ref, acc_a, acc_b, small_conv, kgrad, *rest):
    keep_ref, away_ref, rest_s, grad_ref, sems = rest[-5:]
    features, width = acc_a.shape
    taps = KERNEL * SLAB
    rest_s[...] = jnp.zeros_like(rest_s)
    rest_s[0:taps, 0 : width + LANES] = kgrad[0:taps, :]
    rest_s[taps : taps + 16, :] = small_conv[...]
    rest_s[taps + 16 : taps + 16 + SLAB, :] = small_ref[...]
    sources = [acc_ref.at[0], acc_ref.at[1], acc_ref.at[2], acc_a, acc_b]
    for source, start, block, at, size in tail_rows(width, features):
        slot = tail_slot(block, place)
        if start < width:
            left = sources[source][start : start + size, :]
            right = sources[source][width + start : width + start + size, :]
            grad_ref[slot, at : at + size, 0:width] = left.astype(BF)
            grad_ref[slot, at : at + size, width:] = right.astype(BF)
        else:
            start = start - width
            grad_ref[slot, at : at + size, :] = rest_s[start : start + size, :].astype(BF)
    send_halves(grad_ref, keep_ref, away_ref, sems)


def pack(place, sums, waits):
    features, width = sums[2].shape
    sent = jax.ShapeDtypeStruct((TAIL_BLOCKS // 2, tail_block(width), features), BF)
    anywhere = pl.BlockSpec(memory_space=pl.ANY)
    return pl.pallas_call(
        pack_kernel,
        out_shape=[sent, sent],
        grid_spec=pltpu.PrefetchScalarGridSpec(
            num_scalar_prefetch=1,
            grid=(1,),
            in_specs=[whole(a) for a in sums] + [anywhere] * len(waits),
            out_specs=[anywhere, anywhere],
            scratch_shapes=[
                pltpu.VMEM((TAIL_BLOCKS * tail_shared(width) - width, features), F32),
                pltpu.VMEM((TAIL_BLOCKS, tail_block(width), features), BF),
                pltpu.SemaphoreType.DMA((2,)),
            ],
        ),
        compiler_params=pltpu.CompilerParams(vmem_limit_bytes=VMEM_LIMIT),
        cost_estimate=pl.CostEstimate(flops=10**9, bytes_accessed=10**7, transcendentals=0),
        name="pack_gradients",
    )(place, *sums, *waits)


def merge(body, outs, ins, waits=(), steps=1):
    waited = len(waits)

    def kernel(*refs):
        body(refs[: len(ins)], refs[len(ins) + waited :])

    def spec(array):
        if steps == 1:
            return whole(array)
        axis = 1 if array.ndim == 4 else 0
        shape = list(array.shape)
        shape[axis] //= steps
        return pl.BlockSpec(
            tuple(shape), lambda i: tuple(i if d == axis else 0 for d in range(len(shape)))
        )

    outs = [jax.ShapeDtypeStruct(shape, BF) for shape in outs]
    return pl.pallas_call(
        kernel,
        out_shape=outs,
        grid=(steps,),
        in_specs=[spec(a) for a in ins] + [pl.BlockSpec(memory_space=pl.ANY)] * waited,
        out_specs=[spec(o) for o in outs],
        compiler_params=pltpu.CompilerParams(vmem_limit_bytes=VMEM_LIMIT),
        cost_estimate=pl.CostEstimate(flops=10**9, bytes_accessed=4 * 10**6, transcendentals=0),
        name="exchange_step",
    )(*ins, *waits)


def total(*values):
    result = values[0].astype(F32)
    for value in values[1:]:
        result = result + value.astype(F32)
    return result.astype(BF)


def sum_core(ins, outs):
    for part, out in enumerate(outs):
        out[...] = total(ins[0][part], ins[1][part])


def sum_first(ins, outs):
    keep_a, got_a, keep_b, got_b = ins
    half = outs[0].shape[0]
    for part in range(2):
        span = slice(part * half, (part + 1) * half)
        outs[part][...] = total(keep_a[span], got_a[span])
        outs[2 + part][...] = total(keep_b[span], got_b[span])


def sum_second(ins, outs):
    keep_a, got_a, keep_b, got_b = ins
    for part, out in enumerate(outs):
        out[0] = total(keep_a[part], got_a[part])
        out[1] = total(keep_b[part], got_b[part])


def sum_all(ins, outs):
    outs[0][...] = total(*[i[...] for i in ins])


def sum_parts(ins, outs):
    for part, out in enumerate(outs):
        span = slice(part * out.shape[0], (part + 1) * out.shape[0])
        out[...] = total(*[i[span] for i in ins])


def first_of(value):
    corner = lax.slice(value, (0,) * value.ndim, (1,) * value.ndim)
    return jnp.clip(corner.astype(F32).reshape(()), 0.0, 0.0)


def late(value, zero):
    return (value.astype(F32) + zero).astype(BF)


def across(value, links):
    if links.size <= 16:
        return value
    groups = [[low + 16 * high for high in range(links.size // 16)] for low in range(16)]
    return lax.psum(value, "dp", axis_index_groups=groups)


def join(*values):
    return jnp.concatenate(values, axis=0)


class Links:
    def __init__(self, size):
        self.size = size
        self.core = ("dp", self.flip(1))
        self.x = ("dp", self.flip(2))
        self.y = ("branch", [(0, 1), (1, 0)])
        self.corner = (
            ("branch", "dp"),
            [(b * size + i, (1 - b) * size + (i ^ 2)) for b in range(2) for i in range(size)],
        )
        self.z = [("dp", self.flip(4 * d)) for d in range(1, 4)]

    def flip(self, bits):
        return [(i, i ^ bits) for i in range(self.size)]


def cut(value, parts):
    return value.reshape(parts, -1, *value.shape[1:])


def send(pairs):
    return [lax.ppermute(value, *hop) for value, hop in pairs]


def plane(links):
    return [links.y, links.x, links.corner]


def load_pieces(pieces, buffer, sems):
    size = pieces[0].shape[0]
    copies = [
        pltpu.make_async_copy(piece, buffer.at[i * size : (i + 1) * size], sems.at[i])
        for i, piece in enumerate(pieces)
    ]
    for copy in copies:
        copy.start()
    for copy in copies:
        copy.wait()


def spread_middle_kernel(place, *rest):
    pieces, outs = rest[:8], rest[8:]
    inner_ref, outer_ref, mixer_ref, ib_ref, *vector_refs = outs[:-4]
    turn_s, rest_ref, grad_ref, sems = outs[-4:]
    load_pieces(pieces, grad_ref, sems)
    groups, width, inner = inner_ref.shape
    block = grad_ref.shape[1]
    features = mixer_ref.shape[1]
    targets = [inner_ref.at[0], inner_ref.at[1], turn_s.at[0], turn_s.at[1]]
    for part in range(MID_BLOCKS):
        start = part * block
        value = grad_ref[mid_slot(part, place)].astype(F32)
        if start < 2 * groups * width:
            target = targets[start // width]
            start = start % width
            target[start : start + block, :] = value
        elif start < 5 * width:
            start = start - 2 * groups * width
            mixer_ref[start : start + block, :] = value[:, :features]
            mixer_ref[width + start : width + start + block, :] = value[:, features:]
        else:
            start = start - 5 * width
            rest_ref[start : start + block, :] = value
    for g in range(groups):
        outer_ref[g] = turn_s[g].T
    ib_ref[...] = jnp.concatenate([rest_ref[0:1, :], rest_ref[1:2, :]], axis=1).reshape(-1)
    for number, ref in enumerate(vector_refs):
        row, col = 2 + number // 2, number % 2 * features
        ref[...] = rest_ref[row : row + 1, col : col + features].reshape(-1)


def spread_middle(place, pieces, width, inner, features):
    block = pieces[0].shape[1]
    outs = [
        jax.ShapeDtypeStruct((2, width, inner), F32),
        jax.ShapeDtypeStruct((2, inner, width), F32),
        jax.ShapeDtypeStruct((features, features), F32),
        jax.ShapeDtypeStruct((2 * inner,), F32),
        *[jax.ShapeDtypeStruct((features,), F32)] * 6,
    ]
    return pl.pallas_call(
        spread_middle_kernel,
        out_shape=outs,
        grid_spec=pltpu.PrefetchScalarGridSpec(
            num_scalar_prefetch=1,
            grid=(1,),
            in_specs=[pl.BlockSpec(memory_space=pl.ANY)] * len(pieces),
            out_specs=[whole(o) for o in outs],
            scratch_shapes=[
                pltpu.VMEM((2, width, inner), F32),
                pltpu.VMEM((MID_BLOCKS * block - 5 * width, inner), F32),
                pltpu.VMEM((MID_BLOCKS, block, inner), BF),
                pltpu.SemaphoreType.DMA((len(pieces),)),
            ],
        ),
        compiler_params=pltpu.CompilerParams(vmem_limit_bytes=VMEM_LIMIT),
        cost_estimate=pl.CostEstimate(flops=3 * 10**9, bytes_accessed=2 * 10**7, transcendentals=0),
        name="shared_gradients",
    )(place, *pieces)


def spread_branch_kernel(place, order_ref, turned_ref, *rest):
    pieces, outs = rest[:8], rest[9:]
    query_ref, keys_ref, values_ref, qb_ref, vb_ref, depth_ref, pb_ref, kw_ref, kb_ref = outs[:9]
    grad_ref, rest_s, sems = outs[9:]
    width = query_ref.shape[1]
    size = pieces[0].shape[0]
    shared = tail_shared(width)
    owned = grad_ref.shape[1] - shared
    copies = []
    for number, piece in enumerate(pieces):
        core, x, y = number // 4, number % 2, number // 2 % 2
        start = core << 4 | x << 3 | y << 2
        target = grad_ref.at[start : start + size]
        if y:
            target = grad_ref.at[start : start + size, owned:, :]
        copies.append(pltpu.make_async_copy(piece, target, sems.at[number]))
    for copy in copies:
        copy.start()
    for copy in copies:
        copy.wait()
    for within in range(4 * width // owned // 2):
        block = (within >> 2) << 3 | within & 3
        value = grad_ref[block ^ (place[MASK_T] & ~4), 0:owned, :].astype(F32)
        start = within * owned
        target = keys_ref if start < width else values_ref
        start = start % width
        target[0, start : start + owned, :] = value[:, :width]
        target[0, width + start : width + start + owned, :] = value[:, width:]
    for block in range(TAIL_BLOCKS):
        value = grad_ref[tail_slot(block, place), owned:, :].astype(F32)
        start = block * shared
        if start < width:
            query_ref[start : start + shared, :] = value[:, :width]
            query_ref[width + start : width + start + shared, :] = value[:, width:]
        else:
            rest_s[start - width : start - width + shared, :] = value
    taps = KERNEL * SLAB
    depth_ref[...] = rest_s[taps : taps + KERNEL, :]
    conv_line = rest_s[taps + KERNEL : taps + KERNEL + 1, :]
    att_line = rest_s[taps + 16 : taps + 17, :]
    qb_ref[...] = att_line[:, :width].reshape(-1)
    pb_ref[...] = conv_line[:, :width].reshape(-1)
    vb_ref[...] = jnp.where(place[SIDE] == 0, att_line[:, width:], conv_line[:, width:])
    kw_ref[...] = mm(turned_ref[...], rest_s[:, 0:width].astype(BF))
    taps_bias = mm(rest_s[:, width : width + LANES].T.astype(BF), order_ref[...])[0:1]
    kb_ref[...] = taps_bias.reshape(-1)


def spread_branch(place, ordered, pieces, width, features, wait):
    block = pieces[0].shape[1]
    outs = [
        jax.ShapeDtypeStruct((features, width), F32),
        jax.ShapeDtypeStruct((1, features, width), F32),
        jax.ShapeDtypeStruct((1, features, width), F32),
        jax.ShapeDtypeStruct((width,), F32),
        jax.ShapeDtypeStruct((1, width), F32),
        jax.ShapeDtypeStruct((KERNEL, features), F32),
        jax.ShapeDtypeStruct((width,), F32),
        jax.ShapeDtypeStruct((HEADS * KERNEL, width), F32),
        jax.ShapeDtypeStruct((HEADS * KERNEL,), F32),
    ]
    return pl.pallas_call(
        spread_branch_kernel,
        out_shape=outs,
        grid_spec=pltpu.PrefetchScalarGridSpec(
            num_scalar_prefetch=1,
            grid=(1,),
            in_specs=[whole(o) for o in ordered]
            + [pl.BlockSpec(memory_space=pl.ANY)] * (len(pieces) + 1),
            out_specs=[whole(o) for o in outs],
            scratch_shapes=[
                pltpu.VMEM((TAIL_BLOCKS, block, features), BF),
                pltpu.VMEM((TAIL_BLOCKS * tail_shared(width) - width, features), F32),
                pltpu.SemaphoreType.DMA((len(pieces),)),
            ],
        ),
        compiler_params=pltpu.CompilerParams(vmem_limit_bytes=VMEM_LIMIT),
        cost_estimate=pl.CostEstimate(flops=2 * 10**9, bytes_accessed=2 * 10**7, transcendentals=0),
        name="branch_gradients",
    )(place, *ordered, *pieces, wait)


def after(values, *others):
    return lax.optimization_barrier((tuple(values), others))[0]


def shards(
    size,
    hidden,
    bounds,
    query_weight,
    query_bias,
    branch_keys,
    branch_values,
    branch_bias,
    depth_kernel,
    point_bias,
    kernel_weight,
    kernel_bias,
    mixer_weight,
    mixer_bias,
    first_gain,
    first_shift,
    inner_weight,
    inner_bias,
    outer_weight,
    outer_bias,
    second_gain,
    second_shift,
    cotangent,
):
    links = Links(size)
    side = lax.axis_index("branch")
    index = lax.axis_index("dp")
    core, x, z = index & 1, (index >> 1) & 1, (index >> 2) & 3
    rows = hidden.shape[0] // 2
    features = hidden.shape[2]
    width = query_weight.shape[1]
    inner = inner_weight.shape[2]
    place = jnp.stack(
        [
            side * rows,
            side,
            core,
            core << 5 | x << 3 | side << 2 | z,
            core << 5 | side << 3 | x << 2 | z,
            core << 4 | x << 3 | side << 2 | z,
        ]
    ).astype(jnp.int32)

    def exchange(value):
        return lax.ppermute(value, *links.y)

    got = exchange(jnp.where(core == 0, branch_keys[0], branch_values[0]))
    got_bias = exchange(branch_bias)
    own_weights = (branch_keys[0], branch_values[0])
    far = ((1 - side) * rows).astype(jnp.int32)
    spread, ordered = spread_table(), order_table()
    flat_kernel = kernel_weight.T
    common = (depth_kernel, query_bias, point_bias, kernel_bias, flat_kernel, ordered, spread)
    bounds = bounds.T
    kept = forward(
        0, place, bounds, hidden, (query_weight, *own_weights, branch_bias, *common), rows
    )
    got, got_bias, cotangent = after((got, got_bias, cotangent), kept[0])
    got_weights = (got, lax.ppermute(got, *links.core))
    cot_got = exchange(lax.dynamic_slice_in_dim(cotangent, far, rows, 0))
    kept = forward(
        1, place, bounds, hidden, (query_weight, *got_weights, got_bias, *common), rows, kept
    )
    cat, q, k, v, probs, att_t, dm, kc, cq, joint, taps, vc = kept
    (cot_got,) = after([cot_got], cat)
    out_own, out_send, dcat, datt, dmix, mid_keep, mid_away = middle(
        place,
        hidden,
        cat,
        cotangent,
        cot_got,
        (
            mixer_weight,
            inner_weight,
            outer_weight,
            mixer_bias,
            first_gain,
            first_shift,
            inner_bias,
            outer_bias,
            second_gain,
            second_shift,
        ),
        rows,
    )
    conv_weights = (
        *own_weights, *got_weights, depth_kernel, flat_kernel, ordered, spread, gather_table()
    )
    att_weights = (query_weight, *own_weights, *got_weights)
    conv_kept = (dm, kc, cq, joint, taps, vc)
    att_kept = (q, k, v, probs, att_t)

    block = mid_keep.shape[1:]
    mid_keep, mid_away = cut(mid_keep, 4), cut(mid_away, 4)
    (mid_got,) = send([(mid_away, links.core)])
    conv0 = conv_back(place, 0, hidden, dcat, dmix, conv_kept, conv_weights, (), ())
    keep_a, away_a, keep_b, away_b = merge(
        sum_core, [(8, *block)] * 4, (mid_keep, mid_got), (), 4
    )
    got_a, got_b, out_got = send([(away_a, links.x), (away_b, links.y), (out_send, links.y)])
    conv1 = conv_back(
        place, 1, hidden, dcat, dmix, conv_kept, conv_weights, tuple(conv0[2:]), (keep_a,)
    )
    keep_a, away_a, keep_b, away_b = merge(
        sum_first, [(4, *block)] * 4, (keep_a, got_a, keep_b, got_b)
    )
    got_a, got_b = send([(away_a, links.y), (away_b, links.x)])
    att0 = att_back(
        place, 0, hidden, dcat, datt, conv0[0], conv0[1], att_kept, att_weights, (), (keep_a,)
    )
    mid, *away = merge(
        sum_second, [(2, *block)] * 4, (keep_a, got_a, keep_b, got_b)
    )
    got_z = send(zip(away, links.z))
    (hid_got0,) = send([(att0[1], links.y)])
    att1 = att_back(
        place,
        1,
        hidden,
        dcat,
        datt,
        conv1[0],
        conv1[1],
        att_kept,
        att_weights,
        tuple(att0[2:]),
        (mid, out_got),
    )
    tail_rows_each = tail_block(width)
    mid = across(total(mid, *got_z), links)
    tail_keep, tail_away = pack(place, (*att1[2:], *conv1[2:]), (mid, hid_got0))
    tail_got = send([(tail_away, links.core)])
    piece = (tail_rows_each, features)
    got_mid = send([(mid, hop) for hop in links.z])
    tail = cut(total(tail_keep, *tail_got), 4)
    got_tail = send(zip(tail[1:], plane(links)))
    tail = cut(total(tail[0], *got_tail), 4)
    got_tail = send(zip(tail[1:], links.z))
    zero = first_of(tail)
    pieces = [mid] + [late(got, zero) for got in got_mid]
    mid_a, mid_b = (join(*[m[order : order + 1] for m in pieces]) for order in range(2))
    got_a, got_b = send([(mid_a, links.y), (mid_b, links.x)])
    tail = across(total(tail[0], *got_tail), links)
    zero = first_of(tail)
    mid_a, mid_b = join(mid_a, late(got_a, zero)), join(mid_b, late(got_b, zero))
    got_a, got_b = send([(mid_a, links.x), (mid_b, links.y)])
    tail = late(tail, first_of(mid_a) + first_of(mid_b))
    got_tail = send([(tail, hop) for hop in links.z])
    mid = (mid_a, got_a, mid_b, got_b)
    tail = join(tail, *got_tail)
    zero = first_of(tail)
    far_mid = send([(late(m, zero), links.core) for m in mid])
    mid = (*mid, *far_mid)
    zero = first_of(far_mid[0])
    tail = late(tail, zero)
    shared = tail[:, tail.shape[1] - tail_shared(width) :]
    got_tail = send([(tail, links.x), (shared, links.y), (shared, links.corner)])
    (hid_got1,) = send([(late(att1[1], first_of(got_tail[0])), links.y)])
    tail = (tail, *got_tail)
    tail = (*tail, *send([(t, links.core) for t in tail]))
    grad_inner, grad_outer, grad_mixer, inner_line, *mid_lines = spread_middle(
        place, mid, width, inner, features
    )
    mixer_line, gain1_line, shift1_line, outer_line, gain2_line, shift2_line = mid_lines
    (
        query_grad,
        keys,
        values,
        query_line,
        value_line,
        depth,
        point_line,
        kernel_grad,
        kernel_line,
    ) = spread_branch(
        place, (ordered, jnp.asarray(ordered.T)), tail, width, features, mixer_line
    )
    def combine(own, got):
        return jnp.where(side == 0, join(own, got), join(got, own))

    output = combine(out_own, out_got)
    hidden_grad = combine(join(att0[0], att1[0]), join(hid_got0, hid_got1).astype(F32))
    return (
        output,
        hidden_grad,
        query_grad,
        query_line,
        keys,
        values,
        value_line,
        depth,
        point_line,
        kernel_grad.T,
        kernel_line,
        grad_mixer,
        mixer_line,
        gain1_line,
        shift1_line,
        grad_inner,
        inner_line,
        grad_outer,
        outer_line,
        gain2_line,
        shift2_line,
    )


def solution(mesh):
    split = P("dp", "branch", None)
    owned = P("branch", None, None)
    return jax.shard_map(
        functools.partial(shards, mesh.shape["dp"]),
        mesh=mesh,
        in_specs=(
            P("dp", None, None),
            P("dp", None),
            P(),
            P(),
            owned,
            owned,
            P("branch", None),
            *([P()] * 14),
            split,
        ),
        out_specs=(
            split,
            split,
            P(),
            P(),
            owned,
            owned,
            P("branch", None),
            *([P()] * 14),
        ),
        check_vma=False,
    )
```

```python
import functools

import jax
import jax.numpy as jnp
import numpy as np
from jax import lax
from jax.experimental import pallas as pl
from jax.experimental.pallas import tpu as pltpu
from jax.sharding import PartitionSpec as P

HEADS = 6
HEAD_SIZE = 64
KERNEL = 9
RADIUS = KERNEL // 2
SLAB = 8
LANES = 128
PAD = 8

NEGATIVE = -1000000000.0
EPSILON = 1e-05
INV_ROOT_TAU = 0.3989422804014327
ROOT_HALF = 0.7071067811865476
MID_BLOCKS = 64
TAIL_BLOCKS = 32
ORDER_BIT = 16
BASE, SIDE, CORE, MASK_A, MASK_B, MASK_T = range(6)

BF = jnp.bfloat16
F32 = jnp.float32
VMEM_LIMIT = 62 * 1024 * 1024


def mm(left, right):
    return jnp.dot(left, right, preferred_element_type=F32)


def mm_nt(left, right):
    return lax.dot_general(left, right, (((1,), (1,)), ((), ())), preferred_element_type=F32)


def block_rows(rows, blocks):
    return -(-rows // (16 * blocks)) * 16


def mid_slot(block, place):
    return block ^ (place[MASK_B] if block & ORDER_BIT else place[MASK_A])


def tail_block(width):
    return 4 * width // TAIL_BLOCKS + tail_shared(width)


def tail_shared(width):
    return -(-(width + LANES) // (16 * TAIL_BLOCKS)) * 16


def tail_rows(width, features):
    owned = 4 * width // TAIL_BLOCKS
    shared = tail_shared(width)
    spots = []
    for block in range(TAIL_BLOCKS):
        branch = block >> 2 & 1
        within = (block >> 3) * 4 + (block & 3)
        start = within * owned
        spots.append((1 + 2 * branch + start // width, start % width, block, 0, owned))
        spots.append((0, block * shared, block, owned, shared))
    return spots


def tail_slot(block, place):
    return block ^ place[MASK_T]


def send_halves(buffer, keep, away, sems):
    half = keep.shape[0]
    copies = [
        pltpu.make_async_copy(buffer.at[half : 2 * half], away, sems.at[1]),
        pltpu.make_async_copy(buffer.at[0:half], keep, sems.at[0]),
    ]
    for copy in copies:
        copy.start()
    for copy in copies:
        copy.wait()


def start_copies(pairs, sems):
    copies = [pltpu.make_async_copy(a, b, sems.at[i]) for i, (a, b) in enumerate(pairs)]
    for copy in copies:
        copy.start()
    return copies


def pick_weights(place, branch, weights):
    own_keys, own_values, first, second = (weights[i] for i in range(4))
    mine, even = place[SIDE] == branch, place[CORE] == 0
    return (
        jnp.where(mine, own_keys, jnp.where(even, first, second)),
        jnp.where(mine, own_values, jnp.where(even, second, first)),
    )


def rowsum(value):
    return jnp.sum(value, axis=0, keepdims=True)


def fill_strips(strips_ref, value, length):
    strips = strips_ref.shape[0]
    zero = jnp.zeros((PAD, LANES), F32)
    for strip in range(strips):
        strips_ref[strip, 0:PAD, :] = zero
        strips_ref[strip, PAD + length : 2 * PAD + length, :] = zero
        strips_ref[strip, PAD : PAD + length, :] = value[
            :, strip * LANES : (strip + 1) * LANES
        ].astype(F32)


def head_pair_rows(rows, head):
    own = rows[head * HEAD_SIZE : (head + 1) * HEAD_SIZE, :]
    zero = jnp.zeros_like(own)
    return jnp.concatenate([own, zero] if head % 2 == 0 else [zero, own], axis=0)


def line(ref):
    return ref[...].reshape(1, -1)


def tapped_weights(order_ref, kw_ref):
    return mm(order_ref[...], kw_ref[...]).astype(BF)


def forward_kernel(
    order,
    place,
    bounds,
    x_ref,
    wq_ref,
    wa_ref,
    wb_ref,
    bb_ref,
    depth_ref,
    qb_ref,
    pb_ref,
    kb_ref,
    kw_ref,
    order_ref,
    spread_ref,
    *rest,
):
    (
        cat_ref,
        q_ref,
        k_ref,
        v_ref,
        probs_ref,
        att_t_ref,
        dm_ref,
        kc_ref,
        cq_ref,
        joint_ref,
        taps_ref,
        vc_ref,
        qt_s,
        vt_s,
        xs_s,
        vs_s,
        tw_s,
        wide_s,
    ) = rest[-18:]
    row = place[BASE] + pl.program_id(0)
    width = HEADS * HEAD_SIZE
    wa, wb = wa_ref[...], wb_ref[...]
    if order:
        even = place[CORE] == 0
        wa, wb = jnp.where(even, wa, wb), jnp.where(even, wb, wa)
    first_end = bounds[0, row]
    valid = bounds[1, row]
    length = x_ref.shape[1]
    x = x_ref[0]
    queries = (mm(x, wq_ref[...]) + line(qb_ref)).astype(BF)

    @pl.when(place[SIDE] == order)
    def _():
        scaled = (queries.astype(F32) * (HEAD_SIZE**-0.5)).astype(BF)
        q_ref[0] = scaled
        qt_s[...] = scaled.T
        k_ref[0] = mm(x, wa).astype(BF)
        v = (mm(x, wb) + bb_ref[...]).astype(BF)
        v_ref[0] = v
        vt_s[...] = v.T
        seen = lax.broadcasted_iota(jnp.int32, (length, 1), 0) < valid
        for head in range(HEADS):
            pair = head // 2
            keys = k_ref[0, :, pair * LANES : (pair + 1) * LANES]
            scores = mm(keys, head_pair_rows(qt_s, head))
            scores = jnp.where(seen, scores, NEGATIVE)
            raised = jnp.exp(scores - jnp.max(scores, axis=0, keepdims=True))
            probs = (raised * (1.0 / rowsum(raised))).astype(BF)
            probs_ref[0, head] = probs
            span = slice(head * HEAD_SIZE, (head + 1) * HEAD_SIZE)
            att_t_ref[0, span, :] = mm(vt_s[span, :], probs).astype(BF)
        cat_ref[0] = att_t_ref[0].T

    @pl.when(place[SIDE] != order)
    def _():
        fill_strips(xs_s, x, length)
        piece = LANES
        for strip in range(xs_s.shape[0]):
            lanes = slice(strip * LANES, (strip + 1) * LANES)
            for at in range(0, length, piece):
                total = None
                for tap in range(KERNEL):
                    begin = PAD - RADIUS + tap + at
                    term = xs_s[strip, begin : begin + piece, :] * depth_ref[tap : tap + 1, lanes]
                    total = term if total is None else total + term
                dm_ref[0, at : at + piece, lanes] = total.astype(BF)
        key_conv = mm(dm_ref[0], wa) + line(pb_ref)
        kc_ref[0] = key_conv
        cq_ref[0] = queries
        joint = (key_conv * queries.astype(F32)).astype(BF)
        joint_ref[0] = joint
        tap_bias = jnp.sum(order_ref[...].astype(F32) * line(kb_ref), axis=1, keepdims=True)
        logits = mm_nt(tapped_weights(order_ref, kw_ref), joint) + tap_bias
        here = lax.broadcasted_iota(jnp.int32, (SLAB, length), 1)

        def segment(position):
            return jnp.where(position <= first_end, 0, jnp.where(position < valid, 1, 2))

        own_segment = segment(here)
        slabs = []
        for tap in range(KERNEL):
            other = here + (tap - RADIUS)
            same = (other >= 0) & (other < length) & (segment(other) == own_segment)
            slabs.append(jnp.where(same, logits[tap * SLAB : (tap + 1) * SLAB], NEGATIVE))
        peak = functools.reduce(jnp.maximum, slabs)
        slabs = [jnp.exp(slab - peak) for slab in slabs]
        inverse = 1.0 / functools.reduce(jnp.add, slabs)
        for tap in range(KERNEL):
            tw_s[tap * SLAB : (tap + 1) * SLAB, :] = slabs[tap] * inverse
        tw_s[KERNEL * SLAB :, :] = jnp.zeros((LANES - KERNEL * SLAB, length), F32)
        taps_ref[0] = tw_s[...]
        taps = tw_s[...].T
        high = taps.astype(BF)
        low = (taps - high.astype(F32)).astype(BF)
        both = jnp.concatenate([high, low], axis=1)
        for tap in range(KERNEL):
            cols = slice(tap * width, (tap + 1) * width)
            wide_s[:, cols] = mm(both, spread_ref[:, cols])
        vc = (mm(x, wb) + bb_ref[...]).astype(BF)
        vc_ref[0] = vc
        fill_strips(vs_s, vc, length)
        for strip in range(vs_s.shape[0]):
            for at in range(0, length, piece):
                total = None
                for tap in range(KERNEL):
                    begin = PAD - RADIUS + tap + at
                    col = tap * width + strip * LANES
                    term = (
                        vs_s[strip, begin : begin + piece, :]
                        * wide_s[at : at + piece, col : col + LANES]
                    )
                    total = term if total is None else total + term
                cat_ref[0, at : at + piece, strip * LANES : (strip + 1) * LANES] = total.astype(BF)


def spread_table():
    table = np.zeros((2 * LANES, KERNEL, HEADS, HEAD_SIZE), np.float32)
    for tap in range(KERNEL):
        for head in range(HEADS):
            table[tap * SLAB + head, tap, head, :] = 1
            table[LANES + tap * SLAB + head, tap, head, :] = 1
    return jnp.asarray(table.reshape(2 * LANES, -1), BF)


def gather_table():
    table = np.zeros((KERNEL, HEADS, HEAD_SIZE, LANES), np.float32)
    for tap in range(KERNEL):
        for head in range(HEADS):
            table[tap, head, :, tap * SLAB + head] = 1
    return jnp.asarray(table.reshape(-1, LANES), BF)


def order_table():
    table = np.zeros((LANES, HEADS * KERNEL), np.float32)
    for tap in range(KERNEL):
        for head in range(HEADS):
            table[tap * SLAB + head, head * KERNEL + tap] = 1
    return jnp.asarray(table, BF)


def whole(array, buffers=2):
    rank = len(array.shape)
    mode = pl.Buffered(buffers) if buffers < 2 else None
    return pl.BlockSpec(array.shape, lambda *_: (0,) * rank, pipeline_mode=mode)


def forward(order, place, bounds, hidden, weights, rows, before=None):
    length, features = hidden.shape[1:]
    width = HEADS * HEAD_SIZE
    spare = rows

    def att_row(r, place, bounds):
        return jnp.where(place[SIDE] == order, r, spare)

    def conv_row(r, place, bounds):
        return jnp.where(place[SIDE] != order, r, spare)

    def saved(row_of, shape, dtype):
        zeros = (0,) * len(shape)
        return (
            jax.ShapeDtypeStruct((rows + 1,) + shape, dtype),
            pl.BlockSpec((1,) + shape, lambda r, p, b: (row_of(r, p, b),) + zeros),
        )

    outs = [
        (
            jax.ShapeDtypeStruct((rows, length, 2 * width), BF),
            pl.BlockSpec((1, length, width), lambda r, p, b: (r, 0, jnp.where(p[SIDE] == order, 0, 1))),
        ),
        saved(att_row, (length, width), BF),
        saved(att_row, (length, width), BF),
        saved(att_row, (length, width), BF),
        saved(att_row, (HEADS, length, length), BF),
        saved(att_row, (width, length), BF),
        saved(conv_row, (length, features), BF),
        saved(conv_row, (length, width), F32),
        saved(conv_row, (length, width), BF),
        saved(conv_row, (length, width), BF),
        saved(conv_row, (LANES, length), F32),
        saved(conv_row, (length, width), BF),
    ]
    in_specs = [pl.BlockSpec((1, length, features), lambda r, p, b: (p[0] + r, 0, 0))]
    in_specs += [whole(w) for w in weights]
    args = [place, bounds, hidden, *weights]
    aliases = {}
    if before is not None:
        aliases = {len(args) + i: i for i in range(len(before))}
        in_specs += [pl.BlockSpec(memory_space=pl.ANY)] * len(before)
        args += list(before)
    return pl.pallas_call(
        functools.partial(forward_kernel, order),
        out_shape=[o[0] for o in outs],
        grid_spec=pltpu.PrefetchScalarGridSpec(
            num_scalar_prefetch=2,
            grid=(rows,),
            in_specs=in_specs,
            out_specs=[o[1] for o in outs],
            scratch_shapes=[
                pltpu.VMEM((width, length), BF),
                pltpu.VMEM((width, length), BF),
                pltpu.VMEM((features // LANES, length + 2 * PAD, LANES), F32),
                pltpu.VMEM((width // LANES, length + 2 * PAD, LANES), F32),
                pltpu.VMEM((LANES, length), F32),
                pltpu.VMEM((length, KERNEL * width), F32),
            ],
        ),
        input_output_aliases=aliases,
        compiler_params=pltpu.CompilerParams(vmem_limit_bytes=VMEM_LIMIT),
        cost_estimate=pl.CostEstimate(flops=10**10, bytes_accessed=2 * 10**7, transcendentals=0),
        name="branch_forward",
    )(*args)


def norm(value):
    center = value - jnp.mean(value, axis=-1, keepdims=True)
    factor = lax.rsqrt(jnp.mean(center * center, axis=-1, keepdims=True) + EPSILON)
    return center * factor, factor


def norm_back(gradient, normed, factor):
    return factor * (
        gradient
        - jnp.mean(gradient, axis=-1, keepdims=True)
        - normed * jnp.mean(gradient * normed, axis=-1, keepdims=True)
    )


def middle_kernel(
    place,
    x_ref,
    cat_ref,
    cot_own_ref,
    cot_got_ref,
    mw_ref,
    iw_any,
    ow_any,
    mixer_bias,
    gain1,
    shift1,
    inner_bias,
    outer_bias,
    gain2,
    shift2,
    own_ref,
    send_ref,
    dcat_ref,
    datt_ref,
    dmix_ref,
    keep_ref,
    away_ref,
    grad_ref,
    sems,
    iw_ref,
    ow_ref,
    weight_sems,
    vec_s,
    rest_s,
    acc_i,
    acc_o,
    acc_m,
    act_s,
    slope_s,
    din_s,
):
    step = pl.program_id(0)
    first_side = place[SIDE] == 0
    features = x_ref.shape[2]
    half = x_ref.shape[1] // 2
    groups, width, inner = iw_ref.shape
    piece = 512

    mixer_bias, gain1, shift1, inner_bias, outer_bias, gain2, shift2 = (
        line(r) for r in (mixer_bias, gain1, shift1, inner_bias, outer_bias, gain2, shift2)
    )

    @pl.when(step == 0)
    def _():
        start_copies([(iw_any, iw_ref), (ow_any, ow_ref)], weight_sems)
        acc_i[...] = jnp.zeros_like(acc_i)
        acc_o[...] = jnp.zeros_like(acc_o)
        acc_m[...] = jnp.zeros_like(acc_m)
        vec_s[...] = jnp.zeros_like(vec_s)

    cat = cat_ref[0]
    normed1, factor1 = norm(x_ref[0].astype(F32) + (mm(cat, mw_ref[...]) + mixer_bias))
    first = (normed1 * gain1 + shift1).astype(BF)
    @pl.when(step == 0)
    def _():
        pltpu.make_async_copy(iw_any, iw_ref, weight_sems.at[0]).wait()
        pltpu.make_async_copy(ow_any, ow_ref, weight_sems.at[1]).wait()

    projected = []
    for g in range(groups):
        part = first[:, g * width : (g + 1) * width]
        for at in range(0, inner, piece):
            lanes = slice(g * inner + at, g * inner + at + piece)
            pre = mm(part, iw_ref[g, :, at : at + piece]) + inner_bias[:, lanes]
            phi = 0.5 + 0.5 * lax.erf(pre * ROOT_HALF)
            bell = jnp.exp(-0.5 * pre * pre) * INV_ROOT_TAU
            act_s[:, lanes] = (pre * phi).astype(BF)
            slope_s[:, lanes] = phi + pre * bell
        projected.append(mm(act_s[:, g * inner : (g + 1) * inner], ow_ref[g]))
    projected = jnp.concatenate(projected, axis=1)
    normed2, factor2 = norm(first.astype(F32) + (projected + outer_bias))
    output = normed2 * gain2 + shift2
    own_ref[0] = jnp.where(first_side, output[:half], output[half:]).astype(BF)
    send_ref[0] = jnp.where(first_side, output[half:], output[:half]).astype(BF)
    cot_own, cot_got = cot_own_ref[0].astype(F32), cot_got_ref[0].astype(F32)
    cot = jnp.concatenate(
        [jnp.where(first_side, cot_own, cot_got), jnp.where(first_side, cot_got, cot_own)], axis=0
    )
    dsecond = norm_back(cot * gain2, normed2, factor2)
    dproj = dsecond.astype(BF)
    vec_s[1:2, 3 * features : 4 * features] += rowsum(dproj.astype(F32))
    vec_s[2:3, 0:features] += rowsum(cot * normed2)
    vec_s[2:3, features : 2 * features] += rowsum(cot)
    dfirst = []
    for g in range(groups):
        cols = slice(g * width, (g + 1) * width)
        dpart = dproj[:, cols]
        for at in range(0, inner, piece):
            lanes = slice(g * inner + at, g * inner + at + piece)
            dact = mm_nt(dpart, ow_ref[g, at : at + piece, :]).astype(BF)
            din = (dact.astype(F32) * slope_s[:, lanes]).astype(BF)
            din_s[:, lanes] = din
            vec_s[0:1, lanes] += rowsum(din.astype(F32))
        group = slice(g * inner, (g + 1) * inner)
        acc_o[g] += mm(dpart.T, act_s[:, group])
        acc_i[g] += mm(first[:, cols].T, din_s[:, group])
        dfirst.append(dsecond[:, cols] + mm_nt(din_s[:, group], iw_ref[g]))
    dfirst = jnp.concatenate(dfirst, axis=1)
    vec_s[1:2, features : 2 * features] += rowsum(dfirst * normed1)
    vec_s[1:2, 2 * features : 3 * features] += rowsum(dfirst)
    dmixed = norm_back(dfirst * gain1, normed1, factor1)
    dmix_ref[0] = dmixed
    dmixer = dmixed.astype(BF)
    vec_s[1:2, 0:features] += rowsum(dmixer.astype(F32))
    acc_m[...] += mm(cat.T, dmixer)
    dcat_ref[0] = mm_nt(dmixer, mw_ref[...]).astype(BF)
    datt_ref[0] = mm_nt(mw_ref[0:width, :], dmixer).astype(BF)

    @pl.when(step == pl.num_programs(0) - 1)
    def _():
        rest_s[0:1, :] = vec_s[0:1, 0:inner]
        rest_s[1:2, :] = vec_s[0:1, inner:]
        rest_s[2:3, :] = vec_s[1:2, 0:inner]
        rest_s[3:4, :] = vec_s[1:2, inner:]
        rest_s[4:5, :] = vec_s[2:3, 0:inner]
        rest_s[5:, :] = jnp.zeros((rest_s.shape[0] - 5, inner), F32)
        block = grad_ref.shape[1]
        sources = [acc_i.at[0], acc_i.at[1], acc_o.at[0], acc_o.at[1]]
        for part in range(MID_BLOCKS):
            start = part * block
            slot = mid_slot(part, place)
            if start < 2 * groups * width:
                source = sources[start // width]
                start = start % width
                grad_ref[slot] = source[start : start + block, :].astype(BF)
            elif start < 5 * width:
                start = start - 2 * groups * width
                grad_ref[slot, :, 0:features] = acc_m[start : start + block, :].astype(BF)
                start = start + width
                grad_ref[slot, :, features:] = acc_m[start : start + block, :].astype(BF)
            else:
                start = start - 5 * width
                grad_ref[slot] = rest_s[start : start + block, :].astype(BF)
        send_halves(grad_ref, keep_ref, away_ref, sems)


def middle(place, hidden, cat, cot_own, cot_got, weights, rows):
    length, features = hidden.shape[1:]
    half = length // 2
    groups, width, inner = weights[1].shape
    block = block_rows(5 * width, MID_BLOCKS)
    sent = jax.ShapeDtypeStruct((MID_BLOCKS // 2, block, inner), BF)

    def per_row(*shape, dtype=BF):
        return (
            jax.ShapeDtypeStruct((rows,) + shape, dtype),
            pl.BlockSpec((1,) + shape, lambda s, p: (s, 0, 0)),
        )

    outs = [
        per_row(half, features),
        per_row(half, features),
        per_row(length, features),
        per_row(width, length),
        per_row(length, features, dtype=F32),
        (sent, pl.BlockSpec(memory_space=pl.ANY)),
        (sent, pl.BlockSpec(memory_space=pl.ANY)),
    ]
    return pl.pallas_call(
        middle_kernel,
        out_shape=[o[0] for o in outs],
        grid_spec=pltpu.PrefetchScalarGridSpec(
            num_scalar_prefetch=1,
            grid=(rows,),
            in_specs=[
                pl.BlockSpec((1, length, features), lambda s, p: (p[0] + s, 0, 0)),
                pl.BlockSpec((1, length, features), lambda s, p: (s, 0, 0)),
                pl.BlockSpec((1, half, features), lambda s, p: (p[0] + s, 0, 0)),
                pl.BlockSpec((1, half, features), lambda s, p: (s, 0, 0)),
                whole(weights[0], 1),
                *[pl.BlockSpec(memory_space=pl.ANY)] * 2,
                *[whole(w, 1) for w in weights[3:]],
            ],
            out_specs=[o[1] for o in outs],
            scratch_shapes=[
                pltpu.VMEM((MID_BLOCKS, block, inner), BF),
                pltpu.SemaphoreType.DMA((2,)),
                pltpu.VMEM((groups, width, inner), BF),
                pltpu.VMEM((groups, inner, width), BF),
                pltpu.SemaphoreType.DMA((2,)),
                pltpu.VMEM((SLAB, groups * inner), F32),
                pltpu.VMEM((MID_BLOCKS * block - 5 * width, inner), F32),
                pltpu.VMEM((groups, width, inner), F32),
                pltpu.VMEM((groups, width, inner), F32),
                pltpu.VMEM((features, features), F32),
                pltpu.VMEM((length, groups * inner), BF),
                pltpu.VMEM((length, groups * inner), F32),
                pltpu.VMEM((length, groups * inner), BF),
            ],
        ),
        compiler_params=pltpu.CompilerParams(vmem_limit_bytes=VMEM_LIMIT),
        cost_estimate=pl.CostEstimate(flops=10**10, bytes_accessed=2 * 10**7, transcendentals=0),
        name="shared_layers",
    )(place, hidden, cat, cot_own, cot_got, *weights)


def conv_back_kernel(
    row,
    waits,
    place,
    x_ref,
    dcat_ref,
    dmix_ref,
    dm_ref,
    kc_ref,
    q_ref,
    joint_ref,
    taps_ref,
    vc_ref,
    own_a_ref,
    own_b_ref,
    got_a_ref,
    got_b_ref,
    depth_ref,
    kw_ref,
    order_ref,
    spread_ref,
    collect_ref,
    *rest,
):
    rest = rest[waits:]
    before = rest[:-20]
    part_ref, dq_ref, acc_a, acc_b, small_ref, kgrad_ref = rest[-20:-14]
    vs_s, xs_s, ys_s, ds_s, prod_s = rest[-14:-9]
    joint_s, q_s, kc_s, w_s, dm_s, x_s, dmix_s, old_s, sems = rest[-9:]
    length, features = x_s.shape
    width = HEADS * HEAD_SIZE
    piece = LANES
    weights = (own_a_ref, own_b_ref, got_a_ref, got_b_ref)
    pairs = [(joint_ref.at[row], joint_s), (q_ref.at[row], q_s), (kc_ref.at[row], kc_s)]
    pairs += [(weight, w_s.at[i]) for i, weight in enumerate(weights)]
    pairs += [(dm_ref.at[row], dm_s), (x_ref.at[place[BASE] + row], x_s), (dmix_ref.at[row], dmix_s)]
    pairs += [(old, old_s.at[i]) for i, old in enumerate(before[:2])]
    copies = start_copies(pairs, sems)
    for index, ref in enumerate((small_ref, kgrad_ref)):
        ref[...] = before[2 + index][...] if before else jnp.zeros_like(ref)
    dconv = dcat_ref[0].astype(F32)
    fill_strips(vs_s, vc_ref[0], length)
    taps_t = taps_ref[0]
    taps = taps_t.T
    high = taps.astype(BF)
    low = (taps - high.astype(F32)).astype(BF)
    both = jnp.concatenate([high, low], axis=1)
    zero = jnp.zeros((PAD, LANES), F32)
    for tap in range(KERNEL):
        spread = mm(both, spread_ref[:, tap * width : (tap + 1) * width])
        for strip in range(width // LANES):
            lanes = slice(strip * LANES, (strip + 1) * LANES)
            begin = PAD - RADIUS + tap
            prod_s[:, tap * width + strip * LANES : tap * width + (strip + 1) * LANES] = (
                dconv[:, lanes] * vs_s[strip, begin : begin + length, :]
            ).astype(BF)
            slot = tap * (width // LANES) + strip
            ys_s[slot, 0:PAD, :] = zero
            ys_s[slot, PAD + length :, :] = zero
            ys_s[slot, PAD : PAD + length, :] = spread[:, lanes] * dconv[:, lanes]
    dvc = []
    for strip in range(width // LANES):
        total = None
        for tap in range(KERNEL):
            begin = PAD + RADIUS - tap
            term = ys_s[tap * (width // LANES) + strip, begin : begin + length, :]
            total = term if total is None else total + term
        dvc.append(total.astype(BF))
    dvc = jnp.concatenate(dvc, axis=1)
    dtaps = mm(prod_s[...], collect_ref[...]).T
    slabs = [dtaps[t * SLAB : (t + 1) * SLAB] for t in range(KERNEL)]
    weights = [taps_t[t * SLAB : (t + 1) * SLAB] for t in range(KERNEL)]
    total = functools.reduce(jnp.add, [a * b for a, b in zip(slabs, weights)])
    slabs = [b * (a - total) for a, b in zip(slabs, weights)]
    slabs.append(jnp.zeros((LANES - KERNEL * SLAB, length), F32))
    dlogits_t = jnp.concatenate(slabs, axis=0)
    dlogits = dlogits_t.T.astype(BF)
    rounded_t = dlogits_t.astype(BF)
    for copy in copies:
        copy.wait()
    wa, wb = pick_weights(place, 1, w_s)
    x = x_s[...]
    kgrad_ref[:, 0:width] += mm(rounded_t, joint_s[...])
    kgrad_ref[:, width : width + LANES] += jnp.broadcast_to(
        jnp.sum(rounded_t.astype(F32), axis=1, keepdims=True), (LANES, LANES)
    )
    djoint = mm(dlogits, tapped_weights(order_ref, kw_ref)).astype(BF).astype(F32)
    dkey = (djoint * q_s[...].astype(F32)).astype(BF)
    dq_ref[0] = (djoint * kc_s[...]).astype(BF)
    small_ref[9:10, 0:width] += rowsum(dkey.astype(F32))
    small_ref[9:10, width : 2 * width] += rowsum(dvc.astype(F32))
    ddepth = mm_nt(dkey, wa).astype(BF)
    acc_a[...] = mm(dm_s[...].T, dkey)
    acc_b[...] = mm(x.T, dvc)
    if before:
        acc_a[...] += old_s[0]
        acc_b[...] += old_s[1]
    part_ref[0] = dmix_s[...] + mm_nt(dvc, wb)
    fill_strips(ds_s, ddepth, length)
    fill_strips(xs_s, x, length)
    for strip in range(features // LANES):
        lanes = slice(strip * LANES, (strip + 1) * LANES)
        sums = [None] * KERNEL
        for at in range(0, length, piece):
            total = part_ref[0, at : at + piece, lanes]
            center = ds_s[strip, PAD + at : PAD + at + piece, :]
            for tap in range(KERNEL):
                begin = PAD + RADIUS - tap + at
                total = total + ds_s[strip, begin : begin + piece, :] * depth_ref[tap : tap + 1, lanes]
                begin = PAD - RADIUS + tap + at
                term = (xs_s[strip, begin : begin + piece, :] * center).reshape(-1, SLAB, LANES)
                term = jnp.sum(term, axis=0)
                sums[tap] = term if sums[tap] is None else sums[tap] + term
            part_ref[0, at : at + piece, lanes] = total
        for tap in range(KERNEL):
            small_ref[tap : tap + 1, lanes] += rowsum(sums[tap])


def conv_back(place, row, hidden, dcat, dmix, kept, weights, before, waits):
    length, features = hidden.shape[1:]
    width = HEADS * HEAD_SIZE

    def by_row(array):
        zeros = (0,) * (array.ndim - 1)
        return pl.BlockSpec((1,) + array.shape[1:], lambda r, p: (row,) + zeros)

    outs = [
        jax.ShapeDtypeStruct((1, length, features), F32),
        jax.ShapeDtypeStruct((1, length, width), BF),
        jax.ShapeDtypeStruct((features, width), F32),
        jax.ShapeDtypeStruct((features, width), F32),
        jax.ShapeDtypeStruct((16, features), F32),
        jax.ShapeDtypeStruct((LANES, width + LANES), F32),
    ]
    strips = features // LANES
    anywhere = pl.BlockSpec(memory_space=pl.ANY)
    return pl.pallas_call(
        functools.partial(conv_back_kernel, row, len(waits)),
        out_shape=outs,
        grid_spec=pltpu.PrefetchScalarGridSpec(
            num_scalar_prefetch=1,
            grid=(1,),
            in_specs=[
                anywhere,
                pl.BlockSpec((1, length, width), lambda r, p: (row, 0, 1)),
                *[anywhere] * 5,
                *[by_row(a) for a in kept[4:]],
                *[anywhere] * 4,
                *[whole(w) for w in weights[4:]],
                *[anywhere] * len(waits),
                *[anywhere] * len(before[:2]),
                *[whole(a) for a in before[2:]],
            ],
            out_specs=[whole(o) for o in outs],
            scratch_shapes=[
                pltpu.VMEM((width // LANES, length + 2 * PAD, LANES), F32),
                pltpu.VMEM((strips, length + 2 * PAD, LANES), F32),
                pltpu.VMEM((KERNEL * width // LANES, length + 2 * PAD, LANES), F32),
                pltpu.VMEM((strips, length + 2 * PAD, LANES), F32),
                pltpu.VMEM((length, KERNEL * width), BF),
                pltpu.VMEM((length, width), BF),
                pltpu.VMEM((length, width), BF),
                pltpu.VMEM((length, width), F32),
                pltpu.VMEM((4, features, width), BF),
                pltpu.VMEM((length, features), BF),
                pltpu.VMEM((length, features), BF),
                pltpu.VMEM((length, features), F32),
                pltpu.VMEM((2, features, width), F32),
                pltpu.SemaphoreType.DMA((12,)),
            ],
        ),
        compiler_params=pltpu.CompilerParams(vmem_limit_bytes=VMEM_LIMIT),
        cost_estimate=pl.CostEstimate(flops=10**10, bytes_accessed=2 * 10**7, transcendentals=0),
        name="convolution_backward",
    )(place, hidden, dcat, dmix, *kept, *weights, *waits, *before)


def att_back_kernel(
    row,
    waits,
    place,
    x_ref,
    dcat_ref,
    datt_ref,
    part_ref,
    dqc_ref,
    q_ref,
    k_ref,
    v_ref,
    probs_ref,
    att_t_ref,
    wq_ref,
    own_a_ref,
    own_b_ref,
    got_a_ref,
    got_b_ref,
    *rest,
):
    rest = rest[waits:]
    before = rest[:-15]
    own_ref, send_ref, acc_s, small_ref, kt_s, dqt_s, dk_s, dv_s, total_s = rest[-15:-6]
    probs_s, x_s, w_s, part_s, old_s, sems = rest[-6:]
    length, features = x_s.shape
    width = HEADS * HEAD_SIZE
    weights = (own_a_ref, own_b_ref, got_a_ref, got_b_ref, wq_ref)
    pairs = [(probs_ref.at[row, head], probs_s.at[head]) for head in range(HEADS)]
    pairs += [(x_ref.at[place[BASE] + row], x_s)]
    pairs += [(weight, w_s.at[i]) for i, weight in enumerate(weights)]
    pairs += [(part_ref.at[0], part_s)]
    pairs += [(old, old_s) for old in before[:1]]
    copies = start_copies(pairs, sems)
    small_ref[...] = before[1][...] if before else jnp.zeros_like(small_ref)
    scaled_keys = (k_ref[0].astype(F32) * (HEAD_SIZE**-0.5)).astype(BF)
    kt_s[...] = scaled_keys.T
    low_lane = lax.broadcasted_iota(jnp.int32, (1, LANES), 1) < HEAD_SIZE
    for pair in range(HEADS // 2):
        lanes = slice(pair * LANES, (pair + 1) * LANES)
        d_pair = dcat_ref[0, :, lanes]
        q_pair = q_ref[0, :, lanes]
        v_pair = v_ref[0, :, lanes]
        dk = jnp.zeros((length, LANES), F32)
        dv = jnp.zeros((length, LANES), F32)
        for head in (2 * pair, 2 * pair + 1):
            span = slice(head * HEAD_SIZE, (head + 1) * HEAD_SIZE)
            keep = low_lane if head % 2 == 0 else jnp.logical_not(low_lane)
            d_own = datt_ref[0, span, :].astype(F32)
            delta = rowsum(d_own * att_t_ref[0, span, :].astype(F32))
            dp = mm(v_pair, head_pair_rows(datt_ref[0], head))
            copies[head].wait()
            probs = probs_s[head]
            dscores = (probs.astype(F32) * (dp - delta)).astype(BF)
            dqt_s[span, :] = mm(kt_s[span, :], dscores)
            dv = dv + mm(probs, jnp.where(keep, d_pair, jnp.zeros_like(d_pair)))
            dk = dk + mm(dscores, jnp.where(keep, q_pair, jnp.zeros_like(q_pair)))
        dk_s[:, lanes] = dk.astype(BF)
        dv_s[:, lanes] = dv.astype(BF)
    dq = dqt_s[...].T.astype(BF).astype(F32) + dqc_ref[0].astype(F32)
    small_ref[0:1, 0:width] += rowsum(dq)
    small_ref[0:1, width : 2 * width] += rowsum(dv_s[...].astype(F32))
    dq = dq.astype(BF)
    for copy in copies[HEADS:]:
        copy.wait()
    wk, wv = pick_weights(place, 0, w_s)
    x_t = x_s[...].T
    for number, gradient in enumerate((dq, dk_s[...], dv_s[...])):
        product = mm(x_t, gradient)
        acc_s[number] = product + old_s[number] if before else product
    total_s[...] = (
        part_s[...]
        + mm_nt(dq, w_s[4])
        + mm_nt(dk_s[...], wk)
        + mm_nt(dv_s[...], wv)
    )
    half = length // 2
    mine = pl.multiple_of(place[SIDE] * half, half)
    other = pl.multiple_of((1 - place[SIDE]) * half, half)
    own_ref[0] = total_s[pl.ds(mine, half), :]
    send_ref[0] = total_s[pl.ds(other, half), :].astype(BF)


def att_back(place, row, hidden, dcat, datt, part, dqc, kept, weights, before, waits):
    length, features = hidden.shape[1:]
    width = HEADS * HEAD_SIZE
    half = length // 2
    anywhere = pl.BlockSpec(memory_space=pl.ANY)

    def by_row(array):
        zeros = (0,) * (array.ndim - 1)
        return pl.BlockSpec((1,) + array.shape[1:], lambda r, p: (row,) + zeros)

    outs = [
        jax.ShapeDtypeStruct((1, half, features), F32),
        jax.ShapeDtypeStruct((1, half, features), BF),
        jax.ShapeDtypeStruct((3, features, width), F32),
        jax.ShapeDtypeStruct((SLAB, features), F32),
    ]
    return pl.pallas_call(
        functools.partial(att_back_kernel, row, len(waits)),
        out_shape=outs,
        grid_spec=pltpu.PrefetchScalarGridSpec(
            num_scalar_prefetch=1,
            grid=(1,),
            in_specs=[
                anywhere,
                pl.BlockSpec((1, length, width), lambda r, p: (row, 0, 0)),
                by_row(datt),
                anywhere,
                whole(dqc),
                *[by_row(a) for a in kept[:3]],
                anywhere,
                by_row(kept[4]),
                *[anywhere] * (len(weights) + len(waits)),
                *[anywhere] * len(before[:1]),
                *[whole(a) for a in before[1:]],
            ],
            out_specs=[whole(o) for o in outs],
            scratch_shapes=[
                pltpu.VMEM((width, length), BF),
                pltpu.VMEM((width, length), F32),
                pltpu.VMEM((length, width), BF),
                pltpu.VMEM((length, width), BF),
                pltpu.VMEM((length, features), F32),
                pltpu.VMEM((HEADS, length, length), BF),
                pltpu.VMEM((length, features), BF),
                pltpu.VMEM((5, features, width), BF),
                pltpu.VMEM((length, features), F32),
                pltpu.VMEM((3, features, width), F32),
                pltpu.SemaphoreType.DMA((HEADS + 8,)),
            ],
        ),
        compiler_params=pltpu.CompilerParams(vmem_limit_bytes=VMEM_LIMIT),
        cost_estimate=pl.CostEstimate(flops=10**10, bytes_accessed=2 * 10**7, transcendentals=0),
        name="attention_backward",
    )(place, hidden, dcat, datt, part, dqc, *kept, *weights, *waits, *before)


def pack_kernel(place, acc_ref, small_ref, acc_a, acc_b, small_conv, kgrad, *rest):
    keep_ref, away_ref, rest_s, grad_ref, sems = rest[-5:]
    features, width = acc_a.shape
    taps = KERNEL * SLAB
    rest_s[...] = jnp.zeros_like(rest_s)
    rest_s[0:taps, 0 : width + LANES] = kgrad[0:taps, :]
    rest_s[taps : taps + 16, :] = small_conv[...]
    rest_s[taps + 16 : taps + 16 + SLAB, :] = small_ref[...]
    sources = [acc_ref.at[0], acc_ref.at[1], acc_ref.at[2], acc_a, acc_b]
    for source, start, block, at, size in tail_rows(width, features):
        slot = tail_slot(block, place)
        if start < width:
            left = sources[source][start : start + size, :]
            right = sources[source][width + start : width + start + size, :]
            grad_ref[slot, at : at + size, 0:width] = left.astype(BF)
            grad_ref[slot, at : at + size, width:] = right.astype(BF)
        else:
            start = start - width
            grad_ref[slot, at : at + size, :] = rest_s[start : start + size, :].astype(BF)
    send_halves(grad_ref, keep_ref, away_ref, sems)


def pack(place, sums, waits):
    features, width = sums[2].shape
    sent = jax.ShapeDtypeStruct((TAIL_BLOCKS // 2, tail_block(width), features), BF)
    anywhere = pl.BlockSpec(memory_space=pl.ANY)
    return pl.pallas_call(
        pack_kernel,
        out_shape=[sent, sent],
        grid_spec=pltpu.PrefetchScalarGridSpec(
            num_scalar_prefetch=1,
            grid=(1,),
            in_specs=[whole(a) for a in sums] + [anywhere] * len(waits),
            out_specs=[anywhere, anywhere],
            scratch_shapes=[
                pltpu.VMEM((TAIL_BLOCKS * tail_shared(width) - width, features), F32),
                pltpu.VMEM((TAIL_BLOCKS, tail_block(width), features), BF),
                pltpu.SemaphoreType.DMA((2,)),
            ],
        ),
        compiler_params=pltpu.CompilerParams(vmem_limit_bytes=VMEM_LIMIT),
        cost_estimate=pl.CostEstimate(flops=10**9, bytes_accessed=10**7, transcendentals=0),
        name="pack_gradients",
    )(place, *sums, *waits)


def merge(body, outs, ins, waits=(), steps=1):
    waited = len(waits)

    def kernel(*refs):
        body(refs[: len(ins)], refs[len(ins) + waited :])

    def spec(array):
        if steps == 1:
            return whole(array)
        axis = 1 if array.ndim == 4 else 0
        shape = list(array.shape)
        shape[axis] //= steps
        return pl.BlockSpec(
            tuple(shape), lambda i: tuple(i if d == axis else 0 for d in range(len(shape)))
        )

    outs = [jax.ShapeDtypeStruct(shape, BF) for shape in outs]
    return pl.pallas_call(
        kernel,
        out_shape=outs,
        grid=(steps,),
        in_specs=[spec(a) for a in ins] + [pl.BlockSpec(memory_space=pl.ANY)] * waited,
        out_specs=[spec(o) for o in outs],
        compiler_params=pltpu.CompilerParams(vmem_limit_bytes=VMEM_LIMIT),
        cost_estimate=pl.CostEstimate(flops=10**9, bytes_accessed=4 * 10**6, transcendentals=0),
        name="exchange_step",
    )(*ins, *waits)


def total(*values):
    result = values[0].astype(F32)
    for value in values[1:]:
        result = result + value.astype(F32)
    return result.astype(BF)


def sum_core(ins, outs):
    for part, out in enumerate(outs):
        out[...] = total(ins[0][part], ins[1][part])


def sum_first(ins, outs):
    keep_a, got_a, keep_b, got_b = ins
    half = outs[0].shape[0]
    for part in range(2):
        span = slice(part * half, (part + 1) * half)
        outs[part][...] = total(keep_a[span], got_a[span])
        outs[2 + part][...] = total(keep_b[span], got_b[span])


def sum_second(ins, outs):
    keep_a, got_a, keep_b, got_b = ins
    for part, out in enumerate(outs):
        out[0] = total(keep_a[part], got_a[part])
        out[1] = total(keep_b[part], got_b[part])


def sum_all(ins, outs):
    outs[0][...] = total(*[i[...] for i in ins])


def sum_parts(ins, outs):
    for part, out in enumerate(outs):
        span = slice(part * out.shape[0], (part + 1) * out.shape[0])
        out[...] = total(*[i[span] for i in ins])


def first_of(value):
    corner = lax.slice(value, (0,) * value.ndim, (1,) * value.ndim)
    return jnp.clip(corner.astype(F32).reshape(()), 0.0, 0.0)


def late(value, zero):
    return (value.astype(F32) + zero).astype(BF)


def across(value, links):
    if links.size <= 16:
        return value
    groups = [[low + 16 * high for high in range(links.size // 16)] for low in range(16)]
    return lax.psum(value, "dp", axis_index_groups=groups)


def join(*values):
    return jnp.concatenate(values, axis=0)


class Links:
    def __init__(self, size):
        self.size = size
        self.core = ("dp", self.flip(1))
        self.x = ("dp", self.flip(2))
        self.y = ("branch", [(0, 1), (1, 0)])
        self.corner = (
            ("branch", "dp"),
            [(b * size + i, (1 - b) * size + (i ^ 2)) for b in range(2) for i in range(size)],
        )
        self.z = [("dp", self.flip(4 * d)) for d in range(1, 4)]

    def flip(self, bits):
        return [(i, i ^ bits) for i in range(self.size)]


def cut(value, parts):
    return value.reshape(parts, -1, *value.shape[1:])


def send(pairs):
    return [lax.ppermute(value, *hop) for value, hop in pairs]


def plane(links):
    return [links.y, links.x, links.corner]


def load_pieces(pieces, buffer, sems):
    size = pieces[0].shape[0]
    copies = [
        pltpu.make_async_copy(piece, buffer.at[i * size : (i + 1) * size], sems.at[i])
        for i, piece in enumerate(pieces)
    ]
    for copy in copies:
        copy.start()
    for copy in copies:
        copy.wait()


def spread_middle_kernel(place, *rest):
    pieces, outs = rest[:8], rest[8:]
    inner_ref, outer_ref, mixer_ref, ib_ref, *vector_refs = outs[:-4]
    turn_s, rest_ref, grad_ref, sems = outs[-4:]
    load_pieces(pieces, grad_ref, sems)
    groups, width, inner = inner_ref.shape
    block = grad_ref.shape[1]
    features = mixer_ref.shape[1]
    targets = [inner_ref.at[0], inner_ref.at[1], turn_s.at[0], turn_s.at[1]]
    for part in range(MID_BLOCKS):
        start = part * block
        value = grad_ref[mid_slot(part, place)].astype(F32)
        if start < 2 * groups * width:
            target = targets[start // width]
            start = start % width
            target[start : start + block, :] = value
        elif start < 5 * width:
            start = start - 2 * groups * width
            mixer_ref[start : start + block, :] = value[:, :features]
            mixer_ref[width + start : width + start + block, :] = value[:, features:]
        else:
            start = start - 5 * width
            rest_ref[start : start + block, :] = value
    for g in range(groups):
        outer_ref[g] = turn_s[g].T
    ib_ref[...] = jnp.concatenate([rest_ref[0:1, :], rest_ref[1:2, :]], axis=1).reshape(-1)
    for number, ref in enumerate(vector_refs):
        row, col = 2 + number // 2, number % 2 * features
        ref[...] = rest_ref[row : row + 1, col : col + features].reshape(-1)


def spread_middle(place, pieces, width, inner, features):
    block = pieces[0].shape[1]
    outs = [
        jax.ShapeDtypeStruct((2, width, inner), F32),
        jax.ShapeDtypeStruct((2, inner, width), F32),
        jax.ShapeDtypeStruct((features, features), F32),
        jax.ShapeDtypeStruct((2 * inner,), F32),
        *[jax.ShapeDtypeStruct((features,), F32)] * 6,
    ]
    return pl.pallas_call(
        spread_middle_kernel,
        out_shape=outs,
        grid_spec=pltpu.PrefetchScalarGridSpec(
            num_scalar_prefetch=1,
            grid=(1,),
            in_specs=[pl.BlockSpec(memory_space=pl.ANY)] * len(pieces),
            out_specs=[whole(o) for o in outs],
            scratch_shapes=[
                pltpu.VMEM((2, width, inner), F32),
                pltpu.VMEM((MID_BLOCKS * block - 5 * width, inner), F32),
                pltpu.VMEM((MID_BLOCKS, block, inner), BF),
                pltpu.SemaphoreType.DMA((len(pieces),)),
            ],
        ),
        compiler_params=pltpu.CompilerParams(vmem_limit_bytes=VMEM_LIMIT),
        cost_estimate=pl.CostEstimate(flops=3 * 10**9, bytes_accessed=2 * 10**7, transcendentals=0),
        name="shared_gradients",
    )(place, *pieces)


def spread_branch_kernel(place, order_ref, turned_ref, *rest):
    pieces, outs = rest[:8], rest[9:]
    query_ref, keys_ref, values_ref, qb_ref, vb_ref, depth_ref, pb_ref, kw_ref, kb_ref = outs[:9]
    grad_ref, rest_s, sems = outs[9:]
    width = query_ref.shape[1]
    size = pieces[0].shape[0]
    shared = tail_shared(width)
    owned = grad_ref.shape[1] - shared
    copies = []
    for number, piece in enumerate(pieces):
        core, x, y = number // 4, number % 2, number // 2 % 2
        start = core << 4 | x << 3 | y << 2
        target = grad_ref.at[start : start + size]
        if y:
            target = grad_ref.at[start : start + size, owned:, :]
        copies.append(pltpu.make_async_copy(piece, target, sems.at[number]))
    for copy in copies:
        copy.start()
    for copy in copies:
        copy.wait()
    for within in range(4 * width // owned // 2):
        block = (within >> 2) << 3 | within & 3
        value = grad_ref[block ^ (place[MASK_T] & ~4), 0:owned, :].astype(F32)
        start = within * owned
        target = keys_ref if start < width else values_ref
        start = start % width
        target[0, start : start + owned, :] = value[:, :width]
        target[0, width + start : width + start + owned, :] = value[:, width:]
    for block in range(TAIL_BLOCKS):
        value = grad_ref[tail_slot(block, place), owned:, :].astype(F32)
        start = block * shared
        if start < width:
            query_ref[start : start + shared, :] = value[:, :width]
            query_ref[width + start : width + start + shared, :] = value[:, width:]
        else:
            rest_s[start - width : start - width + shared, :] = value
    taps = KERNEL * SLAB
    depth_ref[...] = rest_s[taps : taps + KERNEL, :]
    conv_line = rest_s[taps + KERNEL : taps + KERNEL + 1, :]
    att_line = rest_s[taps + 16 : taps + 17, :]
    qb_ref[...] = att_line[:, :width].reshape(-1)
    pb_ref[...] = conv_line[:, :width].reshape(-1)
    vb_ref[...] = jnp.where(place[SIDE] == 0, att_line[:, width:], conv_line[:, width:])
    kw_ref[...] = mm(turned_ref[...], rest_s[:, 0:width].astype(BF))
    taps_bias = mm(rest_s[:, width : width + LANES].T.astype(BF), order_ref[...])[0:1]
    kb_ref[...] = taps_bias.reshape(-1)


def spread_branch(place, ordered, pieces, width, features, wait):
    block = pieces[0].shape[1]
    outs = [
        jax.ShapeDtypeStruct((features, width), F32),
        jax.ShapeDtypeStruct((1, features, width), F32),
        jax.ShapeDtypeStruct((1, features, width), F32),
        jax.ShapeDtypeStruct((width,), F32),
        jax.ShapeDtypeStruct((1, width), F32),
        jax.ShapeDtypeStruct((KERNEL, features), F32),
        jax.ShapeDtypeStruct((width,), F32),
        jax.ShapeDtypeStruct((HEADS * KERNEL, width), F32),
        jax.ShapeDtypeStruct((HEADS * KERNEL,), F32),
    ]
    return pl.pallas_call(
        spread_branch_kernel,
        out_shape=outs,
        grid_spec=pltpu.PrefetchScalarGridSpec(
            num_scalar_prefetch=1,
            grid=(1,),
            in_specs=[whole(o) for o in ordered]
            + [pl.BlockSpec(memory_space=pl.ANY)] * (len(pieces) + 1),
            out_specs=[whole(o) for o in outs],
            scratch_shapes=[
                pltpu.VMEM((TAIL_BLOCKS, block, features), BF),
                pltpu.VMEM((TAIL_BLOCKS * tail_shared(width) - width, features), F32),
                pltpu.SemaphoreType.DMA((len(pieces),)),
            ],
        ),
        compiler_params=pltpu.CompilerParams(vmem_limit_bytes=VMEM_LIMIT),
        cost_estimate=pl.CostEstimate(flops=2 * 10**9, bytes_accessed=2 * 10**7, transcendentals=0),
        name="branch_gradients",
    )(place, *ordered, *pieces, wait)


def after(values, *others):
    return lax.optimization_barrier((tuple(values), others))[0]


def shards(
    size,
    hidden,
    bounds,
    query_weight,
    query_bias,
    branch_keys,
    branch_values,
    branch_bias,
    depth_kernel,
    point_bias,
    kernel_weight,
    kernel_bias,
    mixer_weight,
    mixer_bias,
    first_gain,
    first_shift,
    inner_weight,
    inner_bias,
    outer_weight,
    outer_bias,
    second_gain,
    second_shift,
    cotangent,
):
    links = Links(size)
    side = lax.axis_index("branch")
    index = lax.axis_index("dp")
    core, x, z = index & 1, (index >> 1) & 1, (index >> 2) & 3
    rows = hidden.shape[0] // 2
    features = hidden.shape[2]
    width = query_weight.shape[1]
    inner = inner_weight.shape[2]
    place = jnp.stack(
        [
            side * rows,
            side,
            core,
            core << 5 | x << 3 | side << 2 | z,
            core << 5 | side << 3 | x << 2 | z,
            core << 4 | x << 3 | side << 2 | z,
        ]
    ).astype(jnp.int32)

    def exchange(value):
        return lax.ppermute(value, *links.y)

    got = exchange(jnp.where(core == 0, branch_keys[0], branch_values[0]))
    got_bias = exchange(branch_bias)
    own_weights = (branch_keys[0], branch_values[0])
    far = ((1 - side) * rows).astype(jnp.int32)
    spread, ordered = spread_table(), order_table()
    flat_kernel = kernel_weight.T
    common = (depth_kernel, query_bias, point_bias, kernel_bias, flat_kernel, ordered, spread)
    bounds = bounds.T
    kept = forward(
        0, place, bounds, hidden, (query_weight, *own_weights, branch_bias, *common), rows
    )
    got, got_bias, cotangent = after((got, got_bias, cotangent), kept[0])
    got_weights = (got, lax.ppermute(got, *links.core))
    cot_got = exchange(lax.dynamic_slice_in_dim(cotangent, far, rows, 0))
    kept = forward(
        1, place, bounds, hidden, (query_weight, *got_weights, got_bias, *common), rows, kept
    )
    cat, q, k, v, probs, att_t, dm, kc, cq, joint, taps, vc = kept
    (cot_got,) = after([cot_got], cat)
    out_own, out_send, dcat, datt, dmix, mid_keep, mid_away = middle(
        place,
        hidden,
        cat,
        cotangent,
        cot_got,
        (
            mixer_weight,
            inner_weight,
            outer_weight,
            mixer_bias,
            first_gain,
            first_shift,
            inner_bias,
            outer_bias,
            second_gain,
            second_shift,
        ),
        rows,
    )
    conv_weights = (
        *own_weights, *got_weights, depth_kernel, flat_kernel, ordered, spread, gather_table()
    )
    att_weights = (query_weight, *own_weights, *got_weights)
    conv_kept = (dm, kc, cq, joint, taps, vc)
    att_kept = (q, k, v, probs, att_t)

    block = mid_keep.shape[1:]
    mid_keep, mid_away = cut(mid_keep, 4), cut(mid_away, 4)
    (mid_got,) = send([(mid_away, links.core)])
    conv0 = conv_back(place, 0, hidden, dcat, dmix, conv_kept, conv_weights, (), ())
    keep_a, away_a, keep_b, away_b = merge(
        sum_core, [(8, *block)] * 4, (mid_keep, mid_got), (), 4
    )
    got_a, got_b, out_got = send([(away_a, links.x), (away_b, links.y), (out_send, links.y)])
    conv1 = conv_back(
        place, 1, hidden, dcat, dmix, conv_kept, conv_weights, tuple(conv0[2:]), (keep_a,)
    )
    keep_a, away_a, keep_b, away_b = merge(
        sum_first, [(4, *block)] * 4, (keep_a, got_a, keep_b, got_b)
    )
    got_a, got_b = send([(away_a, links.y), (away_b, links.x)])
    att0 = att_back(
        place, 0, hidden, dcat, datt, conv0[0], conv0[1], att_kept, att_weights, (), (keep_a,)
    )
    mid, *away = merge(
        sum_second, [(2, *block)] * 4, (keep_a, got_a, keep_b, got_b)
    )
    got_z = send(zip(away, links.z))
    (hid_got0,) = send([(att0[1], links.y)])
    att1 = att_back(
        place,
        1,
        hidden,
        dcat,
        datt,
        conv1[0],
        conv1[1],
        att_kept,
        att_weights,
        tuple(att0[2:]),
        (mid, out_got),
    )
    tail_rows_each = tail_block(width)
    mid = across(total(mid, *got_z), links)
    tail_keep, tail_away = pack(place, (*att1[2:], *conv1[2:]), (mid, hid_got0))
    tail_got = send([(tail_away, links.core)])
    piece = (tail_rows_each, features)
    got_mid = send([(mid, hop) for hop in links.z])
    tail = cut(total(tail_keep, *tail_got), 4)
    got_tail = send(zip(tail[1:], plane(links)))
    tail = cut(total(tail[0], *got_tail), 4)
    got_tail = send(zip(tail[1:], links.z))
    zero = first_of(tail)
    pieces = [mid] + [late(got, zero) for got in got_mid]
    mid_a, mid_b = (join(*[m[order : order + 1] for m in pieces]) for order in range(2))
    got_a, got_b = send([(mid_a, links.y), (mid_b, links.x)])
    tail = across(total(tail[0], *got_tail), links)
    zero = first_of(tail)
    mid_a, mid_b = join(mid_a, late(got_a, zero)), join(mid_b, late(got_b, zero))
    got_a, got_b = send([(mid_a, links.x), (mid_b, links.y)])
    tail = late(tail, first_of(mid_a) + first_of(mid_b))
    got_tail = send([(tail, hop) for hop in links.z])
    mid = (mid_a, got_a, mid_b, got_b)
    tail = join(tail, *got_tail)
    zero = first_of(tail)
    far_mid = send([(late(m, zero), links.core) for m in mid])
    mid = (*mid, *far_mid)
    zero = first_of(far_mid[0])
    tail = late(tail, zero)
    shared = tail[:, tail.shape[1] - tail_shared(width) :]
    got_tail = send([(tail, links.x), (shared, links.y), (shared, links.corner)])
    (hid_got1,) = send([(late(att1[1], first_of(got_tail[0])), links.y)])
    tail = (tail, *got_tail)
    tail = (*tail, *send([(t, links.core) for t in tail]))
    grad_inner, grad_outer, grad_mixer, inner_line, *mid_lines = spread_middle(
        place, mid, width, inner, features
    )
    mixer_line, gain1_line, shift1_line, outer_line, gain2_line, shift2_line = mid_lines
    (
        query_grad,
        keys,
        values,
        query_line,
        value_line,
        depth,
        point_line,
        kernel_grad,
        kernel_line,
    ) = spread_branch(
        place, (ordered, jnp.asarray(ordered.T)), tail, width, features, mixer_line
    )
    def combine(own, got):
        return jnp.where(side == 0, join(own, got), join(got, own))

    output = combine(out_own, out_got)
    hidden_grad = combine(join(att0[0], att1[0]), join(hid_got0, hid_got1).astype(F32))
    return (
        output,
        hidden_grad,
        query_grad,
        query_line,
        keys,
        values,
        value_line,
        depth,
        point_line,
        kernel_grad.T,
        kernel_line,
        grad_mixer,
        mixer_line,
        gain1_line,
        shift1_line,
        grad_inner,
        inner_line,
        grad_outer,
        outer_line,
        gain2_line,
        shift2_line,
    )


def solution(mesh):
    split = P("dp", "branch", None)
    owned = P("branch", None, None)
    return jax.shard_map(
        functools.partial(shards, mesh.shape["dp"]),
        mesh=mesh,
        in_specs=(
            P("dp", None, None),
            P("dp", None),
            P(),
            P(),
            owned,
            owned,
            P("branch", None),
            *([P()] * 14),
            split,
        ),
        out_specs=(
            split,
            split,
            P(),
            P(),
            owned,
            owned,
            P("branch", None),
            *([P()] * 14),
        ),
        check_vma=False,
    )
```
